256 devices in a mesh: gx: 8 (over z), gy: 32 (over y, x, core).
Axes of the slice: x: 4, y: 4, z: 8, core: 2. Of those that a mesh axis runs over, the one named last changes fastest.
Arguments:
- source: float32 [64, 1024, 256], P('gx', 'gy'), may hold values from -4 to 4
- material: int32 [64, 1024, 256], P('gx', 'gy'), may hold values from 0 to 2
- boundary_flags: int32 [64, 1024, 256], P('gx', 'gy'), may hold values 0 or 1
Outputs:
- pressure: float32 [64, 1024, 256], P('gx', 'gy')
- residual: float32 [64, 1024, 256], P('gx', 'gy')
The draws below stay inside these ranges and needn't reach their ends.
All inputs are finite; a program needn't handle non-finite values. No bound on the sum of `boundary_flags` on one device may be relied on, other than what follows from the above.
Results may differ from the reference program's by a relative error of at most 0.0003.
Values sent between devices are 32-bit elements; how exact they have to be, the bound alone decides.
No kernel may reach another device: no remote copies, remote signals or barrier semaphores. Data moves between devices by JAX's collectives and lax.ppermute only.
A program may use at most 128 MiB of HBM per device.

```python
import math
import jax
import jax.numpy as jnp

NZ = 256
FINE_LEVELS = 3
PRE_SWEEPS = 3
POST_SWEEPS = 2
COARSE_SWEEPS = 8
NX = 64
NY = 1024


def draw_source(key, part):
    key = jax.random.fold_in(key, 11)
    rough_key, phase_key = jax.random.split(key)
    phases = jax.random.uniform(phase_key, (3,), jnp.float32, 0.0, 2.0 * math.pi)
    first_wave = jnp.cos(2.0 * math.pi * (jnp.arange(NX, dtype=jnp.float32) + 0.5) / NX + phases[0])
    second_wave = jnp.cos(2.0 * math.pi * (jnp.arange(NY, dtype=jnp.float32) + 0.5) / NY + phases[1])
    third_wave = jnp.cos(math.pi * (jnp.arange(NZ, dtype=jnp.float32) + 0.5) / NZ + phases[2])
    product_wave = first_wave[:, None, None] * second_wave[None, :, None] * third_wave[None, None, :]
    rough_part = jnp.clip(jax.random.normal(rough_key, (NX, NY, NZ), jnp.float32), -3.9, 3.9)
    smooth = 0.05 * product_wave
    return (rough_part + smooth).astype(jnp.float32)


def set_ends(values, rng, least, top_value):
    longest = values.shape.index(max(values.shape))
    spots = []
    for shift in (0, 1):
        where = [jax.random.randint(jax.random.fold_in(rng, axis), (), 0, length) for axis, length in enumerate(values.shape)]
        where[longest] = (where[longest] + shift) % values.shape[longest]
        spots.append(tuple(where))
    return values.at[spots[0]].set(least).at[spots[1]].set(top_value)


def setup_inputs(seed: int = 0) -> dict:
    key_list = jax.random.split(jax.random.key(seed), 4)
    return {
        "source": draw_source(jax.random.fold_in(key_list[3], 71), 0),
        "material": set_ends(jax.random.randint(key_list[1], (NX, NY, NZ), 0, 3), jax.random.fold_in(key_list[1], 1), 0, 2).astype(jnp.int32),
        "boundary_flags": set_ends((jax.random.randint(key_list[2], (NX, NY, NZ), 0, 256) < 1).astype(jnp.int32), jax.random.fold_in(key_list[2], 1), 0, 1),
    }


OMEGA = 0.8
SHIFT = 0.001
ROBIN = 2.0
INVERSE_SOLID = 1.0 / 3.0
INVERSE_DENSE = 0.125


def coefficients(material, boundary_flags):
    inverse = jnp.where(material == 0, 1.0, jnp.where(material == 1, INVERSE_SOLID, INVERSE_DENSE)).astype(jnp.float32)
    reaction = (SHIFT + ROBIN * boundary_flags.astype(jnp.float32)).astype(jnp.float32)
    return jnp.stack([inverse, reaction])


def harmonic(former, latter):
    summed = former + latter
    return 2.0 * former * latter / jnp.where(summed > 0, summed, 1.0)


def trimmed(array, margin):
    if margin == 0:
        return array
    return array[margin:-margin, margin:-margin, margin:-margin]


def prepare(padded, scaling, rim_width):
    inverse = padded[0]
    reaction = padded[1]
    faces_x = harmonic(inverse[1:], inverse[:-1])
    faces_y = harmonic(inverse[:, 1:], inverse[:, :-1])
    faces_z = harmonic(inverse[:, :, 1:], inverse[:, :, :-1])
    summed = faces_x[1:, 1:-1, 1:-1] + faces_x[:-1, 1:-1, 1:-1]
    summed = summed + faces_y[1:-1, 1:, 1:-1] + faces_y[1:-1, :-1, 1:-1]
    summed = summed + faces_z[1:-1, 1:-1, 1:] + faces_z[1:-1, 1:-1, :-1]
    diagonal = scaling * summed + reaction[1:-1, 1:-1, 1:-1]
    diagonal = jnp.where(diagonal > 0, diagonal, 1.0)
    return (faces_x, faces_y, faces_z, reaction, diagonal, scaling, rim_width)


def operate(padded, stencil, inner_width):
    faces_x, faces_y, faces_z, reaction, diagonal, scaling, rim_width = stencil
    margin = rim_width - inner_width
    faces_x = trimmed(faces_x, margin)
    faces_y = trimmed(faces_y, margin)
    faces_z = trimmed(faces_z, margin)
    reaction = trimmed(reaction, margin)
    center = padded[1:-1, 1:-1, 1:-1]
    fluxes = faces_x[1:, 1:-1, 1:-1] * (center - padded[2:, 1:-1, 1:-1])
    fluxes = fluxes + faces_x[:-1, 1:-1, 1:-1] * (center - padded[:-2, 1:-1, 1:-1])
    fluxes = fluxes + faces_y[1:-1, 1:, 1:-1] * (center - padded[1:-1, 2:, 1:-1])
    fluxes = fluxes + faces_y[1:-1, :-1, 1:-1] * (center - padded[1:-1, :-2, 1:-1])
    fluxes = fluxes + faces_z[1:-1, 1:-1, 1:] * (center - padded[1:-1, 1:-1, 2:])
    fluxes = fluxes + faces_z[1:-1, 1:-1, :-1] * (center - padded[1:-1, 1:-1, :-2])
    return scaling * fluxes + reaction[1:-1, 1:-1, 1:-1] * center


def relax(padded, source_now, stencil, inner_width):
    applied = operate(padded, stencil, inner_width)
    diagonal = trimmed(stencil[4], stencil[6] - inner_width)
    return padded[1:-1, 1:-1, 1:-1] + OMEGA * (source_now - applied) / diagonal


def start_field(source_now, stencil):
    return OMEGA * source_now / trimmed(stencil[4], stencil[6] - 1)


def coarsen(array):
    shape = array.shape
    lead = shape[:-3]
    blocks = array.reshape(lead + (shape[-3] // 2, 2, shape[-2] // 2, 2, shape[-1] // 2, 2))
    return jnp.mean(blocks, axis=(-5, -3, -1))


def refine(array):
    return jnp.repeat(jnp.repeat(jnp.repeat(array, 2, axis=0), 2, axis=1), 2, axis=2)


def pad_stack(stacked):
    return jnp.pad(stacked, ((0, 0), (1, 1), (1, 1), (1, 1)))


def reference(source, material, boundary_flags):
    coef = coefficients(material, boundary_flags)
    saved = []
    current = source
    for level_index in range(FINE_LEVELS):
        stencil = prepare(pad_stack(coef), 0.25 ** level_index, 1)
        pressure = start_field(current, stencil)
        for repeat in range(PRE_SWEEPS - 1):
            pressure = relax(jnp.pad(pressure, 1), current, stencil, 1)
        residue = current - operate(jnp.pad(pressure, 1), stencil, 1)
        saved.append((pressure, current, stencil))
        current = coarsen(residue)
        coef = coarsen(coef)
    stencil = prepare(pad_stack(coef), 0.25 ** FINE_LEVELS, 1)
    correction = start_field(current, stencil)
    for repeat in range(COARSE_SWEEPS - 1):
        correction = relax(jnp.pad(correction, 1), current, stencil, 1)
    for level_index in reversed(range(FINE_LEVELS)):
        pressure, current, stencil = saved[level_index]
        pressure = pressure + refine(correction)
        for repeat in range(POST_SWEEPS):
            pressure = relax(jnp.pad(pressure, 1), current, stencil, 1)
        correction = pressure
    residual = source - operate(jnp.pad(correction, 1), saved[0][2], 1)
    return correction, residual
```

```python
import functools

import jax
import jax.numpy as jnp
from jax import lax
from jax.experimental import pallas as pl
from jax.experimental.pallas import tpu as pltpu
from jax.sharding import PartitionSpec as P

F32 = jnp.float32
OMEGA = 0.8
SHIFT = 0.001
ROBIN = 2.0
INVERSE_SOLID = 1.0 / 3.0
INVERSE_DENSE = 0.125
MIB = 1 << 20


def swap(block, axis, parity):
    count = lax.axis_size(axis)
    pairs = [(i, i + 1) for i in range(parity, count - 1, 2)]
    return lax.ppermute(block, axis, pairs + [(b, a) for a, b in pairs])


def swaps(first, second, axis):
    return swap(first, axis, 0), swap(second, axis, 1)


def iota(shape, dim):
    return lax.broadcasted_iota(jnp.int32, shape, dim)


def dot(a, b):
    return lax.dot_general(
        a,
        b,
        (((1,), (0,)), ((), ())),
        precision=lax.Precision.HIGHEST,
        preferred_element_type=F32,
    )


def inverse_density(material):
    return jnp.where(
        material == 0, F32(1.0), jnp.where(material == 1, F32(INVERSE_SOLID), F32(INVERSE_DENSE))
    )


def reaction_of(flags):
    return F32(SHIFT) + F32(ROBIN) * flags.astype(F32)


def recip(x):
    return 1.0 / x


def harmonic(a, b):
    return (2.0 * a * b) * recip(jnp.maximum(a + b, F32(1e-30)))


def coarsen_z0():
    return jnp.where(iota((256, 128), 0) // 2 == iota((256, 128), 1), F32(0.125), F32(0.0))


def coarsen_z1(half):
    lane = iota((128, 128), 1)
    hit = (iota((128, 128), 0) // 2 == lane % 64) & (lane // 64 == half)
    return jnp.where(hit, F32(0.125), F32(0.0))


def coarsen_z2():
    hit = (iota((128, 128), 0) % 64) // 2 == iota((128, 128), 1) % 32
    return jnp.where(hit, F32(0.125), F32(0.0))


def fold_level2(tiles):
    t = dot(tiles, coarsen_z2())
    keep = (iota((64, 128), 0) % 8) // 2 == iota((64, 128), 1) // 32
    t = jnp.where(keep, t, F32(0.0))
    return jnp.sum(t.reshape(8, 8, 128), axis=1)


def pair_rows(ref, count):
    return ref[:, pl.ds(0, count, stride=2), :] + ref[:, pl.ds(1, count, stride=2), :]


def fold_level1(tmp):
    t = pair_rows(tmp, 8)
    return dot(t[0], coarsen_z1(0)) + dot(t[1], coarsen_z1(1))


def next_y(v):
    return pltpu.roll(v, v.shape[0] - 1, 0)


def last_y(v):
    return pltpu.roll(v, 1, 0)


def next_z(v):
    return pltpu.roll(v, v.shape[1] - 1, 1)


def last_z(v):
    return pltpu.roll(v, 1, 1)


def weights(b, c, g, wx, wy, wz, rd, v, scaling, low, high):
    scale = F32(scaling)
    prev = scale * harmonic(b[low - 1], b[low])
    wx[low - 1] = prev
    shape = prev.shape
    inside = iota(shape, 1) < shape[1] - 1

    def body(x, prev):
        here = b[x]
        cur = scale * harmonic(here, b[x + 1])
        wx[x] = cur
        fy = scale * harmonic(here, next_y(here))
        wy[x] = fy
        fz = jnp.where(inside, scale * harmonic(here, next_z(here)), F32(0.0))
        wz[x] = fz
        d = (prev + cur) + (fy + last_y(fy)) + (fz + last_z(fz)) + c[x]
        r = jnp.where(d > 0, F32(OMEGA) * recip(jnp.where(d > 0, d, F32(1.0))), F32(0.0))
        rd[x] = r
        v[x] = r * g[x]
        return cur

    lax.fori_loop(low, high, body, prev)


def rows(v, g, c, wx, wy, wz, low, high, emit):
    first = wx[low - 1] * (v[low - 1] - v[low])

    def body(x, prev):
        here = v[x]
        cur = wx[x] * (here - v[x + 1])
        fy = wy[x] * (here - next_y(here))
        fz = wz[x] * (here - next_z(here))
        flux = (cur - prev) + (fy - last_y(fy)) + (fz - last_z(fz))
        emit(x, here, g[x] - (flux + c[x] * here))
        return cur

    lax.fori_loop(low, high, body, first)


def sweep(src, dst, g, c, wx, wy, wz, rd, low, high):
    def emit(x, here, res):
        dst[x] = here + rd[x] * res

    rows(src, g, c, wx, wy, wz, low, high, emit)


def k_pack_x0(idx, m, f, g, s0, s1):
    even = lax.rem(idx[0], 2) == 0
    for out, high in ((s0, even), (s1, jnp.logical_not(even))):
        four = jnp.where(high, 4, 0)
        three = jnp.where(high, 5, 0)
        for k in range(4):
            out[k] = inverse_density(m[four + k])
        for k in range(3):
            out[4 + k] = reaction_of(f[three + k])
            out[7 + k] = g[three + k]


def k_coefs(m, f, b1, c1, bc2, tmp0, tmp1):
    z0 = coarsen_z0()
    for k, out in ((0, b1), (1, c1)):
        for x in range(4):
            if k == 0:
                tmp0[x] = inverse_density(m[2 * x]) + inverse_density(m[2 * x + 1])
            else:
                tmp0[x] = reaction_of(f[2 * x]) + reaction_of(f[2 * x + 1])
        for x in range(4):
            out[x] = fold_y0(tmp0, x, z0)
        for x in range(2):
            tmp1[x] = out[2 * x] + out[2 * x + 1]
        bc2[k] = fold_level1(tmp1)


def fold_y0(tmp, x, z0):
    low = tmp[x, :, 0:128]
    high = tmp[x, :, 128:256]
    half = z0[0:128, 0:64]
    del half
    t = dot(low, z0[0:128]) + dot(high, z0[128:256])
    sel = jnp.where(iota((16, 32), 1) // 2 == iota((16, 32), 0), F32(1.0), F32(0.0))
    return dot(sel, t)


def strip_tiles(out, t, value):
    out[t, 0:4, :] = value[:, 0:128]
    out[t, 4:8, :] = value[:, 128:256]


def each_side(odd, low, high, r0, r1, put):
    @pl.when(odd == 0)
    def _():
        put(r0, True)
        put(r1, False)

    @pl.when(odd == 1)
    def _():
        put(r0, False)
        put(r1, True)


def pick_sides(odd, r0, r1):
    def low(k):
        return jnp.where(odd == 0, r1[k], r0[k])

    def high(k):
        return jnp.where(odd == 0, r0[k], r1[k])

    return low, high


def k_pack_y0(idx, m, f, g, r0, r1, s0, s1):
    odd_x = lax.rem(idx[0], 2)
    odd_y = lax.rem(idx[1], 2)

    def fill(out, at):
        cut = pl.ds(at, 4)

        def side(k):
            return r0[k, cut, :], r1[k, cut, :]

        t = 0
        for x in range(-4, 12):
            if 0 <= x < 8:
                val = inverse_density(m[x, cut, :])
            else:
                a, b = side(x + 4 if x < 0 else x - 8)
                val = jnp.where(odd_x == 0, b, a) if x < 0 else jnp.where(odd_x == 0, a, b)
            strip_tiles(out, t, val)
            t += 1
        for base, own in ((4, f), (7, g)):
            for x in range(-3, 11):
                if 0 <= x < 8:
                    val = own[x, cut, :]
                    if base == 4:
                        val = reaction_of(val)
                else:
                    a, b = side(base + (x + 3 if x < 0 else x - 8))
                    val = jnp.where(odd_x == 0, b, a) if x < 0 else jnp.where(odd_x == 0, a, b)
                strip_tiles(out, t, val)
                t += 1

    @pl.when(odd_y == 0)
    def _():
        fill(s0, 28)
        fill(s1, 0)

    @pl.when(odd_y == 1)
    def _():
        fill(s0, 0)
        fill(s1, 28)


def put_strips0(ext, first_row, count, buf, base, high):
    at = 40 if high else 4
    for k in range(count):
        ext[first_row + k, at : at + 4, 0:128] = buf[base + k, 0:4, :]
        ext[first_row + k, at : at + 4, 128:256] = buf[base + k, 4:8, :]


def k_descend0(
    idx, m, f, g, r0x, r1x, r0y, r1y, b1, c1,
    v0, g1, s0, s1, wx, wy, wz, rd, ce, ge,
    be, va, vb, tmp,
):
    odd_x = lax.rem(idx[0], 2)
    odd_y = lax.rem(idx[1], 2)
    zeros = jnp.zeros((16, 8, 256), F32)
    for ext in (be, ce, ge):
        ext[:, 0:8, :] = zeros
        ext[:, 40:48, :] = zeros
    for x in range(8):
        be[4 + x, 8:40, :] = inverse_density(m[x])
        ce[4 + x, 8:40, :] = reaction_of(f[x])
        ge[4 + x, 8:40, :] = g[x]

    def put_x(buf, high):
        for k in range(4):
            be[(12 if high else 0) + k, 8:40, :] = buf[k]
        for k in range(3):
            ce[(12 if high else 1) + k, 8:40, :] = buf[4 + k]
            ge[(12 if high else 1) + k, 8:40, :] = buf[7 + k]

    each_side(odd_x, None, None, r0x, r1x, put_x)

    def put_y(buf, high):
        put_strips0(be, 0, 16, buf, 0, high)
        put_strips0(ce, 1, 14, buf, 16, high)
        put_strips0(ge, 1, 14, buf, 30, high)

    each_side(odd_y, None, None, r0y, r1y, put_y)

    weights(be, ce, ge, wx, wy, wz, rd, va, 1.0, 1, 15)
    sweep(va, vb, ge, ce, wx, wy, wz, rd, 2, 14)
    sweep(vb, va, ge, ce, wx, wy, wz, rd, 3, 13)
    for x in range(8):
        v0[x] = va[4 + x, 8:40, :]

    def emit(x, here, res):
        k = x - 4
        own = res[8:40, :]

        @pl.when(lax.rem(k, 2) == 0)
        def _():
            tmp[k // 2] = own

        @pl.when(lax.rem(k, 2) == 1)
        def _():
            tmp[k // 2] += own

    rows(va, ge, ce, wx, wy, wz, 4, 12, emit)
    z0 = coarsen_z0()
    for x in range(4):
        g1[x] = fold_y0(tmp, x, z0)

    for out, high in ((s0, odd_x == 0), (s1, odd_x == 1)):
        one = jnp.where(high, 1, 0)
        for k in range(4):
            out[k] = b1[k]
        for k in range(3):
            out[4 + k] = c1[one + k]
            out[7 + k] = g1[one + k]


def k_pack_y1(idx, g1, b1, c1, r0, r1, s0, s1):
    odd_x = lax.rem(idx[0], 2)
    odd_y = lax.rem(idx[1], 2)

    def fill(out, at):
        cut = pl.ds(at, 4)
        t = 0
        for own, base, reach in ((b1, 0, 4), (c1, 4, 3), (g1, 7, 3)):
            for x in range(-reach, 4 + reach):
                if 0 <= x < 4:
                    val = own[x, cut, :]
                else:
                    k = base + (x + reach if x < 0 else x - 4)
                    a, b = r0[k, cut, :], r1[k, cut, :]
                    val = jnp.where(odd_x == 0, b, a) if x < 0 else jnp.where(odd_x == 0, a, b)
                half = 4 * (t % 2)
                out[t // 2, half : half + 4, :] = val
                t += 1

    @pl.when(odd_y == 0)
    def _():
        fill(s0, 12)
        fill(s1, 0)

    @pl.when(odd_y == 1)
    def _():
        fill(s0, 0)
        fill(s1, 12)


def k_descend1(
    idx, g1, b1, c1, bc2, v0, r0x, r1x, r0y, r1y,
    v1, pay, sv0, sv1, wx, wy, wz, rd, ce, ge,
    be, va, vb, tmp,
):
    odd_x = lax.rem(idx[0], 2)
    odd_y = lax.rem(idx[1], 2)
    zeros = jnp.zeros((12, 8, 128), F32)
    for ext in (be, ce, ge):
        ext[:, 0:8, :] = zeros
        ext[:, 24:32, :] = zeros
    for x in range(4):
        be[4 + x, 8:24, :] = b1[x]
        ce[4 + x, 8:24, :] = c1[x]
        ge[4 + x, 8:24, :] = g1[x]

    def put_x(buf, high):
        for k in range(4):
            be[(8 if high else 0) + k, 8:24, :] = buf[k]
        for k in range(3):
            ce[(8 if high else 1) + k, 8:24, :] = buf[4 + k]
            ge[(8 if high else 1) + k, 8:24, :] = buf[7 + k]

    each_side(odd_x, None, None, r0x, r1x, put_x)

    def put_y(buf, high):
        at = 24 if high else 4
        t = 0
        for ext, first, count in ((be, 0, 12), (ce, 1, 10), (ge, 1, 10)):
            for k in range(count):
                half = 4 * (t % 2)
                ext[first + k, at : at + 4, :] = buf[t // 2, half : half + 4, :]
                t += 1

    each_side(odd_y, None, None, r0y, r1y, put_y)

    weights(be, ce, ge, wx, wy, wz, rd, va, 0.25, 1, 11)
    sweep(va, vb, ge, ce, wx, wy, wz, rd, 2, 10)
    sweep(vb, va, ge, ce, wx, wy, wz, rd, 3, 9)
    for x in range(4):
        v1[x] = va[4 + x, 8:24, :]

    def emit(x, here, res):
        k = x - 4
        own = res[8:24, :]

        @pl.when(lax.rem(k, 2) == 0)
        def _():
            tmp[k // 2] = own

        @pl.when(lax.rem(k, 2) == 1)
        def _():
            tmp[k // 2] += own

    rows(va, ge, ce, wx, wy, wz, 4, 8, emit)
    g2 = fold_level1(tmp)
    for k in range(8):
        pay[k, 0] = g2
        pay[k, 1] = bc2[0]
        pay[k, 2] = bc2[1]

    for out, high in ((sv0, odd_x == 0), (sv1, odd_x == 1)):
        five = jnp.where(high, 5, 0)
        for k in range(3):
            row = v0[five + k]
            for q in range(2):
                for h in range(2):
                    out[4 * k + 2 * q + h] = row[16 * q : 16 * q + 16, 128 * h : 128 * h + 128]
        for k in range(4):
            out[12 + k] = v1[k]


def k_pack_y2(idx, v0, v1, rv0, rv1, gathered, s0, s1):
    odd_x = lax.rem(idx[0], 2)
    odd_y = lax.rem(idx[1], 2)
    for out in (s0, s1):
        for k in range(3):
            for i in range(8):
                out[8 * k + i] = gathered[i, k]

    def fill(out, high):
        cut = pl.ds(28 if high else 0, 4)
        q = 1 if high else 0
        part = pl.ds(12 if high else 0, 4)
        for t, x in enumerate(range(-3, 11)):
            if 0 <= x < 8:
                strip_tiles(out, 24 + t, v0[x, cut, :])
            else:
                k = 4 * (x + 3 if x < 0 else x - 8) + 2 * q
                for h in range(2):
                    a, b = rv0[k + h, part, :], rv1[k + h, part, :]
                    val = jnp.where(odd_x == 0, b, a) if x < 0 else jnp.where(odd_x == 0, a, b)
                    out[24 + t, 4 * h : 4 * h + 4, :] = val
        for t, x in enumerate(range(-4, 8)):
            if 0 <= x < 4:
                val = v1[x, part, :]
            else:
                k = 12 + (x + 4 if x < 0 else x - 4)
                a, b = rv0[k, part, :], rv1[k, part, :]
                val = jnp.where(odd_x == 0, b, a) if x < 0 else jnp.where(odd_x == 0, a, b)
            half = 4 * (t % 2)
            out[38 + t // 2, half : half + 4, :] = val

    @pl.when(odd_y == 0)
    def _():
        fill(s0, True)
        fill(s1, False)

    @pl.when(odd_y == 1)
    def _():
        fill(s0, False)
        fill(s1, True)


def upper(shape):
    return iota(shape, len(shape) - 1) >= 64


def pair_next(v):
    mask = upper(v[0].shape)
    out = []
    for i in range(8):
        after = v[i + 1] if i < 7 else jnp.zeros_like(v[0])
        out.append(pltpu.roll(jnp.where(mask, v[i], after), 64, 1))
    return out


def pair_last(f):
    mask = upper(f[0].shape)
    out = []
    for i in range(8):
        before = f[i - 1] if i > 0 else jnp.zeros_like(f[0])
        out.append(pltpu.roll(jnp.where(mask, before, f[i]), 64, 1))
    return out


def weights2(b, c, scaling):
    scale = F32(scaling)
    inside = iota(b[0].shape, 1) % 64 < 63
    wx = [scale * harmonic(p, q) for p, q in zip(b, pair_next(b))]
    wy = [scale * harmonic(p, next_y(p)) for p in b]
    wz = [jnp.where(inside, scale * harmonic(p, next_z(p)), F32(0.0)) for p in b]
    back = pair_last(wx)
    rd = []
    for i in range(8):
        d = (wx[i] + back[i]) + (wy[i] + last_y(wy[i])) + (wz[i] + last_z(wz[i])) + c[i]
        rd.append(jnp.where(d > 0, F32(OMEGA) * recip(jnp.where(d > 0, d, F32(1.0))), F32(0.0)))
    return wx, wy, wz, rd


def residual2(v, g, c, wx, wy, wz):
    fx = [w * (p - q) for w, p, q in zip(wx, v, pair_next(v))]
    back = pair_last(fx)
    out = []
    for i in range(8):
        fy = wy[i] * (v[i] - next_y(v[i]))
        fz = wz[i] * (v[i] - next_z(v[i]))
        flux = (fx[i] - back[i]) + (fy - last_y(fy)) + (fz - last_z(fz))
        out.append(g[i] - (flux + c[i] * v[i]))
    return out


def k_descend2(idx, gathered, r0, r1, v2, pay, wx2, wy2, wz2, rd2, ce2, ge2, be2, tmp):
    odd_y = lax.rem(idx[1], 2)
    for k, ext in enumerate((ge2, be2, ce2)):
        for i in range(8):
            ext[i, 8:16, :] = gathered[i, k]

    def put(buf, high):
        at = 16 if high else 0
        for k, ext in enumerate((ge2, be2, ce2)):
            for i in range(8):
                ext[i, at : at + 8, :] = buf[8 * k + i]

    each_side(odd_y, None, None, r0, r1, put)
    b = [be2[i] for i in range(8)]
    c = [ce2[i] for i in range(8)]
    g = [ge2[i] for i in range(8)]
    wx, wy, wz, rd = weights2(b, c, 0.0625)
    for i in range(8):
        wx2[i] = wx[i]
        wy2[i] = wy[i]
        wz2[i] = wz[i]
        rd2[i] = rd[i]
    v = [p * q for p, q in zip(rd, g)]
    for _ in range(2):
        r = residual2(v, g, c, wx, wy, wz)
        v = [p + q * s for p, q, s in zip(v, rd, r)]
    r = residual2(v, g, c, wx, wy, wz)
    for i in range(8):
        v2[i] = v[i]
        tmp[8 * i : 8 * i + 8, :] = r[i][8:16, :]
    folded = [fold_level2(tmp[...])]
    for k in (1, 2):
        for i in range(8):
            tmp[8 * i : 8 * i + 8, :] = gathered[i, k]
        folded.append(fold_level2(tmp[...]))
    for j in range(32):
        for k in range(3):
            pay[j, k] = folded[k]


def block_next(v):
    head = iota(v[0].shape, 1) < 32
    out = []
    for t in range(7):
        after = v[t + 1] if t < 6 else jnp.zeros_like(v[0])
        out.append(pltpu.roll(jnp.where(head, after, v[t]), 96, 1))
    return out


def block_last(f):
    tail = iota(f[0].shape, 1) >= 96
    out = []
    for t in range(7):
        before = f[t - 1] if t > 0 else jnp.zeros_like(f[0])
        out.append(pltpu.roll(jnp.where(tail, before, f[t]), 32, 1))
    return out


def solve3(g, b, c):
    scale = F32(0.015625)
    shape = g[0].shape
    inside_x = iota(shape, 0) < 7
    inside_z = iota(shape, 1) % 32 < 31
    zero = F32(0.0)
    wx = [jnp.where(inside_x, scale * harmonic(p, next_y(p)), zero) for p in b]
    wy = [scale * harmonic(p, q) for p, q in zip(b, block_next(b))]
    wz = [jnp.where(inside_z, scale * harmonic(p, next_z(p)), zero) for p in b]
    back = block_last(wy)
    rd = []
    for t in range(7):
        d = (wx[t] + last_y(wx[t])) + (wy[t] + back[t]) + (wz[t] + last_z(wz[t])) + c[t]
        rd.append(jnp.where(d > 0, F32(OMEGA) * recip(jnp.where(d > 0, d, F32(1.0))), zero))
    e = [p * q for p, q in zip(rd, g)]
    for _ in range(7):
        fy = [w * (p - q) for w, p, q in zip(wy, e, block_next(e))]
        back = block_last(fy)
        new = []
        for t in range(7):
            fx = wx[t] * (e[t] - next_y(e[t]))
            fz = wz[t] * (e[t] - next_z(e[t]))
            flux = (fx - last_y(fx)) + (fy[t] - back[t]) + (fz - last_z(fz))
            new.append(e[t] + rd[t] * (g[t] - (flux + c[t] * e[t])))
        e = new
    return e


def k_ascend(
    idx, coarse,
    v2, wx2, wy2, wz2, rd2, ce2, ge2,
    v1, wx1, wy1, wz1, rd1, ce1, ge1,
    v0, wx0, wy0, wz0, rd0, ce0, ge0,
    rv0, rv1, r0y, r1y,
    pressure, residual,
    e3, m2, p2, p1a, p1b, p0a, p0b,
):
    ix = idx[0]
    iy = idx[1]
    odd_x = lax.rem(ix, 2)
    odd_y = lax.rem(iy, 2)
    zero = F32(0.0)

    parts = ([], [], [])
    for t in range(7):
        at = iy + (t - 3)
        inside = jnp.logical_and(at >= 0, at < 32)
        at = jnp.clip(at, 0, 31)
        for k in range(3):
            parts[k].append(jnp.where(inside, coarse[at, k], zero))
    e = solve3(*parts)
    for t in range(3):
        e3[t] = e[2 + t]

    group = iota((8, 128), 1) // 32 == iota((8, 128), 0) // 2
    for i in range(8):
        for t in range(3):
            row = jnp.broadcast_to(e3[t, i : i + 1, :], (8, 128))
            m2[24 * i + 8 * t : 24 * i + 8 * t + 8, :] = jnp.where(group, row, zero)
    spread = jnp.where(
        iota((128, 128), 0) % 32 == (iota((128, 128), 1) % 64) // 2, F32(1.0), zero
    )
    fine = dot(m2[...], spread)
    v = [v2[i] + fine[24 * i : 24 * i + 24, :] for i in range(8)]
    g = [ge2[i] for i in range(8)]
    c = [ce2[i] for i in range(8)]
    wx = [wx2[i] for i in range(8)]
    wy = [wy2[i] for i in range(8)]
    wz = [wz2[i] for i in range(8)]
    for _ in range(2):
        r = residual2(v, g, c, wx, wy, wz)
        v = [v[i] + rd2[i] * r[i] for i in range(8)]
    for i in range(8):
        p2[i] = v[i]

    p1a[...] = jnp.zeros((12, 32, 128), F32)
    for x in range(4):
        p1a[4 + x, 8:24, :] = v1[x]

    def put_x1(buf, high):
        for k in range(4):
            p1a[(8 if high else 0) + k, 8:24, :] = buf[12 + k]

    each_side(odd_x, None, None, rv0, rv1, put_x1)

    def put_y1(buf, high):
        at = 24 if high else 4
        for t in range(12):
            half = 4 * (t % 2)
            p1a[t, at : at + 4, :] = buf[38 + t // 2, half : half + 4, :]

    each_side(odd_y, None, None, r0y, r1y, put_y1)

    double16 = jnp.where(iota((32, 16), 0) // 2 == iota((32, 16), 1), F32(1.0), zero)
    lane = iota((128, 128), 0)
    for q in range(3):
        at = ix + (q - 1)
        inside = jnp.logical_and(at >= 0, at < 8)
        at = jnp.clip(at, 0, 7)
        src = jnp.where(inside, p2[at, 4:20, :], zero)
        tall = dot(double16, src)
        for h in range(2):
            hit = (lane % 64 == iota((128, 128), 1) // 2) & (lane // 64 == h)
            fine = dot(tall, jnp.where(hit, F32(1.0), zero))
            for x in range(2):
                row = 4 * q + 2 * h + x
                p1a[row] = p1a[row] + fine
    sweep(p1a, p1b, ge1, ce1, wx1, wy1, wz1, rd1, 1, 11)
    sweep(p1b, p1a, ge1, ce1, wx1, wy1, wz1, rd1, 2, 10)

    p0a[...] = jnp.zeros((16, 48, 256), F32)
    for x in range(8):
        p0a[4 + x, 8:40, :] = v0[x]

    def put_x0(buf, high):
        for k in range(3):
            for q in range(2):
                for h in range(2):
                    p0a[(12 if high else 1) + k, 8 + 16 * q : 24 + 16 * q, 128 * h : 128 * h + 128] = (
                        buf[4 * k + 2 * q + h]
                    )

    each_side(odd_x, None, None, rv0, rv1, put_x0)

    def put_y0(buf, high):
        put_strips0(p0a, 1, 14, buf, 24, high)

    each_side(odd_y, None, None, r0y, r1y, put_y0)

    double24 = jnp.where(iota((48, 24), 0) // 2 == iota((48, 24), 1), F32(1.0), zero)
    wide = jnp.where(iota((128, 256), 0) == iota((128, 256), 1) // 2, F32(1.0), zero)
    for x in range(8):
        fine = dot(dot(double24, p1a[2 + x, 4:28, :]), wide)
        for h in range(2):
            row = 2 * x + h
            p0a[row] = p0a[row] + fine
    sweep(p0a, p0b, ge0, ce0, wx0, wy0, wz0, rd0, 2, 14)
    sweep(p0b, p0a, ge0, ce0, wx0, wy0, wz0, rd0, 3, 13)

    def emit(x, here, res):
        pressure[x - 4] = here[8:40, :]
        residual[x - 4] = res[8:40, :]

    rows(p0a, ge0, ce0, wx0, wy0, wz0, 4, 12, emit)


def call(kernel, name, outs, scratch, limit, *args):
    vmem = pl.BlockSpec(memory_space=pltpu.VMEM)
    smem = pl.BlockSpec(memory_space=pltpu.SMEM)
    return pl.pallas_call(
        kernel,
        name=name,
        out_shape=[jax.ShapeDtypeStruct(s, F32) for s in outs],
        in_specs=[smem if a.ndim == 1 else vmem for a in args],
        out_specs=[vmem for _ in outs],
        scratch_shapes=[pltpu.VMEM(s, F32) for s in scratch],
        compiler_params=pltpu.CompilerParams(vmem_limit_bytes=limit * MIB),
    )(*args)


E0 = (16, 48, 256)
E1 = (12, 32, 128)
E2 = (8, 24, 128)


def per_device(source, material, flags):
    idx = jnp.stack([lax.axis_index("gx"), lax.axis_index("gy")]).astype(jnp.int32)

    s0, s1 = call(k_pack_x0, "pack_x0", [(10, 32, 256)] * 2, [], 8, idx, material, flags, source)
    r0x, r1x = swaps(s0, s1, "gx")
    b1, c1, bc2 = call(
        k_coefs, "coefs", [(4, 16, 128), (4, 16, 128), (2, 8, 128)],
        [(4, 32, 256), (2, 16, 128)], 8, material, flags,
    )
    s0, s1 = call(
        k_pack_y0, "pack_y0", [(44, 8, 128)] * 2, [], 8, idx, material, flags, source, r0x, r1x
    )
    r0y, r1y = swaps(s0, s1, "gy")
    v0, g1, s0, s1, wx0, wy0, wz0, rd0, ce0, ge0 = call(
        k_descend0, "descend0",
        [(8, 32, 256), (4, 16, 128), (10, 16, 128), (10, 16, 128)] + [E0] * 6,
        [E0, E0, E0, (4, 32, 256)], 24,
        idx, material, flags, source, r0x, r1x, r0y, r1y, b1, c1,
    )
    r0x, r1x = swaps(s0, s1, "gx")
    s0, s1 = call(k_pack_y1, "pack_y1", [(16, 8, 128)] * 2, [], 8, idx, g1, b1, c1, r0x, r1x)
    r0y, r1y = swaps(s0, s1, "gy")
    v1, pay, sv0, sv1, wx1, wy1, wz1, rd1, ce1, ge1 = call(
        k_descend1, "descend1",
        [(4, 16, 128), (8, 3, 8, 128), (16, 16, 128), (16, 16, 128)] + [E1] * 6,
        [E1, E1, E1, (2, 16, 128)], 16,
        idx, g1, b1, c1, bc2, v0, r0x, r1x, r0y, r1y,
    )
    gathered = lax.all_to_all(pay, "gx", 0, 0)
    rv0, rv1 = swaps(sv0, sv1, "gx")
    s0, s1 = call(
        k_pack_y2, "pack_y2", [(44, 8, 128)] * 2, [], 8, idx, v0, v1, rv0, rv1, gathered
    )
    r0y, r1y = swaps(s0, s1, "gy")
    v2, pay, wx2, wy2, wz2, rd2, ce2, ge2 = call(
        k_descend2, "descend2",
        [E2, (32, 3, 8, 128)] + [E2] * 6,
        [E2, (64, 128)], 16,
        idx, gathered, r0y, r1y,
    )
    coarse = lax.all_to_all(pay, "gy", 0, 0)
    pressure, residual = call(
        k_ascend, "ascend",
        [(8, 32, 256)] * 2,
        [(3, 8, 128), (192, 128), E2, E1, E1, E0, E0], 32,
        idx, coarse,
        v2, wx2, wy2, wz2, rd2, ce2, ge2,
        v1, wx1, wy1, wz1, rd1, ce1, ge1,
        v0, wx0, wy0, wz0, rd0, ce0, ge0,
        rv0, rv1, r0y, r1y,
    )
    return pressure, residual


def solution(mesh):
    spec = P("gx", "gy", None)
    return jax.shard_map(
        per_device,
        mesh=mesh,
        in_specs=(spec, spec, spec),
        out_specs=(spec, spec),
        check_vma=False,
    )
```

```python
import jax
import jax.numpy as jnp
from jax import lax
from jax.experimental import pallas as pl
from jax.experimental.pallas import tpu as pltpu
from jax.sharding import PartitionSpec as P

F32 = jnp.float32
BF16 = jnp.bfloat16
OMEGA = 0.8
SHIFT = 0.001
ROBIN = 2.0
INVERSE_SOLID = 1.0 / 3.0
INVERSE_DENSE = 0.125
MIB = 1 << 20


def shift(block, axis, step):
    count = lax.axis_size(axis)
    return lax.ppermute(block, axis, [(i, (i + step) % count) for i in range(count)])


def exchange(low, high, axis):
    return shift(high, axis, 1), shift(low, axis, -1)


def swap_chips(block, axis, parity):
    count = lax.axis_size(axis)
    pairs = [(i, i + 2) for i in range(count - 2) if (i // 2) % 2 == parity]
    if parity == 1:
        pairs = [(0, 1)] + pairs + [(count - 2, count - 1)]
    return lax.ppermute(block, axis, pairs + [(b, a) for a, b in pairs])


def iota(shape, dim):
    return lax.broadcasted_iota(jnp.int32, shape, dim)


def pick(a, w):
    count = a.shape[0]
    a1 = a.astype(BF16)
    rest = a - a1.astype(F32)
    a2 = rest.astype(BF16)
    a3 = (rest - a2.astype(F32)).astype(BF16)
    out = jnp.dot(
        jnp.concatenate([a1, a2, a3], axis=0), w.astype(BF16), preferred_element_type=F32
    )
    return out[:count] + out[count : 2 * count] + out[2 * count :]


def inverse_density(material):
    return jnp.where(
        material == 0, F32(1.0), jnp.where(material == 1, F32(INVERSE_SOLID), F32(INVERSE_DENSE))
    )


def reaction_of(flags):
    return F32(SHIFT) + F32(ROBIN) * flags.astype(F32)


def harmonic(a, b):
    return (2.0 * a * b) * (1.0 / jnp.maximum(a + b, F32(1e-30)))


def step_of(d):
    return jnp.where(d > 0, F32(OMEGA) / jnp.where(d > 0, d, F32(1.0)), F32(0.0))


def fold_level0(tmp):
    parts = []
    for h in range(2):
        parts.append(
            jnp.concatenate(
                [
                    tmp[x, h, pl.ds(0, 16, stride=2), :] + tmp[x, h, pl.ds(1, 16, stride=2), :]
                    for x in range(4)
                ],
                axis=0,
            )
        )
    w = jnp.where(iota((256, 128), 0) // 2 == iota((256, 128), 1), F32(0.125), F32(0.0))
    return pick(jnp.concatenate(parts, axis=1), w)


def fold_level1(tmp):
    parts = [
        tmp[x, pl.ds(0, 8, stride=2), :] + tmp[x, pl.ds(1, 8, stride=2), :] for x in range(2)
    ]
    row = iota((256, 128), 0)
    lane = iota((256, 128), 1)
    hit = ((row % 128) // 2 == lane % 64) & (row // 128 == lane // 64)
    return pick(jnp.concatenate(parts, axis=1), jnp.where(hit, F32(0.125), F32(0.0)))


def fold_level2(tiles):
    count = tiles.shape[0] // 64
    hit = (iota((128, 128), 0) % 64) // 2 == iota((128, 128), 1) % 32
    t = pick(tiles, jnp.where(hit, F32(0.125), F32(0.0))).reshape(count, 8, 8, 128)
    keep = iota(t.shape, 2) // 2 == iota(t.shape, 3) // 32
    t = jnp.sum(jnp.where(keep, t, F32(0.0)), axis=2)
    return [t[k] for k in range(count)]


def next_y(v):
    return pltpu.roll(v, v.shape[0] - 1, 0)


def last_y(v):
    return pltpu.roll(v, 1, 0)


def next_z(v):
    return pltpu.roll(v, v.shape[1] - 1, 1)


def last_z(v):
    return pltpu.roll(v, 1, 1)


def weights(b, s, v, scaling, low, high, unroll):
    wx, wy, wz, wl, rd, c, g = s
    scale = F32(scaling)
    prev = scale * harmonic(b[low - 1], b[low])
    wx[low - 1] = prev
    shape = prev.shape
    inside = iota(shape, 1) < shape[1] - 1

    def body(x, prev):
        here = b[x]
        cur = scale * harmonic(here, b[x + 1])
        wx[x] = cur
        fy = scale * harmonic(here, next_y(here))
        wy[x] = fy
        fz = jnp.where(inside, scale * harmonic(here, next_z(here)), F32(0.0))
        wz[x] = fz
        fl = last_z(fz)
        wl[x] = fl
        r = step_of((prev + cur) + (fy + last_y(fy)) + (fz + fl) + c[x])
        rd[x] = r
        v[x] = r * g[x]
        return cur

    lax.fori_loop(low, high, body, prev, unroll=unroll)


def row_residual(v, s, x, prev):
    wx, wy, wz, wl, rd, c, g = s
    here = v[x]
    cur = wx[x] * (here - v[x + 1])
    fy = wy[x] * (here - next_y(here))
    fz = wz[x] * (here - next_z(here)) + wl[x] * (here - last_z(here))
    flux = (cur - prev) + (fy - last_y(fy)) + fz
    return here, g[x] - (flux + c[x] * here), cur


def sweep(src, dst, s, low, high, unroll):
    rd = s[4]

    def body(x, prev):
        here, res, cur = row_residual(src, s, x, prev)
        dst[x] = here + rd[x] * res
        return cur

    first = s[0][low - 1] * (src[low - 1] - src[low])
    lax.fori_loop(low, high, body, first, unroll=unroll)


def residual_rows(v, s, low, high):
    prev = s[0][low - 1] * (v[low - 1] - v[low])
    for x in range(low, high):
        here, res, prev = row_residual(v, s, x, prev)
        yield x, here, res


def gate(inside, value):
    return jnp.where(inside, value, F32(0.0))


def k_pack_x0(idx, m, f, g, low, high, b0, c0, g0, mv, fv, sems):
    copies = [
        pltpu.make_async_copy(m, mv, sems.at[0]),
        pltpu.make_async_copy(f, fv, sems.at[1]),
        pltpu.make_async_copy(g, g0, sems.at[2]),
    ]
    for copy in copies:
        copy.start()
    copies[0].wait()
    for x in range(8):
        b0[x] = inverse_density(mv[x])
    for k in range(4):
        low[k] = gate(idx[0] > 0, b0[k])
        high[k] = gate(idx[0] < idx[2] - 1, b0[4 + k])
    copies[1].wait()
    for x in range(8):
        c0[x] = reaction_of(fv[x])
    for k in range(3):
        low[4 + k] = c0[k]
        high[4 + k] = c0[5 + k]
    copies[2].wait()
    for k in range(3):
        low[7 + k] = g0[k]
        high[7 + k] = g0[5 + k]


def split_pair(tmp, k, value):
    for h in range(2):
        tmp[k, h] = value[:, 128 * h : 128 * h + 128]


def k_coefs(b0, c0, b1, c1, bc2, tmp0, tmp1):
    for k, (src, out) in enumerate(((b0, b1), (c0, c1))):
        for x in range(4):
            split_pair(tmp0, x, src[2 * x] + src[2 * x + 1])
        t = fold_level0(tmp0)
        for x in range(4):
            out[x] = t[16 * x : 16 * x + 16]
        for x in range(2):
            tmp1[x] = t[32 * x : 32 * x + 16] + t[32 * x + 16 : 32 * x + 32]
        bc2[k] = fold_level1(tmp1)


def strip_tiles(out, t, value):
    out[t, 0:4, :] = value[:, 0:128]
    out[t, 4:8, :] = value[:, 128:256]


def k_pack_y0(idx, b0, c0, g0, below, above, low, high):
    for out, at, inside in ((low, 0, idx[1] > 0), (high, 28, idx[1] < idx[3] - 1)):
        cut = pl.ds(at, 4)
        t = 0
        for own, base, reach in ((b0, 0, 4), (c0, 4, 3), (g0, 7, 3)):
            for x in range(-reach, 8 + reach):
                if x < 0:
                    val = below[base + x + reach, cut, :]
                elif x < 8:
                    val = own[x, cut, :]
                else:
                    val = above[base + x - 8, cut, :]
                strip_tiles(out, t, gate(inside, val) if base == 0 else val)
                t += 1


def put_strips0(ext, first_row, count, buf, base, high):
    at = 40 if high else 4
    for k in range(count):
        ext[first_row + k, at : at + 4, 0:128] = buf[base + k, 0:4, :]
        ext[first_row + k, at : at + 4, 128:256] = buf[base + k, 4:8, :]


def assemble0(b0, c0, g0, below, above, left, right, be, ce, ge):
    zeros = jnp.zeros((8, 256), F32)
    for ext, own, base, reach, strips in (
        (be, b0, 0, 4, 0), (ce, c0, 4, 3, 16), (ge, g0, 7, 3, 30)
    ):
        for x in range(16):
            ext[x, 0:8, :] = zeros
            ext[x, 40:48, :] = zeros
        for x in range(-reach, 8 + reach):
            if x < 0:
                val = below[base + x + reach]
            elif x < 8:
                val = own[x]
            else:
                val = above[base + x - 8]
            ext[4 + x, 8:40, :] = val
        put_strips0(ext, 4 - reach, 8 + 2 * reach, left, strips, False)
        put_strips0(ext, 4 - reach, 8 + 2 * reach, right, strips, True)


def k_descend0(
    idx, b0, c0, g0, below, above, left, right, b1, c1,
    v0, g1, low, high,
    be, ce, ge, wx, wy, wz, wl, rd, va, vb, tmp,
):
    assemble0(b0, c0, g0, below, above, left, right, be, ce, ge)
    s = (wx, wy, wz, wl, rd, ce, ge)
    weights(be, s, va, 1.0, 1, 15, 7)
    sweep(va, vb, s, 2, 14, 6)
    sweep(vb, va, s, 3, 13, 5)
    for x in range(8):
        v0[x] = va[4 + x, 8:40, :]
    kept = None
    for x, here, res in residual_rows(va, s, 4, 12):
        if x % 2 == 0:
            kept = res[8:40, :]
        else:
            split_pair(tmp, (x - 4) // 2, kept + res[8:40, :])
    t = fold_level0(tmp)
    for x in range(4):
        g1[x] = t[16 * x : 16 * x + 16]
        low[x] = gate(idx[0] > 0, b1[x])
        high[x] = gate(idx[0] < idx[2] - 1, b1[x])
    for k in range(3):
        low[4 + k] = c1[k]
        high[4 + k] = c1[1 + k]
        low[7 + k] = t[16 * k : 16 * k + 16]
        high[7 + k] = t[16 * k + 16 : 16 * k + 32]


def k_pack_y1(idx, g1, b1, c1, below, above, low, high):
    for out, at, inside in ((low, 0, idx[1] > 0), (high, 12, idx[1] < idx[3] - 1)):
        cut = pl.ds(at, 4)
        t = 0
        for own, base, reach in ((b1, 0, 4), (c1, 4, 3), (g1, 7, 3)):
            for x in range(-reach, 4 + reach):
                if x < 0:
                    val = below[base + x + reach, cut, :]
                elif x < 4:
                    val = own[x, cut, :]
                else:
                    val = above[base + x - 4, cut, :]
                half = 4 * (t % 2)
                out[t // 2, half : half + 4, :] = gate(inside, val) if base == 0 else val
                t += 1


def k_descend1(
    idx, g1, b1, c1, bc2, v0, below, above, left, right,
    v1, pay, low, high, be, ce, ge,
    wx, wy, wz, wl, rd, va, vb, tmp,
):
    zeros = jnp.zeros((8, 128), F32)
    t = 0
    for ext, own, base, reach in ((be, b1, 0, 4), (ce, c1, 4, 3), (ge, g1, 7, 3)):
        for x in range(12):
            ext[x, 0:8, :] = zeros
            ext[x, 24:32, :] = zeros
        for x in range(-reach, 4 + reach):
            if x < 0:
                val = below[base + x + reach]
            elif x < 4:
                val = own[x]
            else:
                val = above[base + x - 4]
            ext[4 + x, 8:24, :] = val
            half = 4 * (t % 2)
            ext[4 + x, 4:8, :] = left[t // 2, half : half + 4, :]
            ext[4 + x, 24:28, :] = right[t // 2, half : half + 4, :]
            t += 1

    s = (wx, wy, wz, wl, rd, ce, ge)
    weights(be, s, va, 0.25, 1, 11, 10)
    sweep(va, vb, s, 2, 10, 8)
    sweep(vb, va, s, 3, 9, 6)
    for x in range(4):
        v1[x] = va[4 + x, 8:24, :]
    kept = None
    for x, here, res in residual_rows(va, s, 4, 8):
        if x % 2 == 0:
            kept = res[8:24, :]
        else:
            tmp[(x - 4) // 2] = kept + res[8:24, :]
    g2 = fold_level1(tmp)
    for k in range(8):
        pay[k, 0] = g2
        pay[k, 1] = bc2[0]
        pay[k, 2] = bc2[1]

    for out, first in ((low, 0), (high, 5)):
        for k in range(3):
            for q in range(2):
                for h in range(2):
                    out[4 * k + 2 * q + h] = v0[
                        first + k, 16 * q : 16 * q + 16, 128 * h : 128 * h + 128
                    ]
        for k in range(4):
            out[12 + k] = va[4 + k, 8:24, :]


def k_pack_y2(idx, v0, v1, below, above, gathered, low, high):
    for out, is_high, inside in (
        (low, False, idx[1] > 0), (high, True, idx[1] < idx[3] - 1)
    ):
        for k in range(3):
            for i in range(8):
                val = gathered[i, k]
                out[8 * k + i] = gate(inside, val) if k == 1 else val
        cut = pl.ds(28 if is_high else 0, 4)
        part = pl.ds(12 if is_high else 0, 4)
        q = 1 if is_high else 0
        for t, x in enumerate(range(-3, 11)):
            if 0 <= x < 8:
                strip_tiles(out, 24 + t, v0[x, cut, :])
            else:
                src = below if x < 0 else above
                k = 4 * (x + 3 if x < 0 else x - 8) + 2 * q
                for h in range(2):
                    out[24 + t, 4 * h : 4 * h + 4, :] = src[k + h, part, :]
        for t, x in enumerate(range(-4, 8)):
            if x < 0:
                val = below[12 + x + 4, part, :]
            elif x < 4:
                val = v1[x, part, :]
            else:
                val = above[12 + x - 4, part, :]
            half = 4 * (t % 2)
            out[38 + t // 2, half : half + 4, :] = val


def upper(shape):
    return iota(shape, len(shape) - 1) >= 64


def pair_next(v):
    mask = upper(v[0].shape)
    out = []
    for i in range(8):
        after = v[i + 1] if i < 7 else jnp.zeros_like(v[0])
        out.append(pltpu.roll(jnp.where(mask, v[i], after), 64, 1))
    return out


def pair_last(f):
    mask = upper(f[0].shape)
    out = []
    for i in range(8):
        before = f[i - 1] if i > 0 else jnp.zeros_like(f[0])
        out.append(pltpu.roll(jnp.where(mask, before, f[i]), 64, 1))
    return out


def weights2(b, c, scaling):
    scale = F32(scaling)
    inside = iota(b[0].shape, 1) % 64 < 63
    wx = [scale * harmonic(p, q) for p, q in zip(b, pair_next(b))]
    wy = [scale * harmonic(p, next_y(p)) for p in b]
    wz = [jnp.where(inside, scale * harmonic(p, next_z(p)), F32(0.0)) for p in b]
    back = pair_last(wx)
    rd = []
    for i in range(8):
        d = (wx[i] + back[i]) + (wy[i] + last_y(wy[i])) + (wz[i] + last_z(wz[i])) + c[i]
        rd.append(step_of(d))
    return wx, wy, wz, rd


def residual2(v, g, c, wx, wy, wz):
    fx = [w * (p - q) for w, p, q in zip(wx, v, pair_next(v))]
    back = pair_last(fx)
    out = []
    for i in range(8):
        fy = wy[i] * (v[i] - next_y(v[i]))
        fz = wz[i] * (v[i] - next_z(v[i]))
        flux = (fx[i] - back[i]) + (fy - last_y(fy)) + (fz - last_z(fz))
        out.append(g[i] - (flux + c[i] * v[i]))
    return out


def k_descend2(gathered, left, right, v2, pay, wx2, wy2, wz2, rd2, ce2, ge2, be2, tmp):
    for k, ext in enumerate((ge2, be2, ce2)):
        for i in range(8):
            ext[i, 0:8, :] = left[8 * k + i]
            ext[i, 8:16, :] = gathered[i, k]
            ext[i, 16:24, :] = right[8 * k + i]
    b = [be2[i] for i in range(8)]
    c = [ce2[i] for i in range(8)]
    g = [ge2[i] for i in range(8)]
    wx, wy, wz, rd = weights2(b, c, 0.0625)
    for i in range(8):
        wx2[i] = wx[i]
        wy2[i] = wy[i]
        wz2[i] = wz[i]
        rd2[i] = rd[i]
    v = [p * q for p, q in zip(rd, g)]
    for _ in range(2):
        r = residual2(v, g, c, wx, wy, wz)
        v = [p + q * s for p, q, s in zip(v, rd, r)]
    r = residual2(v, g, c, wx, wy, wz)
    for i in range(8):
        v2[i] = v[i]
    for k, src in enumerate((r, b, c)):
        for t in range(2):
            for i in range(8):
                at = 64 * (2 * k + t) + 8 * i
                tmp[at : at + 8, :] = src[i][4 + 8 * t : 12 + 8 * t, :]
    for t, tile in enumerate(fold_level2(tmp[...])):
        pay[t] = tile


TILES = 6


def block_next(v):
    head = iota(v[0].shape, 1) < 32
    out = []
    for t in range(TILES):
        after = v[t + 1] if t < TILES - 1 else jnp.zeros_like(v[0])
        out.append(pltpu.roll(jnp.where(head, after, v[t]), 96, 1))
    return out


def block_last(f):
    tail = iota(f[0].shape, 1) >= 96
    out = []
    for t in range(TILES):
        before = f[t - 1] if t > 0 else jnp.zeros_like(f[0])
        out.append(pltpu.roll(jnp.where(tail, before, f[t]), 32, 1))
    return out


def solve3(g, b, c):
    scale = F32(0.015625)
    shape = g[0].shape
    inside_x = iota(shape, 0) < 7
    inside_z = iota(shape, 1) % 32 < 31
    zero = F32(0.0)
    wx = [jnp.where(inside_x, scale * harmonic(p, next_y(p)), zero) for p in b]
    wy = [scale * harmonic(p, q) for p, q in zip(b, block_next(b))]
    wz = [jnp.where(inside_z, scale * harmonic(p, next_z(p)), zero) for p in b]
    xl = [last_y(p) for p in wx]
    yl = block_last(wy)
    zl = [last_z(p) for p in wz]
    rd = []
    for t in range(TILES):
        d = (wx[t] + xl[t]) + (wy[t] + yl[t]) + (wz[t] + zl[t]) + c[t]
        rd.append(step_of(d))
    e = [p * q for p, q in zip(rd, g)]
    for _ in range(7):
        up = block_next(e)
        down = block_last(e)
        new = []
        for t in range(TILES):
            h = e[t]
            flux = wx[t] * (h - next_y(h)) + xl[t] * (h - last_y(h))
            flux = flux + (wy[t] * (h - up[t]) + yl[t] * (h - down[t]))
            flux = flux + (wz[t] * (h - next_z(h)) + zl[t] * (h - last_z(h)))
            new.append(h + rd[t] * (g[t] - (flux + c[t] * h)))
        e = new
    return e


def k_prepare(
    b0, c0, g0, below0, above0, left0, right0, be1, ce1, ge1,
    v0, v1, below, above, left, right,
    p0, ce, ge, wx, wy, wz, wl, rd, p1, wx1, wy1, wz1, wl1, rd1,
    be, va, va1,
):
    assemble0(b0, c0, g0, below0, above0, left0, right0, be, ce, ge)
    weights(be, (wx, wy, wz, wl, rd, ce, ge), va, 1.0, 2, 14, 6)
    weights(be1, (wx1, wy1, wz1, wl1, rd1, ce1, ge1), va1, 0.25, 1, 11, 10)
    narrow = jnp.zeros((8, 128), F32)
    wide = jnp.zeros((8, 256), F32)
    for t, x in enumerate(range(-4, 8)):
        p1[t, 0:8, :] = narrow
        p1[t, 24:32, :] = narrow
        if x < 0:
            p1[t, 8:24, :] = below[12 + x + 4]
        elif x < 4:
            p1[t, 8:24, :] = v1[x]
        else:
            p1[t, 8:24, :] = above[12 + x - 4]
        half = 4 * (t % 2)
        p1[t, 4:8, :] = left[38 + t // 2, half : half + 4, :]
        p1[t, 24:28, :] = right[38 + t // 2, half : half + 4, :]
    for x in range(-3, 11):
        p0[4 + x, 0:8, :] = wide
        p0[4 + x, 40:48, :] = wide
        if 0 <= x < 8:
            p0[4 + x, 8:40, :] = v0[x]
        else:
            src = below if x < 0 else above
            k = 4 * (x + 3 if x < 0 else x - 8)
            for q in range(2):
                for h in range(2):
                    p0[4 + x, 8 + 16 * q : 24 + 16 * q, 128 * h : 128 * h + 128] = (
                        src[k + 2 * q + h]
                    )
    put_strips0(p0, 1, 14, left, 24, False)
    put_strips0(p0, 1, 14, right, 24, True)


def k_ascend(
    idx, own3, r0, r1, v2, wx2, wy2, wz2, rd2, ce2, ge2,
    p0, ce0, ge0, wx0, wy0, wz0, wl0, rd0,
    p1, ce1, ge1, wx1, wy1, wz1, wl1, rd1,
    pressure, residual,
    all3, m2, p2, p1a, p1b, p0a, p0b, f1, f0,
):
    ix = idx[0]
    iy = idx[1]
    count = idx[3]
    even_chip = lax.rem(iy // 2, 2) == 0
    zero = F32(0.0)

    for k in range(3):
        first = [jnp.where(even_chip, r1[2 * k + t], r0[2 * k + t]) for t in range(2)]
        last = [jnp.where(even_chip, r0[2 * k + t], r1[2 * k + t]) for t in range(2)]
        at = TILES * k
        all3[at] = gate(iy >= 2, first[0])
        all3[at + 1] = jnp.where(iy >= 2, first[1], gate(iy == 1, first[0]))
        all3[at + 2] = own3[2 * k]
        all3[at + 3] = own3[2 * k + 1]
        all3[at + 4] = jnp.where(iy < count - 2, last[0], gate(iy == count - 2, last[1]))
        all3[at + 5] = gate(iy < count - 2, last[1])
    e = solve3(*[[all3[TILES * k + t] for t in range(TILES)] for k in range(3)])

    group = iota((8, 128), 1) // 32 == iota((8, 128), 0) // 2
    for t in range(2):
        for i in range(8):
            row = jnp.broadcast_to(e[2 + t][i : i + 1, :], (8, 128))
            m2[16 * i + 8 * t : 16 * i + 8 * t + 8, :] = jnp.where(group, row, zero)
    spread = jnp.where(
        iota((128, 128), 0) % 32 == (iota((128, 128), 1) % 64) // 2, F32(1.0), zero
    )
    fine = pick(m2[...], spread)
    for i in range(8):
        p2[i] = v2[i]
        p2[i, 4:20, :] += fine[16 * i : 16 * i + 16, :]
    v = [p2[i] for i in range(8)]
    g = [ge2[i] for i in range(8)]
    c = [ce2[i] for i in range(8)]
    wx = [wx2[i] for i in range(8)]
    wy = [wy2[i] for i in range(8)]
    wz = [wz2[i] for i in range(8)]
    for _ in range(2):
        r = residual2(v, g, c, wx, wy, wz)
        v = [v[i] + rd2[i] * r[i] for i in range(8)]
    for i in range(8):
        p2[i] = v[i]

    parts = []
    for q in range(3):
        at = ix + (q - 1)
        inside = jnp.logical_and(at >= 0, at < idx[2])
        parts.append(jnp.where(inside, p2[jnp.clip(at, 0, 7), 4:20, :], zero))
    row = iota((128, 256), 0)
    lane = iota((128, 256), 1)
    hit = (row % 64 == (lane % 128) // 2) & (row // 64 == lane // 128)
    fine = pick(jnp.concatenate(parts, axis=0), jnp.where(hit, F32(1.0), zero))
    for q in range(3):
        for h in range(2):
            part = fine[16 * q : 16 * q + 16, 128 * h : 128 * h + 128]
            f1[2 * q + h, pl.ds(0, 16, stride=2), :] = part
            f1[2 * q + h, pl.ds(1, 16, stride=2), :] = part
    for x in range(12):
        p1a[x] = p1[x] + f1[x // 2]
    s1 = (wx1, wy1, wz1, wl1, rd1, ce1, ge1)
    sweep(p1a, p1b, s1, 1, 11, 10)
    sweep(p1b, p1a, s1, 2, 10, 8)

    wide = jnp.where(iota((128, 256), 0) == iota((128, 256), 1) // 2, F32(1.0), zero)
    fine = pick(jnp.concatenate([p1a[2 + x, 4:28, :] for x in range(8)], axis=0), wide)
    for x in range(8):
        for h in range(2):
            part = fine[24 * x : 24 * x + 24, 128 * h : 128 * h + 128]
            f0[x, h, pl.ds(0, 24, stride=2), :] = part
            f0[x, h, pl.ds(1, 24, stride=2), :] = part
    for x in range(1, 15):
        for h in range(2):
            cut = pl.ds(128 * h, 128)
            p0a[x, :, cut] = p0[x, :, cut] + f0[x // 2, h]
    s0 = (wx0, wy0, wz0, wl0, rd0, ce0, ge0)
    sweep(p0a, p0b, s0, 2, 14, 6)
    sweep(p0b, p0a, s0, 3, 13, 5)
    for x, here, res in residual_rows(p0a, s0, 4, 12):
        pressure[x - 4] = here[8:40, :]
        residual[x - 4] = res[8:40, :]


def call(kernel, name, outs, scratch, limit, *args, anywhere=()):
    vmem = pl.BlockSpec(memory_space=pltpu.VMEM)
    smem = pl.BlockSpec(memory_space=pltpu.SMEM)
    hbm = pl.BlockSpec(memory_space=pltpu.HBM)
    specs = [smem if a.ndim == 1 else vmem for a in args]
    for k in anywhere:
        specs[k] = hbm
    return pl.pallas_call(
        kernel,
        name=name,
        out_shape=[jax.ShapeDtypeStruct(s, F32) for s in outs],
        in_specs=specs,
        out_specs=[vmem for _ in outs],
        scratch_shapes=[pltpu.VMEM(s, F32) if isinstance(s, tuple) else s for s in scratch],
        compiler_params=pltpu.CompilerParams(vmem_limit_bytes=limit * MIB),
    )(*args)


B0 = (8, 32, 256)
E0 = (16, 48, 256)
E1 = (12, 32, 128)
E2 = (8, 24, 128)


def per_device(source, material, flags):
    idx = jnp.stack(
        [
            lax.axis_index("gx").astype(jnp.int32),
            lax.axis_index("gy").astype(jnp.int32),
            jnp.int32(lax.axis_size("gx")),
            jnp.int32(lax.axis_size("gy")),
        ]
    )

    low, high, b0, c0, g0 = call(
        k_pack_x0, "pack_x0", [(10, 32, 256)] * 2 + [B0] * 3,
        [pltpu.VMEM(B0, jnp.int32), pltpu.VMEM(B0, jnp.int32), pltpu.SemaphoreType.DMA((3,))],
        4, idx, material, flags, source, anywhere=(1, 2, 3),
    )
    below0, above0 = exchange(low, high, "gx")
    b1, c1, bc2 = call(
        k_coefs, "coefs", [(4, 16, 128), (4, 16, 128), (2, 8, 128)],
        [(4, 2, 32, 128), (2, 16, 128)], 4, b0, c0,
    )
    low, high = call(
        k_pack_y0, "pack_y0", [(44, 8, 128)] * 2, [], 4, idx, b0, c0, g0, below0, above0
    )
    left0, right0 = exchange(low, high, "gy")
    blocks0 = (b0, c0, g0, below0, above0, left0, right0)
    v0, g1, low, high = call(
        k_descend0, "descend0",
        [B0, (4, 16, 128), (10, 16, 128), (10, 16, 128)],
        [E0] * 10 + [(4, 2, 32, 128)], 12,
        idx, *blocks0, b1, c1,
    )
    below, above = exchange(low, high, "gx")
    low, high = call(
        k_pack_y1, "pack_y1", [(16, 8, 128)] * 2, [], 4, idx, g1, b1, c1, below, above
    )
    left, right = exchange(low, high, "gy")
    v1, pay, low, high, be1, ce1, ge1 = call(
        k_descend1, "descend1",
        [(4, 16, 128), (8, 3, 8, 128), (16, 16, 128), (16, 16, 128)] + [E1] * 3,
        [E1] * 7 + [(2, 16, 128)], 4,
        idx, g1, b1, c1, bc2, v0, below, above, left, right,
    )
    gathered = lax.all_to_all(pay, "gx", 0, 0)
    below, above = exchange(low, high, "gx")
    low, high = call(
        k_pack_y2, "pack_y2", [(44, 8, 128)] * 2, [], 4, idx, v0, v1, below, above, gathered
    )
    left, right = exchange(low, high, "gy")
    v2, own3, *s2 = call(
        k_descend2, "descend2", [E2, (6, 8, 128)] + [E2] * 6, [E2, (384, 128)], 4,
        gathered, left, right,
    )
    r0, r1 = swap_chips(own3, "gy", 0), swap_chips(own3, "gy", 1)
    p0, ce0, ge0, wx0, wy0, wz0, wl0, rd0, p1, *w1 = call(
        k_prepare, "prepare", [E0] * 8 + [E1] * 6, [E0, E0, E1], 8,
        *blocks0, be1, ce1, ge1, v0, v1, below, above, left, right,
    )
    pressure, residual = call(
        k_ascend, "ascend", [B0] * 2,
        [(18, 8, 128), (128, 128), E2, E1, E1, E0, E0, (6, 32, 128), (8, 2, 48, 128)], 8,
        idx, own3, r0, r1, v2, *s2,
        p0, ce0, ge0, wx0, wy0, wz0, wl0, rd0, p1, ce1, ge1, *w1,
    )
    return pressure, residual


def solution(mesh):
    spec = P("gx", "gy", None)
    return jax.shard_map(
        per_device,
        mesh=mesh,
        in_specs=(spec, spec, spec),
        out_specs=(spec, spec),
        check_vma=False,
    )
```

```python
import jax
import jax.numpy as jnp
from jax import lax
from jax.experimental import pallas as pl
from jax.experimental.pallas import tpu as pltpu
from jax.sharding import PartitionSpec as P

F32 = jnp.float32
BF16 = jnp.bfloat16
OMEGA = 0.8
SHIFT = 0.001
ROBIN = 2.0
INVERSE_SOLID = 1.0 / 3.0
INVERSE_DENSE = 0.125
MIB = 1 << 20


def shift(block, axis, step):
    count = lax.axis_size(axis)
    return lax.ppermute(block, axis, [(i, (i + step) % count) for i in range(count)])


def exchange(low, high, axis):
    return shift(high, axis, 1), shift(low, axis, -1)


def swap_chips(block, axis, parity):
    count = lax.axis_size(axis)
    pairs = [(i, i + 2) for i in range(count - 2) if (i // 2) % 2 == parity]
    if parity == 1:
        pairs = [(0, 1)] + pairs + [(count - 2, count - 1)]
    return lax.ppermute(block, axis, pairs + [(b, a) for a, b in pairs])


def iota(shape, dim):
    return lax.broadcasted_iota(jnp.int32, shape, dim)


def pick(a, w):
    count = a.shape[0]
    a1 = a.astype(BF16)
    rest = a - a1.astype(F32)
    a2 = rest.astype(BF16)
    a3 = (rest - a2.astype(F32)).astype(BF16)
    out = jnp.dot(
        jnp.concatenate([a1, a2, a3], axis=0), w.astype(BF16), preferred_element_type=F32
    )
    return out[:count] + out[count : 2 * count] + out[2 * count :]


def inverse_density(material):
    return jnp.where(
        material == 0, F32(1.0), jnp.where(material == 1, F32(INVERSE_SOLID), F32(INVERSE_DENSE))
    )


def reaction_of(flags):
    return F32(SHIFT) + F32(ROBIN) * flags.astype(F32)


def harmonic(a, b):
    return (2.0 * a * b) * (1.0 / jnp.maximum(a + b, F32(1e-30)))


def step_of(d):
    return jnp.where(d > 0, F32(OMEGA) / jnp.where(d > 0, d, F32(1.0)), F32(0.0))


def fold_level0(tmp):
    parts = []
    for h in range(2):
        parts.append(
            jnp.concatenate(
                [
                    tmp[x, h, pl.ds(0, 16, stride=2), :] + tmp[x, h, pl.ds(1, 16, stride=2), :]
                    for x in range(4)
                ],
                axis=0,
            )
        )
    w = jnp.where(iota((256, 128), 0) // 2 == iota((256, 128), 1), F32(0.125), F32(0.0))
    return pick(jnp.concatenate(parts, axis=1), w)


def fold_level1(tmp):
    parts = [
        tmp[x, pl.ds(0, 8, stride=2), :] + tmp[x, pl.ds(1, 8, stride=2), :] for x in range(2)
    ]
    row = iota((256, 128), 0)
    lane = iota((256, 128), 1)
    hit = ((row % 128) // 2 == lane % 64) & (row // 128 == lane // 64)
    return pick(jnp.concatenate(parts, axis=1), jnp.where(hit, F32(0.125), F32(0.0)))


def fold_level2(tiles):
    count = tiles.shape[0] // 64
    hit = (iota((128, 128), 0) % 64) // 2 == iota((128, 128), 1) % 32
    t = pick(tiles, jnp.where(hit, F32(0.125), F32(0.0))).reshape(count, 8, 8, 128)
    keep = iota(t.shape, 2) // 2 == iota(t.shape, 3) // 32
    t = jnp.sum(jnp.where(keep, t, F32(0.0)), axis=2)
    return [t[k] for k in range(count)]


def next_y(v):
    return pltpu.roll(v, v.shape[0] - 1, 0)


def last_y(v):
    return pltpu.roll(v, 1, 0)


def next_z(v):
    return pltpu.roll(v, v.shape[1] - 1, 1)


def last_z(v):
    return pltpu.roll(v, 1, 1)


def weights(b, s, v, scaling, low, high, unroll):
    wx, wy, wz, wl, rd, c, g = s
    scale = F32(scaling)
    prev = scale * harmonic(b[low - 1], b[low])
    wx[low - 1] = prev
    shape = prev.shape
    inside = iota(shape, 1) < shape[1] - 1

    def body(x, prev):
        here = b[x]
        cur = scale * harmonic(here, b[x + 1])
        wx[x] = cur
        fy = scale * harmonic(here, next_y(here))
        wy[x] = fy
        fz = jnp.where(inside, scale * harmonic(here, next_z(here)), F32(0.0))
        wz[x] = fz
        fl = last_z(fz)
        wl[x] = fl
        r = step_of((prev + cur) + (fy + last_y(fy)) + (fz + fl) + c[x])
        rd[x] = r
        v[x] = r * g[x]
        return cur

    lax.fori_loop(low, high, body, prev, unroll=unroll)


def row_residual(v, s, x, prev):
    wx, wy, wz, wl, rd, c, g = s
    here = v[x]
    cur = wx[x] * (here - v[x + 1])
    fy = wy[x] * (here - next_y(here))
    fz = wz[x] * (here - next_z(here)) + wl[x] * (here - last_z(here))
    flux = (cur - prev) + (fy - last_y(fy)) + fz
    return here, g[x] - (flux + c[x] * here), cur


def sweep(src, dst, s, low, high, unroll):
    rd = s[4]

    def body(x, prev):
        here, res, cur = row_residual(src, s, x, prev)
        dst[x] = here + rd[x] * res
        return cur

    first = s[0][low - 1] * (src[low - 1] - src[low])
    lax.fori_loop(low, high, body, first, unroll=unroll)


def residual_rows(v, s, low, high):
    prev = s[0][low - 1] * (v[low - 1] - v[low])
    for x in range(low, high):
        here, res, prev = row_residual(v, s, x, prev)
        yield x, here, res


def place(axis):
    return lax.axis_index(axis)


def gate(inside, value):
    return jnp.where(inside, value, F32(0.0))


def k_load0(m, f, g, left, right, b0, c0, g0, mv, fv, sems):
    copies = [
        pltpu.make_async_copy(m, mv, sems.at[0]),
        pltpu.make_async_copy(f, fv, sems.at[1]),
        pltpu.make_async_copy(g, g0, sems.at[2]),
    ]
    for copy in copies:
        copy.start()
    copies[0].wait()
    for x in range(8):
        b0[x] = inverse_density(mv[x])
        strip_tiles(left, x, gate(place("gy") > 0, b0[x, 0:4, :]))
        strip_tiles(right, x, gate(place("gy") < lax.axis_size("gy") - 1, b0[x, 28:32, :]))
    copies[1].wait()
    for x in range(8):
        c0[x] = reaction_of(fv[x])
        strip_tiles(left, 8 + x, c0[x, 0:4, :])
        strip_tiles(right, 8 + x, c0[x, 28:32, :])
    copies[2].wait()
    for x in range(8):
        strip_tiles(left, 16 + x, g0[x, 0:4, :])
        strip_tiles(right, 16 + x, g0[x, 28:32, :])


def k_edge0(b0, c0, g0, low, high):
    for k in range(4):
        low[k] = gate(place("gx") > 0, b0[k])
        high[k] = gate(place("gx") < lax.axis_size("gx") - 1, b0[4 + k])
    for k in range(3):
        low[4 + k] = c0[k]
        high[4 + k] = c0[5 + k]
        low[7 + k] = g0[k]
        high[7 + k] = g0[5 + k]


def split_pair(tmp, k, value):
    for h in range(2):
        tmp[k, h] = value[:, 128 * h : 128 * h + 128]


def k_coefs(b0, c0, b1, c1, bc2, tmp0, tmp1):
    for k, (src, out) in enumerate(((b0, b1), (c0, c1))):
        for x in range(4):
            split_pair(tmp0, x, src[2 * x] + src[2 * x + 1])
        t = fold_level0(tmp0)
        for x in range(4):
            out[x] = t[16 * x : 16 * x + 16]
        for x in range(2):
            tmp1[x] = t[32 * x : 32 * x + 16] + t[32 * x + 16 : 32 * x + 32]
        bc2[k] = fold_level1(tmp1)


def strip_tiles(out, t, value):
    out[t, 0:4, :] = value[:, 0:128]
    out[t, 4:8, :] = value[:, 128:256]


def k_corner0(left, right, low, high):
    for side, strips in enumerate((left, right)):
        for k in range(4):
            low[10 * side + k] = gate(place("gx") > 0, strips[k])
            high[10 * side + k] = gate(place("gx") < lax.axis_size("gx") - 1, strips[4 + k])
        for k in range(3):
            low[10 * side + 4 + k] = strips[8 + k]
            high[10 * side + 4 + k] = strips[13 + k]
            low[10 * side + 7 + k] = strips[16 + k]
            high[10 * side + 7 + k] = strips[21 + k]


def put_strip0(ext, row, tile, high):
    at = 40 if high else 4
    ext[row, at : at + 4, 0:128] = tile[0:4, :]
    ext[row, at : at + 4, 128:256] = tile[4:8, :]


def assemble0(b0, c0, g0, below, above, left, right, under, over, be, ce, ge):
    zeros = jnp.zeros((8, 256), F32)
    for which, (ext, own, base, reach) in enumerate(
        ((be, b0, 0, 4), (ce, c0, 4, 3), (ge, g0, 7, 3))
    ):
        for x in range(16):
            ext[x, 0:8, :] = zeros
            ext[x, 40:48, :] = zeros
        for x in range(-reach, 8 + reach):
            if x < 0:
                k = base + x + reach
                val, strips = below[k], (under[k], under[10 + k])
            elif x < 8:
                k = 8 * which + x
                val, strips = own[x], (left[k], right[k])
            else:
                k = base + x - 8
                val, strips = above[k], (over[k], over[10 + k])
            ext[4 + x, 8:40, :] = val
            put_strip0(ext, 4 + x, strips[0], False)
            put_strip0(ext, 4 + x, strips[1], True)


def k_descend0(
    b0, c0, g0, below, above, left, right, under, over, b1, c1,
    v0, g1, low, high,
    be, ce, ge, wx, wy, wz, wl, rd, va, vb, tmp,
):
    assemble0(b0, c0, g0, below, above, left, right, under, over, be, ce, ge)
    s = (wx, wy, wz, wl, rd, ce, ge)
    weights(be, s, va, 1.0, 1, 15, 7)
    sweep(va, vb, s, 2, 14, 6)
    sweep(vb, va, s, 3, 13, 5)
    for x in range(8):
        v0[x] = va[4 + x, 8:40, :]
    kept = None
    for x, here, res in residual_rows(va, s, 4, 12):
        if x % 2 == 0:
            kept = res[8:40, :]
        else:
            split_pair(tmp, (x - 4) // 2, kept + res[8:40, :])
    t = fold_level0(tmp)
    for x in range(4):
        g1[x] = t[16 * x : 16 * x + 16]
        low[x] = gate(place("gx") > 0, b1[x])
        high[x] = gate(place("gx") < lax.axis_size("gx") - 1, b1[x])
    for k in range(3):
        low[4 + k] = c1[k]
        high[4 + k] = c1[1 + k]
        low[7 + k] = t[16 * k : 16 * k + 16]
        high[7 + k] = t[16 * k + 16 : 16 * k + 32]


def k_pack_y1(g1, b1, c1, v0, below, above, low, high, vlow, vhigh):
    for out, at, inside in ((low, 0, place("gy") > 0), (high, 12, place("gy") < lax.axis_size("gy") - 1)):
        cut = pl.ds(at, 4)
        t = 0
        for own, base, reach in ((b1, 0, 4), (c1, 4, 3), (g1, 7, 3)):
            for x in range(-reach, 4 + reach):
                if x < 0:
                    val = below[base + x + reach, cut, :]
                elif x < 4:
                    val = own[x, cut, :]
                else:
                    val = above[base + x - 4, cut, :]
                half = 4 * (t % 2)
                out[t // 2, half : half + 4, :] = gate(inside, val) if base == 0 else val
                t += 1
        for x in range(8):
            strip_tiles(out, 16 + x, v0[x, pl.ds(0 if at == 0 else 28, 4), :])
    for k in range(3):
        vlow[k] = v0[k]
        vhigh[k] = v0[5 + k]


def k_descend1(
    g1, b1, c1, bc2, below, above, left, right,
    v1, pay, low, high, be, ce, ge,
    wx, wy, wz, wl, rd, va, vb, tmp,
):
    zeros = jnp.zeros((8, 128), F32)
    t = 0
    for ext, own, base, reach in ((be, b1, 0, 4), (ce, c1, 4, 3), (ge, g1, 7, 3)):
        for x in range(12):
            ext[x, 0:8, :] = zeros
            ext[x, 24:32, :] = zeros
        for x in range(-reach, 4 + reach):
            if x < 0:
                val = below[base + x + reach]
            elif x < 4:
                val = own[x]
            else:
                val = above[base + x - 4]
            ext[4 + x, 8:24, :] = val
            half = 4 * (t % 2)
            ext[4 + x, 4:8, :] = left[t // 2, half : half + 4, :]
            ext[4 + x, 24:28, :] = right[t // 2, half : half + 4, :]
            t += 1

    s = (wx, wy, wz, wl, rd, ce, ge)
    weights(be, s, va, 0.25, 1, 11, 10)
    sweep(va, vb, s, 2, 10, 8)
    sweep(vb, va, s, 3, 9, 6)
    for x in range(4):
        v1[x] = va[4 + x, 8:24, :]
    kept = None
    for x, here, res in residual_rows(va, s, 4, 8):
        if x % 2 == 0:
            kept = res[8:24, :]
        else:
            tmp[(x - 4) // 2] = kept + res[8:24, :]
    g2 = fold_level1(tmp)
    for k in range(8):
        pay[k, 0] = g2
        pay[k, 1] = bc2[0]
        pay[k, 2] = bc2[1]

    for out, first in ((low, 0), (high, 5)):
        for k in range(4):
            for q in range(2):
                out[2 * k + q] = va[4 + k, 8 + 8 * q : 16 + 8 * q, :]
        for k in range(3):
            out[8 + k] = left[16 + first + k]
            out[11 + k] = right[16 + first + k]


def k_pack_y2(v1, below, above, gathered, low, high):
    for out, is_high, inside in (
        (low, False, place("gy") > 0), (high, True, place("gy") < lax.axis_size("gy") - 1)
    ):
        for k in range(3):
            for i in range(8):
                val = gathered[i, k]
                out[8 * k + i] = gate(inside, val) if k == 1 else val
        q = 1 if is_high else 0
        cut = pl.ds(4 * q, 4)
        for t, x in enumerate(range(-4, 8)):
            if x < 0:
                val = below[2 * (x + 4) + q, cut, :]
            elif x < 4:
                val = v1[x, pl.ds(12 * q, 4), :]
            else:
                val = above[2 * (x - 4) + q, cut, :]
            half = 4 * (t % 2)
            out[24 + t // 2, half : half + 4, :] = val


def upper(shape):
    return iota(shape, len(shape) - 1) >= 64


def pair_next(v):
    mask = upper(v[0].shape)
    out = []
    for i in range(8):
        after = v[i + 1] if i < 7 else jnp.zeros_like(v[0])
        out.append(pltpu.roll(jnp.where(mask, v[i], after), 64, 1))
    return out


def pair_last(f):
    mask = upper(f[0].shape)
    out = []
    for i in range(8):
        before = f[i - 1] if i > 0 else jnp.zeros_like(f[0])
        out.append(pltpu.roll(jnp.where(mask, before, f[i]), 64, 1))
    return out


def weights2(b, c, scaling):
    scale = F32(scaling)
    inside = iota(b[0].shape, 1) % 64 < 63
    wx = [scale * harmonic(p, q) for p, q in zip(b, pair_next(b))]
    wy = [scale * harmonic(p, next_y(p)) for p in b]
    wz = [jnp.where(inside, scale * harmonic(p, next_z(p)), F32(0.0)) for p in b]
    back = pair_last(wx)
    rd = []
    for i in range(8):
        d = (wx[i] + back[i]) + (wy[i] + last_y(wy[i])) + (wz[i] + last_z(wz[i])) + c[i]
        rd.append(step_of(d))
    return wx, wy, wz, rd


def residual2(v, g, c, wx, wy, wz):
    fx = [w * (p - q) for w, p, q in zip(wx, v, pair_next(v))]
    back = pair_last(fx)
    out = []
    for i in range(8):
        fy = wy[i] * (v[i] - next_y(v[i]))
        fz = wz[i] * (v[i] - next_z(v[i]))
        flux = (fx[i] - back[i]) + (fy - last_y(fy)) + (fz - last_z(fz))
        out.append(g[i] - (flux + c[i] * v[i]))
    return out


def k_descend2(gathered, left, right, v2, pay, wx2, wy2, wz2, rd2, ce2, ge2, be2, tmp):
    for k, ext in enumerate((ge2, be2, ce2)):
        for i in range(8):
            ext[i, 0:8, :] = left[8 * k + i]
            ext[i, 8:16, :] = gathered[i, k]
            ext[i, 16:24, :] = right[8 * k + i]
    b = [be2[i] for i in range(8)]
    c = [ce2[i] for i in range(8)]
    g = [ge2[i] for i in range(8)]
    wx, wy, wz, rd = weights2(b, c, 0.0625)
    for i in range(8):
        wx2[i] = wx[i]
        wy2[i] = wy[i]
        wz2[i] = wz[i]
        rd2[i] = rd[i]
    v = [p * q for p, q in zip(rd, g)]
    for _ in range(2):
        r = residual2(v, g, c, wx, wy, wz)
        v = [p + q * s for p, q, s in zip(v, rd, r)]
    r = residual2(v, g, c, wx, wy, wz)
    for i in range(8):
        v2[i] = v[i]
    for k, src in enumerate((r, b, c)):
        for t in range(2):
            for i in range(8):
                at = 64 * (2 * k + t) + 8 * i
                tmp[at : at + 8, :] = src[i][4 + 8 * t : 12 + 8 * t, :]
    for t, tile in enumerate(fold_level2(tmp[...])):
        pay[t] = tile


TILES = 6


def block_next(v):
    head = iota(v[0].shape, 1) < 32
    out = []
    for t in range(TILES):
        after = v[t + 1] if t < TILES - 1 else jnp.zeros_like(v[0])
        out.append(pltpu.roll(jnp.where(head, after, v[t]), 96, 1))
    return out


def block_last(f):
    tail = iota(f[0].shape, 1) >= 96
    out = []
    for t in range(TILES):
        before = f[t - 1] if t > 0 else jnp.zeros_like(f[0])
        out.append(pltpu.roll(jnp.where(tail, before, f[t]), 32, 1))
    return out


def solve3(g, b, c):
    scale = F32(0.015625)
    shape = g[0].shape
    inside_x = iota(shape, 0) < 7
    inside_z = iota(shape, 1) % 32 < 31
    zero = F32(0.0)
    wx = [jnp.where(inside_x, scale * harmonic(p, next_y(p)), zero) for p in b]
    wy = [scale * harmonic(p, q) for p, q in zip(b, block_next(b))]
    wz = [jnp.where(inside_z, scale * harmonic(p, next_z(p)), zero) for p in b]
    xl = [last_y(p) for p in wx]
    yl = block_last(wy)
    zl = [last_z(p) for p in wz]
    rd = []
    for t in range(TILES):
        d = (wx[t] + xl[t]) + (wy[t] + yl[t]) + (wz[t] + zl[t]) + c[t]
        rd.append(step_of(d))
    e = [p * q for p, q in zip(rd, g)]
    for _ in range(7):
        up = block_next(e)
        down = block_last(e)
        new = []
        for t in range(TILES):
            h = e[t]
            flux = wx[t] * (h - next_y(h)) + xl[t] * (h - last_y(h))
            flux = flux + (wy[t] * (h - up[t]) + yl[t] * (h - down[t]))
            flux = flux + (wz[t] * (h - next_z(h)) + zl[t] * (h - last_z(h)))
            new.append(h + rd[t] * (g[t] - (flux + c[t] * h)))
        e = new
    return e


def k_prepare(
    b0, c0, g0, below0, above0, left0, right0, under0, over0, be1, ce1, ge1,
    v0, below, above, left, right, v1, below1, above1, left1, right1,
    p0, ce, ge, wx, wy, wz, wl, rd, p1, wx1, wy1, wz1, wl1, rd1,
    be, va, va1,
):
    assemble0(b0, c0, g0, below0, above0, left0, right0, under0, over0, be, ce, ge)
    weights(be, (wx, wy, wz, wl, rd, ce, ge), va, 1.0, 2, 14, 6)
    weights(be1, (wx1, wy1, wz1, wl1, rd1, ce1, ge1), va1, 0.25, 1, 11, 10)
    narrow = jnp.zeros((8, 128), F32)
    wide = jnp.zeros((8, 256), F32)
    for t, x in enumerate(range(-4, 8)):
        p1[t, 0:8, :] = narrow
        p1[t, 24:32, :] = narrow
        if 0 <= x < 4:
            p1[t, 8:24, :] = v1[x]
        else:
            for q in range(2):
                src, k = (below1, x + 4) if x < 0 else (above1, x - 4)
                p1[t, 8 + 8 * q : 16 + 8 * q, :] = src[2 * k + q]
        half = 4 * (t % 2)
        p1[t, 4:8, :] = left1[24 + t // 2, half : half + 4, :]
        p1[t, 24:28, :] = right1[24 + t // 2, half : half + 4, :]
    for x in range(-3, 11):
        p0[4 + x, 0:8, :] = wide
        p0[4 + x, 40:48, :] = wide
        if x < 0:
            k = x + 3
            val, strips = below[k], (below1[8 + k], below1[11 + k])
        elif x < 8:
            val, strips = v0[x], (left[16 + x], right[16 + x])
        else:
            k = x - 8
            val, strips = above[k], (above1[8 + k], above1[11 + k])
        p0[4 + x, 8:40, :] = val
        put_strip0(p0, 4 + x, strips[0], False)
        put_strip0(p0, 4 + x, strips[1], True)


def k_ascend(
    own3, r0, r1, v2, wx2, wy2, wz2, rd2, ce2, ge2,
    p0, ce0, ge0, wx0, wy0, wz0, wl0, rd0,
    p1, ce1, ge1, wx1, wy1, wz1, wl1, rd1,
    pressure, residual,
    all3, m2, p2, p1a, p1b, p0a, p0b, f1, f0,
):
    ix = place("gx")
    iy = place("gy")
    count = lax.axis_size("gy")
    even_chip = lax.rem(iy // 2, 2) == 0
    zero = F32(0.0)

    for k in range(3):
        first = [jnp.where(even_chip, r1[2 * k + t], r0[2 * k + t]) for t in range(2)]
        last = [jnp.where(even_chip, r0[2 * k + t], r1[2 * k + t]) for t in range(2)]
        at = TILES * k
        all3[at] = gate(iy >= 2, first[0])
        all3[at + 1] = jnp.where(iy >= 2, first[1], gate(iy == 1, first[0]))
        all3[at + 2] = own3[2 * k]
        all3[at + 3] = own3[2 * k + 1]
        all3[at + 4] = jnp.where(iy < count - 2, last[0], gate(iy == count - 2, last[1]))
        all3[at + 5] = gate(iy < count - 2, last[1])
    e = solve3(*[[all3[TILES * k + t] for t in range(TILES)] for k in range(3)])

    group = iota((8, 128), 1) // 32 == iota((8, 128), 0) // 2
    for t in range(2):
        for i in range(8):
            row = jnp.broadcast_to(e[2 + t][i : i + 1, :], (8, 128))
            m2[16 * i + 8 * t : 16 * i + 8 * t + 8, :] = jnp.where(group, row, zero)
    spread = jnp.where(
        iota((128, 128), 0) % 32 == (iota((128, 128), 1) % 64) // 2, F32(1.0), zero
    )
    fine = pick(m2[...], spread)
    for i in range(8):
        p2[i] = v2[i]
        p2[i, 4:20, :] += fine[16 * i : 16 * i + 16, :]
    v = [p2[i] for i in range(8)]
    g = [ge2[i] for i in range(8)]
    c = [ce2[i] for i in range(8)]
    wx = [wx2[i] for i in range(8)]
    wy = [wy2[i] for i in range(8)]
    wz = [wz2[i] for i in range(8)]
    for _ in range(2):
        r = residual2(v, g, c, wx, wy, wz)
        v = [v[i] + rd2[i] * r[i] for i in range(8)]
    for i in range(8):
        p2[i] = v[i]

    parts = []
    for q in range(3):
        at = ix + (q - 1)
        inside = jnp.logical_and(at >= 0, at < lax.axis_size("gx"))
        parts.append(jnp.where(inside, p2[jnp.clip(at, 0, 7), 4:20, :], zero))
    row = iota((128, 256), 0)
    lane = iota((128, 256), 1)
    hit = (row % 64 == (lane % 128) // 2) & (row // 64 == lane // 128)
    fine = pick(jnp.concatenate(parts, axis=0), jnp.where(hit, F32(1.0), zero))
    for q in range(3):
        for h in range(2):
            part = fine[16 * q : 16 * q + 16, 128 * h : 128 * h + 128]
            f1[2 * q + h, pl.ds(0, 16, stride=2), :] = part
            f1[2 * q + h, pl.ds(1, 16, stride=2), :] = part
    for x in range(12):
        p1a[x] = p1[x] + f1[x // 2]
    s1 = (wx1, wy1, wz1, wl1, rd1, ce1, ge1)
    sweep(p1a, p1b, s1, 1, 11, 10)
    sweep(p1b, p1a, s1, 2, 10, 8)

    wide = jnp.where(iota((128, 256), 0) == iota((128, 256), 1) // 2, F32(1.0), zero)
    fine = pick(jnp.concatenate([p1a[2 + x, 4:28, :] for x in range(8)], axis=0), wide)
    for x in range(8):
        for h in range(2):
            part = fine[24 * x : 24 * x + 24, 128 * h : 128 * h + 128]
            f0[x, h, pl.ds(0, 24, stride=2), :] = part
            f0[x, h, pl.ds(1, 24, stride=2), :] = part
    for x in range(1, 15):
        for h in range(2):
            cut = pl.ds(128 * h, 128)
            p0a[x, :, cut] = p0[x, :, cut] + f0[x // 2, h]
    s0 = (wx0, wy0, wz0, wl0, rd0, ce0, ge0)
    sweep(p0a, p0b, s0, 2, 14, 6)
    sweep(p0b, p0a, s0, 3, 13, 5)
    for x, here, res in residual_rows(p0a, s0, 4, 12):
        pressure[x - 4] = here[8:40, :]
        residual[x - 4] = res[8:40, :]


def call(kernel, name, outs, scratch, limit, *args, anywhere=()):
    vmem = pl.BlockSpec(memory_space=pltpu.VMEM)
    hbm = pl.BlockSpec(memory_space=pltpu.HBM)
    specs = [vmem for _ in args]
    for k in anywhere:
        specs[k] = hbm
    return pl.pallas_call(
        kernel,
        name=name,
        out_shape=[jax.ShapeDtypeStruct(s, F32) for s in outs],
        in_specs=specs,
        out_specs=[vmem for _ in outs],
        scratch_shapes=[pltpu.VMEM(s, F32) if isinstance(s, tuple) else s for s in scratch],
        compiler_params=pltpu.CompilerParams(vmem_limit_bytes=limit * MIB),
    )(*args)


B0 = (8, 32, 256)
E0 = (16, 48, 256)
E1 = (12, 32, 128)
E2 = (8, 24, 128)


def per_device(source, material, flags):
    source, material, flags = (
        pltpu.with_memory_space_constraint(a, pltpu.HBM) for a in (source, material, flags)
    )
    left, right, b0, c0, g0 = call(
        k_load0, "load0", [(24, 8, 128)] * 2 + [B0] * 3,
        [pltpu.VMEM(B0, jnp.int32), pltpu.VMEM(B0, jnp.int32), pltpu.SemaphoreType.DMA((3,))],
        4, material, flags, source, anywhere=(0, 1, 2),
    )
    left0, right0 = exchange(left, right, "gy")
    low, high = call(k_edge0, "edge0", [(10, 32, 256)] * 2, [], 4, b0, c0, g0)
    below0, above0 = exchange(low, high, "gx")
    low, high = call(k_corner0, "corner0", [(20, 8, 128)] * 2, [], 4, left0, right0)
    under0, over0 = exchange(low, high, "gx")
    b1, c1, bc2 = call(
        k_coefs, "coefs", [(4, 16, 128), (4, 16, 128), (2, 8, 128)],
        [(4, 2, 32, 128), (2, 16, 128)], 4, b0, c0,
    )
    blocks0 = (b0, c0, g0, below0, above0, left0, right0, under0, over0)
    v0, g1, low, high = call(
        k_descend0, "descend0",
        [B0, (4, 16, 128), (10, 16, 128), (10, 16, 128)],
        [E0] * 10 + [(4, 2, 32, 128)], 12,
        *blocks0, b1, c1,
    )
    below, above = exchange(low, high, "gx")
    low, high, vlow, vhigh = call(
        k_pack_y1, "pack_y1", [(24, 8, 128)] * 2 + [(3, 32, 256)] * 2, [], 4,
        g1, b1, c1, v0, below, above,
    )
    left, right = exchange(low, high, "gy")
    vbelow, vabove = exchange(vlow, vhigh, "gx")
    v1, pay, low, high, be1, ce1, ge1 = call(
        k_descend1, "descend1",
        [(4, 16, 128), (8, 3, 8, 128), (14, 8, 128), (14, 8, 128)] + [E1] * 3,
        [E1] * 7 + [(2, 16, 128)], 4,
        g1, b1, c1, bc2, below, above, left, right,
    )
    gathered = lax.all_to_all(pay, "gx", 0, 0)
    below1, above1 = exchange(low, high, "gx")
    low, high = call(
        k_pack_y2, "pack_y2", [(30, 8, 128)] * 2, [], 4, v1, below1, above1, gathered
    )
    left1, right1 = exchange(low, high, "gy")
    v2, own3, *s2 = call(
        k_descend2, "descend2", [E2, (6, 8, 128)] + [E2] * 6, [E2, (384, 128)], 4,
        gathered, left1, right1,
    )
    r0, r1 = swap_chips(own3, "gy", 0), swap_chips(own3, "gy", 1)
    p0, ce0, ge0, wx0, wy0, wz0, wl0, rd0, p1, *w1 = call(
        k_prepare, "prepare", [E0] * 8 + [E1] * 6, [E0, E0, E1], 8,
        *blocks0, be1, ce1, ge1, v0, vbelow, vabove, left, right,
        v1, below1, above1, left1, right1,
    )
    pressure, residual = call(
        k_ascend, "ascend", [B0] * 2,
        [(18, 8, 128), (128, 128), E2, E1, E1, E0, E0, (6, 32, 128), (8, 2, 48, 128)], 8,
        own3, r0, r1, v2, *s2,
        p0, ce0, ge0, wx0, wy0, wz0, wl0, rd0, p1, ce1, ge1, *w1,
    )
    return pressure, residual


def solution(mesh):
    spec = P("gx", "gy", None)
    return jax.shard_map(
        per_device,
        mesh=mesh,
        in_specs=(spec, spec, spec),
        out_specs=(spec, spec),
        check_vma=False,
    )
```

```python
import jax
import jax.numpy as jnp
from jax import lax
from jax.experimental import pallas as pl
from jax.experimental.pallas import tpu as pltpu
from jax.sharding import PartitionSpec as P

F32 = jnp.float32
BF16 = jnp.bfloat16
OMEGA = 0.8
SHIFT = 0.001
ROBIN = 2.0
INVERSE_SOLID = 1.0 / 3.0
INVERSE_DENSE = 0.125
MIB = 1 << 20


def shift(block, axis, step):
    count = lax.axis_size(axis)
    return lax.ppermute(block, axis, [(i, (i + step) % count) for i in range(count)])


def exchange(low, high, axis):
    return shift(high, axis, 1), shift(low, axis, -1)


def swap_chips(block, axis, parity):
    count = lax.axis_size(axis)
    pairs = [(i, i + 2) for i in range(count - 2) if (i // 2) % 2 == parity]
    if parity == 1:
        pairs = [(0, 1)] + pairs + [(count - 2, count - 1)]
    return lax.ppermute(block, axis, pairs + [(b, a) for a, b in pairs])


def iota(shape, dim):
    return lax.broadcasted_iota(jnp.int32, shape, dim)


def pick(a, w):
    count = a.shape[0]
    a1 = a.astype(BF16)
    rest = a - a1.astype(F32)
    a2 = rest.astype(BF16)
    a3 = (rest - a2.astype(F32)).astype(BF16)
    out = jnp.dot(
        jnp.concatenate([a1, a2, a3], axis=0), w.astype(BF16), preferred_element_type=F32
    )
    return out[:count] + out[count : 2 * count] + out[2 * count :]


def inverse_density(material):
    return jnp.where(
        material == 0, F32(1.0), jnp.where(material == 1, F32(INVERSE_SOLID), F32(INVERSE_DENSE))
    )


def reaction_of(flags):
    return F32(SHIFT) + F32(ROBIN) * flags.astype(F32)


def harmonic(a, b):
    return (2.0 * a * b) * (1.0 / jnp.maximum(a + b, F32(1e-30)))


def step_of(d):
    return jnp.where(d > 0, F32(OMEGA) / jnp.where(d > 0, d, F32(1.0)), F32(0.0))


def fold_level0(tmp):
    parts = []
    for h in range(2):
        parts.append(
            jnp.concatenate(
                [
                    tmp[x, h, pl.ds(0, 16, stride=2), :] + tmp[x, h, pl.ds(1, 16, stride=2), :]
                    for x in range(4)
                ],
                axis=0,
            )
        )
    w = jnp.where(iota((256, 128), 0) // 2 == iota((256, 128), 1), F32(0.125), F32(0.0))
    return pick(jnp.concatenate(parts, axis=1), w)


def fold_level1(tmp):
    parts = [
        tmp[x, pl.ds(0, 8, stride=2), :] + tmp[x, pl.ds(1, 8, stride=2), :] for x in range(2)
    ]
    row = iota((256, 128), 0)
    lane = iota((256, 128), 1)
    hit = ((row % 128) // 2 == lane % 64) & (row // 128 == lane // 64)
    return pick(jnp.concatenate(parts, axis=1), jnp.where(hit, F32(0.125), F32(0.0)))


def fold_level2(tiles):
    count = tiles.shape[0] // 64
    hit = (iota((128, 128), 0) % 64) // 2 == iota((128, 128), 1) % 32
    t = pick(tiles, jnp.where(hit, F32(0.125), F32(0.0))).reshape(count, 8, 8, 128)
    keep = iota(t.shape, 2) // 2 == iota(t.shape, 3) // 32
    t = jnp.sum(jnp.where(keep, t, F32(0.0)), axis=2)
    return [t[k] for k in range(count)]


def next_y(v):
    return pltpu.roll(v, v.shape[0] - 1, 0)


def last_y(v):
    return pltpu.roll(v, 1, 0)


def next_z(v):
    return pltpu.roll(v, v.shape[1] - 1, 1)


def last_z(v):
    return pltpu.roll(v, 1, 1)


def weights(b, s, v, scaling, low, high, unroll):
    wx, wy, wz, wl, rd, c, g = s
    scale = F32(scaling)
    prev = scale * harmonic(b[low - 1], b[low])
    wx[low - 1] = prev
    shape = prev.shape
    inside = iota(shape, 1) < shape[1] - 1

    def body(x, prev):
        here = b[x]
        cur = scale * harmonic(here, b[x + 1])
        wx[x] = cur
        fy = scale * harmonic(here, next_y(here))
        wy[x] = fy
        fz = jnp.where(inside, scale * harmonic(here, next_z(here)), F32(0.0))
        wz[x] = fz
        fl = last_z(fz)
        wl[x] = fl
        r = step_of((prev + cur) + (fy + last_y(fy)) + (fz + fl) + c[x])
        rd[x] = r
        v[x] = r * g[x]
        return cur

    lax.fori_loop(low, high, body, prev, unroll=unroll)


def row_residual(v, s, x, prev):
    wx, wy, wz, wl, rd, c, g = s
    here = v[x]
    cur = wx[x] * (here - v[x + 1])
    fy = wy[x] * (here - next_y(here))
    fz = wz[x] * (here - next_z(here)) + wl[x] * (here - last_z(here))
    flux = (cur - prev) + (fy - last_y(fy)) + fz
    return here, g[x] - (flux + c[x] * here), cur


def sweep(src, dst, s, low, high, unroll):
    rd = s[4]

    def body(x, prev):
        here, res, cur = row_residual(src, s, x, prev)
        dst[x] = here + rd[x] * res
        return cur

    first = s[0][low - 1] * (src[low - 1] - src[low])
    lax.fori_loop(low, high, body, first, unroll=unroll)


def residual_rows(v, s, low, high):
    prev = s[0][low - 1] * (v[low - 1] - v[low])
    for x in range(low, high):
        here, res, prev = row_residual(v, s, x, prev)
        yield x, here, res


def place(axis):
    return lax.axis_index(axis)


def gate(inside, value):
    return jnp.where(inside, value, F32(0.0))


def k_load0(m, f, g, left, right, b0, c0, g0, mv, fv, sems):
    copies = [
        pltpu.make_async_copy(m, mv, sems.at[0]),
        pltpu.make_async_copy(f, fv, sems.at[1]),
        pltpu.make_async_copy(g, g0, sems.at[2]),
    ]
    for copy in copies:
        copy.start()
    copies[0].wait()
    for x in range(8):
        b0[x] = inverse_density(mv[x])
        strip_tiles(left, x, gate(place("gy") > 0, b0[x, 0:4, :]))
        inside = place("gy") < lax.axis_size("gy") - 1
        strip_tiles(right, x, gate(inside, b0[x, 28:32, :]))
    copies[1].wait()
    for x in range(8):
        c0[x] = reaction_of(fv[x])
        strip_tiles(left, 8 + x, c0[x, 0:4, :])
        strip_tiles(right, 8 + x, c0[x, 28:32, :])
    copies[2].wait()
    for x in range(8):
        strip_tiles(left, 16 + x, g0[x, 0:4, :])
        strip_tiles(right, 16 + x, g0[x, 28:32, :])


def k_edge0(b0, c0, g0, low, high):
    for k in range(3):
        low[k] = gate(place("gx") > 0, b0[k])
        high[k] = gate(place("gx") < lax.axis_size("gx") - 1, b0[5 + k])
        low[3 + k] = c0[k] + harmonic(b0[2], b0[3]) if k == 2 else c0[k]
        high[3 + k] = c0[5 + k] + harmonic(b0[5], b0[4]) if k == 0 else c0[5 + k]
        low[6 + k] = g0[k]
        high[6 + k] = g0[5 + k]


def split_pair(tmp, k, value):
    for h in range(2):
        tmp[k, h] = value[:, 128 * h : 128 * h + 128]


def k_coefs(b0, c0, b1, c1, bc2, tmp0, tmp1):
    for k, (src, out) in enumerate(((b0, b1), (c0, c1))):
        for x in range(4):
            split_pair(tmp0, x, src[2 * x] + src[2 * x + 1])
        t = fold_level0(tmp0)
        for x in range(4):
            out[x] = t[16 * x : 16 * x + 16]
        for x in range(2):
            tmp1[x] = t[32 * x : 32 * x + 16] + t[32 * x + 16 : 32 * x + 32]
        bc2[k] = fold_level1(tmp1)


def strip_tiles(out, t, value):
    out[t, 0:4, :] = value[:, 0:128]
    out[t, 4:8, :] = value[:, 128:256]


CORNER = 7


def k_corner0(left, right, low, high):
    for side, strips in enumerate((left, right)):
        at = CORNER * side
        for k in range(3):
            low[at + k] = gate(place("gx") > 0, strips[k])
            high[at + k] = gate(place("gx") < lax.axis_size("gx") - 1, strips[5 + k])
        for k in range(2):
            low[at + 3 + k] = strips[8 + k]
            high[at + 3 + k] = strips[14 + k]
            low[at + 5 + k] = strips[16 + k]
            high[at + 5 + k] = strips[22 + k]


def put_strip0(ext, row, tile, high):
    at = 36 if high else 0
    ext[row, at : at + 4, 0:128] = tile[0:4, :]
    ext[row, at : at + 4, 128:256] = tile[4:8, :]


def assemble0(b0, c0, g0, below, above, left, right, under, over, be, ce, ge):
    zero = jnp.zeros((8, 128), F32)
    for which, (ext, own, corner, reach) in enumerate(
        ((be, b0, 0, 3), (ce, c0, 3, 2), (ge, g0, 5, 2))
    ):
        for x in range(-3, 11):
            if x < 0:
                val = below[3 * which + x + 3]
                k = corner + x + reach
                near = x >= -reach
                strips = (under[k], under[CORNER + k]) if near else (zero, zero)
            elif x < 8:
                val = own[x]
                strips = left[8 * which + x], right[8 * which + x]
            else:
                val = above[3 * which + x - 8]
                k = corner + x - 8
                near = x - 8 < reach
                strips = (over[k], over[CORNER + k]) if near else (zero, zero)
            ext[4 + x, 4:36, :] = val
            put_strip0(ext, 4 + x, strips[0], False)
            put_strip0(ext, 4 + x, strips[1], True)
    for x in (0, 15):
        be[x] = jnp.zeros(be.shape[1:], F32)


def k_descend0(
    b0, c0, g0, below, above, left, right, under, over, b1, c1,
    v0, g1, low, high,
    be, ce, ge, wx, wy, wz, wl, rd, va, vb, tmp,
):
    assemble0(b0, c0, g0, below, above, left, right, under, over, be, ce, ge)
    s = (wx, wy, wz, wl, rd, ce, ge)
    weights(be, s, va, 1.0, 1, 15, 7)
    sweep(va, vb, s, 2, 14, 6)
    sweep(vb, va, s, 3, 13, 5)
    for x in range(8):
        v0[x] = va[4 + x, 4:36, :]
    kept = None
    for x, here, res in residual_rows(va, s, 4, 12):
        if x % 2 == 0:
            kept = res
        else:
            split_pair(tmp, (x - 4) // 2, (kept + res)[4:36, :])
    t = fold_level0(tmp)
    for x in range(4):
        g1[x] = t[16 * x : 16 * x + 16]
        low[x] = gate(place("gx") > 0, b1[x])
        high[x] = gate(place("gx") < lax.axis_size("gx") - 1, b1[x])
    for k in range(3):
        low[4 + k] = c1[k]
        high[4 + k] = c1[1 + k]
        low[7 + k] = t[16 * k : 16 * k + 16]
        high[7 + k] = t[16 * k + 16 : 16 * k + 32]


def k_pack_y1(g1, b1, c1, v0, below, above, low, high):
    for out, at, inside in ((low, 0, place("gy") > 0), (high, 12, place("gy") < lax.axis_size("gy") - 1)):
        cut = pl.ds(at, 4)
        t = 0
        for own, base, reach in ((b1, 0, 4), (c1, 4, 3), (g1, 7, 3)):
            for x in range(-reach, 4 + reach):
                if x < 0:
                    val = below[base + x + reach, cut, :]
                elif x < 4:
                    val = own[x, cut, :]
                else:
                    val = above[base + x - 4, cut, :]
                half = 4 * (t % 2)
                out[t // 2, half : half + 4, :] = gate(inside, val) if base == 0 else val
                t += 1
        for x in range(8):
            strip_tiles(out, 16 + x, v0[x, pl.ds(0 if at == 0 else 28, 4), :])


def k_descend1(
    g1, b1, c1, bc2, below, above, left, right,
    v1, pay, be, ce, ge,
    wx, wy, wz, wl, rd, va, vb, tmp,
):
    zeros = jnp.zeros((8, 128), F32)
    t = 0
    for ext, own, base, reach in ((be, b1, 0, 4), (ce, c1, 4, 3), (ge, g1, 7, 3)):
        for x in range(12):
            ext[x, 0:8, :] = zeros
            ext[x, 24:32, :] = zeros
        for x in range(-reach, 4 + reach):
            if x < 0:
                val = below[base + x + reach]
            elif x < 4:
                val = own[x]
            else:
                val = above[base + x - 4]
            ext[4 + x, 8:24, :] = val
            half = 4 * (t % 2)
            ext[4 + x, 4:8, :] = left[t // 2, half : half + 4, :]
            ext[4 + x, 24:28, :] = right[t // 2, half : half + 4, :]
            t += 1

    s = (wx, wy, wz, wl, rd, ce, ge)
    weights(be, s, va, 0.25, 1, 11, 10)
    sweep(va, vb, s, 2, 10, 8)
    sweep(vb, va, s, 3, 9, 6)
    for x in range(4):
        v1[x] = va[4 + x, 8:24, :]
    kept = None
    for x, here, res in residual_rows(va, s, 4, 8):
        if x % 2 == 0:
            kept = res[8:24, :]
        else:
            tmp[(x - 4) // 2] = kept + res[8:24, :]
    g2 = fold_level1(tmp)
    for k in range(8):
        pay[k, 0] = g2
        pay[k, 1] = bc2[0]
        pay[k, 2] = bc2[1]


def k_pack_v(v0, v1, left, right, low, high):
    for out, first, edge in ((low, 0, 0), (high, 5, 6)):
        for k in range(3):
            for q in range(4):
                for h in range(2):
                    out[8 * k + 2 * q + h] = v0[
                        first + k, 8 * q : 8 * q + 8, 128 * h : 128 * h + 128
                    ]
        for k in range(2):
            out[24 + k] = left[16 + edge + k]
            out[26 + k] = right[16 + edge + k]
        for k in range(4):
            for q in range(2):
                out[28 + 2 * k + q] = v1[k, 8 * q : 8 * q + 8, :]


def k_pack_y2(v1, below, above, gathered, low, high):
    for out, q, inside in (
        (low, 0, place("gy") > 0), (high, 1, place("gy") < lax.axis_size("gy") - 1)
    ):
        for k in range(3):
            for i in range(8):
                val = gathered[i, k]
                out[8 * k + i] = gate(inside, val) if k == 1 else val
        cut = pl.ds(4 * q, 4)
        for t, x in enumerate(range(-4, 8)):
            if x < 0:
                val = below[28 + 2 * (x + 4) + q, cut, :]
            elif x < 4:
                val = v1[x, pl.ds(12 * q, 4), :]
            else:
                val = above[28 + 2 * (x - 4) + q, cut, :]
            half = 4 * (t % 2)
            out[24 + t // 2, half : half + 4, :] = val


def upper(shape):
    return iota(shape, len(shape) - 1) >= 64


def pair_next(v):
    mask = upper(v[0].shape)
    out = []
    for i in range(8):
        after = v[i + 1] if i < 7 else jnp.zeros_like(v[0])
        out.append(pltpu.roll(jnp.where(mask, v[i], after), 64, 1))
    return out


def pair_last(f):
    mask = upper(f[0].shape)
    out = []
    for i in range(8):
        before = f[i - 1] if i > 0 else jnp.zeros_like(f[0])
        out.append(pltpu.roll(jnp.where(mask, before, f[i]), 64, 1))
    return out


def weights2(b, c, scaling):
    scale = F32(scaling)
    inside = iota(b[0].shape, 1) % 64 < 63
    wx = [scale * harmonic(p, q) for p, q in zip(b, pair_next(b))]
    wy = [scale * harmonic(p, next_y(p)) for p in b]
    wz = [jnp.where(inside, scale * harmonic(p, next_z(p)), F32(0.0)) for p in b]
    back = pair_last(wx)
    rd = []
    for i in range(8):
        d = (wx[i] + back[i]) + (wy[i] + last_y(wy[i])) + (wz[i] + last_z(wz[i])) + c[i]
        rd.append(step_of(d))
    return wx, wy, wz, rd


def residual2(v, g, c, wx, wy, wz):
    fx = [w * (p - q) for w, p, q in zip(wx, v, pair_next(v))]
    back = pair_last(fx)
    out = []
    for i in range(8):
        fy = wy[i] * (v[i] - next_y(v[i]))
        fz = wz[i] * (v[i] - next_z(v[i]))
        flux = (fx[i] - back[i]) + (fy - last_y(fy)) + (fz - last_z(fz))
        out.append(g[i] - (flux + c[i] * v[i]))
    return out


def k_descend2(gathered, left, right, v2, pay, wx2, wy2, wz2, rd2, ce2, ge2, be2, tmp):
    for k, ext in enumerate((ge2, be2, ce2)):
        for i in range(8):
            ext[i, 0:8, :] = left[8 * k + i]
            ext[i, 8:16, :] = gathered[i, k]
            ext[i, 16:24, :] = right[8 * k + i]
    b = [be2[i] for i in range(8)]
    c = [ce2[i] for i in range(8)]
    g = [ge2[i] for i in range(8)]
    wx, wy, wz, rd = weights2(b, c, 0.0625)
    for i in range(8):
        wx2[i] = wx[i]
        wy2[i] = wy[i]
        wz2[i] = wz[i]
        rd2[i] = rd[i]
    v = [p * q for p, q in zip(rd, g)]
    for _ in range(2):
        r = residual2(v, g, c, wx, wy, wz)
        v = [p + q * s for p, q, s in zip(v, rd, r)]
    r = residual2(v, g, c, wx, wy, wz)
    for i in range(8):
        v2[i] = v[i]
    for k, src in enumerate((r, b, c)):
        for t in range(2):
            for i in range(8):
                at = 64 * (2 * k + t) + 8 * i
                tmp[at : at + 8, :] = src[i][4 + 8 * t : 12 + 8 * t, :]
    for t, tile in enumerate(fold_level2(tmp[...])):
        pay[t] = tile


TILES = 6


def block_next(v):
    head = iota(v[0].shape, 1) < 32
    out = []
    for t in range(TILES):
        after = v[t + 1] if t < TILES - 1 else jnp.zeros_like(v[0])
        out.append(pltpu.roll(jnp.where(head, after, v[t]), 96, 1))
    return out


def block_last(f):
    tail = iota(f[0].shape, 1) >= 96
    out = []
    for t in range(TILES):
        before = f[t - 1] if t > 0 else jnp.zeros_like(f[0])
        out.append(pltpu.roll(jnp.where(tail, before, f[t]), 32, 1))
    return out


def solve3(g, b, c):
    scale = F32(0.015625)
    shape = g[0].shape
    inside_x = iota(shape, 0) < 7
    inside_z = iota(shape, 1) % 32 < 31
    zero = F32(0.0)
    wx = [jnp.where(inside_x, scale * harmonic(p, next_y(p)), zero) for p in b]
    wy = [scale * harmonic(p, q) for p, q in zip(b, block_next(b))]
    wz = [jnp.where(inside_z, scale * harmonic(p, next_z(p)), zero) for p in b]
    xl = [last_y(p) for p in wx]
    yl = block_last(wy)
    zl = [last_z(p) for p in wz]
    rd = []
    for t in range(TILES):
        d = (wx[t] + xl[t]) + (wy[t] + yl[t]) + (wz[t] + zl[t]) + c[t]
        rd.append(step_of(d))
    e = [p * q for p, q in zip(rd, g)]
    for _ in range(7):
        up = block_next(e)
        down = block_last(e)
        new = []
        for t in range(TILES):
            h = e[t]
            flux = wx[t] * (h - next_y(h)) + xl[t] * (h - last_y(h))
            flux = flux + (wy[t] * (h - up[t]) + yl[t] * (h - down[t]))
            flux = flux + (wz[t] * (h - next_z(h)) + zl[t] * (h - last_z(h)))
            new.append(h + rd[t] * (g[t] - (flux + c[t] * h)))
        e = new
    return e


def k_prepare(
    b0, c0, g0, below0, above0, left0, right0, under0, over0, be1, ce1, ge1,
    v0, v1, left, right, below, above, left1, right1,
    p0, ce, ge, wx, wy, wz, wl, rd, p1, wx1, wy1, wz1, wl1, rd1,
    be, va, va1,
):
    assemble0(b0, c0, g0, below0, above0, left0, right0, under0, over0, be, ce, ge)
    weights(be, (wx, wy, wz, wl, rd, ce, ge), va, 1.0, 2, 14, 6)
    weights(be1, (wx1, wy1, wz1, wl1, rd1, ce1, ge1), va1, 0.25, 1, 11, 10)
    zero = jnp.zeros((8, 128), F32)
    for t, x in enumerate(range(-4, 8)):
        p1[t, 0:8, :] = zero
        p1[t, 24:32, :] = zero
        if 0 <= x < 4:
            p1[t, 8:24, :] = v1[x]
        else:
            src, k = (below, x + 4) if x < 0 else (above, x - 4)
            for q in range(2):
                p1[t, 8 + 8 * q : 16 + 8 * q, :] = src[28 + 2 * k + q]
        half = 4 * (t % 2)
        p1[t, 4:8, :] = left1[24 + t // 2, half : half + 4, :]
        p1[t, 24:28, :] = right1[24 + t // 2, half : half + 4, :]
    for x in range(-3, 11):
        if 0 <= x < 8:
            p0[4 + x, 4:36, :] = v0[x]
            strips = left[16 + x], right[16 + x]
        else:
            src, k = (below, x + 3) if x < 0 else (above, x - 8)
            for q in range(4):
                for h in range(2):
                    p0[4 + x, 4 + 8 * q : 12 + 8 * q, 128 * h : 128 * h + 128] = (
                        src[8 * k + 2 * q + h]
                    )
            e = x + 2 if x < 0 else x - 8
            strips = (src[24 + e], src[26 + e]) if 0 <= e < 2 else (zero, zero)
        put_strip0(p0, 4 + x, strips[0], False)
        put_strip0(p0, 4 + x, strips[1], True)


def k_ascend(
    own3, r0, r1, v2, wx2, wy2, wz2, rd2, ce2, ge2,
    p0, ce0, ge0, wx0, wy0, wz0, wl0, rd0,
    p1, ce1, ge1, wx1, wy1, wz1, wl1, rd1,
    pressure, residual,
    all3, m2, p2, p1a, p1b, p0a, p0b, f1, f0, own, res0, sems,
):
    ix = place("gx")
    iy = place("gy")
    count = lax.axis_size("gy")
    even_chip = lax.rem(iy // 2, 2) == 0
    zero = F32(0.0)

    for k in range(3):
        first = [jnp.where(even_chip, r1[2 * k + t], r0[2 * k + t]) for t in range(2)]
        last = [jnp.where(even_chip, r0[2 * k + t], r1[2 * k + t]) for t in range(2)]
        at = TILES * k
        all3[at] = gate(iy >= 2, first[0])
        all3[at + 1] = jnp.where(iy >= 2, first[1], gate(iy == 1, first[0]))
        all3[at + 2] = own3[2 * k]
        all3[at + 3] = own3[2 * k + 1]
        all3[at + 4] = jnp.where(iy < count - 2, last[0], gate(iy == count - 2, last[1]))
        all3[at + 5] = gate(iy < count - 2, last[1])
    e = solve3(*[[all3[TILES * k + t] for t in range(TILES)] for k in range(3)])

    group = iota((8, 128), 1) // 32 == iota((8, 128), 0) // 2
    for t in range(2):
        for i in range(8):
            row = jnp.broadcast_to(e[2 + t][i : i + 1, :], (8, 128))
            m2[16 * i + 8 * t : 16 * i + 8 * t + 8, :] = jnp.where(group, row, zero)
    spread = jnp.where(
        iota((128, 128), 0) % 32 == (iota((128, 128), 1) % 64) // 2, F32(1.0), zero
    )
    fine = pick(m2[...], spread)
    for i in range(8):
        p2[i] = v2[i]
        p2[i, 4:20, :] += fine[16 * i : 16 * i + 16, :]
    v = [p2[i] for i in range(8)]
    g = [ge2[i] for i in range(8)]
    c = [ce2[i] for i in range(8)]
    wx = [wx2[i] for i in range(8)]
    wy = [wy2[i] for i in range(8)]
    wz = [wz2[i] for i in range(8)]
    for _ in range(2):
        r = residual2(v, g, c, wx, wy, wz)
        v = [v[i] + rd2[i] * r[i] for i in range(8)]
    for i in range(8):
        p2[i] = v[i]

    parts = []
    for q in range(3):
        at = ix + (q - 1)
        inside = jnp.logical_and(at >= 0, at < lax.axis_size("gx"))
        parts.append(jnp.where(inside, p2[jnp.clip(at, 0, 7), 4:20, :], zero))
    row = iota((128, 256), 0)
    lane = iota((128, 256), 1)
    hit = (row % 64 == (lane % 128) // 2) & (row // 64 == lane // 128)
    fine = pick(jnp.concatenate(parts, axis=0), jnp.where(hit, F32(1.0), zero))
    for q in range(3):
        for h in range(2):
            part = fine[16 * q : 16 * q + 16, 128 * h : 128 * h + 128]
            f1[2 * q + h, pl.ds(0, 16, stride=2), :] = part
            f1[2 * q + h, pl.ds(1, 16, stride=2), :] = part
    for x in range(12):
        p1a[x] = p1[x] + f1[x // 2]
    s1 = (wx1, wy1, wz1, wl1, rd1, ce1, ge1)
    sweep(p1a, p1b, s1, 1, 11, 10)
    sweep(p1b, p1a, s1, 2, 10, 8)

    wide = jnp.where(iota((128, 256), 0) == iota((128, 256), 1) // 2, F32(1.0), zero)
    fine = pick(jnp.concatenate([p1a[2 + x, 6:26, :] for x in range(8)], axis=0), wide)
    for x in range(8):
        for h in range(2):
            part = fine[20 * x : 20 * x + 20, 128 * h : 128 * h + 128]
            f0[x, h, pl.ds(0, 20, stride=2), :] = part
            f0[x, h, pl.ds(1, 20, stride=2), :] = part
    for x in range(1, 15):
        for h in range(2):
            cut = pl.ds(128 * h, 128)
            p0a[x, :, cut] = p0[x, :, cut] + f0[x // 2, h]
    s0 = (wx0, wy0, wz0, wl0, rd0, ce0, ge0)
    sweep(p0a, p0b, s0, 2, 14, 6)
    sweep(p0b, p0a, s0, 3, 13, 5)
    for x in range(8):
        own[x] = p0a[4 + x, 4:36, :]
    copies = [pltpu.make_async_copy(own, pressure, sems.at[0])]
    copies[0].start()
    for x, here, res in residual_rows(p0a, s0, 4, 12):
        res0[x - 4] = res[4:36, :]
        if x % 4 == 3:
            cut = pl.ds(x - 7, 4)
            copies.append(pltpu.make_async_copy(res0.at[cut], residual.at[cut], sems.at[x // 4]))
            copies[-1].start()
    for copy in copies:
        copy.wait()


def call(kernel, name, outs, scratch, limit, *args, anywhere=(), to_hbm=False):
    vmem = pl.BlockSpec(memory_space=pltpu.VMEM)
    hbm = pl.BlockSpec(memory_space=pltpu.HBM)
    specs = [vmem for _ in args]
    for k in anywhere:
        specs[k] = hbm
    return pl.pallas_call(
        kernel,
        name=name,
        out_shape=[jax.ShapeDtypeStruct(s, F32) for s in outs],
        in_specs=specs,
        out_specs=[hbm if to_hbm else vmem for _ in outs],
        scratch_shapes=[pltpu.VMEM(s, F32) if isinstance(s, tuple) else s for s in scratch],
        compiler_params=pltpu.CompilerParams(vmem_limit_bytes=limit * MIB),
    )(*args)


B0 = (8, 32, 256)
E0 = (16, 40, 256)
E1 = (12, 32, 128)
E2 = (8, 24, 128)


def per_device(source, material, flags):
    source, material, flags = (
        pltpu.with_memory_space_constraint(a, pltpu.HBM) for a in (source, material, flags)
    )
    left, right, b0, c0, g0 = call(
        k_load0, "load0", [(24, 8, 128)] * 2 + [B0] * 3,
        [pltpu.VMEM(B0, jnp.int32), pltpu.VMEM(B0, jnp.int32), pltpu.SemaphoreType.DMA((3,))],
        4, material, flags, source, anywhere=(0, 1, 2),
    )
    left0, right0 = exchange(left, right, "gy")
    low, high = call(k_edge0, "edge0", [(9, 32, 256)] * 2, [], 4, b0, c0, g0)
    below0, above0 = exchange(low, high, "gx")
    low, high = call(k_corner0, "corner0", [(14, 8, 128)] * 2, [], 4, left0, right0)
    under0, over0 = exchange(low, high, "gx")
    b1, c1, bc2 = call(
        k_coefs, "coefs", [(4, 16, 128), (4, 16, 128), (2, 8, 128)],
        [(4, 2, 32, 128), (2, 16, 128)], 4, b0, c0,
    )
    blocks0 = (b0, c0, g0, below0, above0, left0, right0, under0, over0)
    v0, g1, low, high = call(
        k_descend0, "descend0",
        [B0, (4, 16, 128), (10, 16, 128), (10, 16, 128)],
        [E0] * 10 + [(4, 2, 32, 128)], 12,
        *blocks0, b1, c1,
    )
    below, above = exchange(low, high, "gx")
    low, high = call(
        k_pack_y1, "pack_y1", [(24, 8, 128)] * 2, [], 4, g1, b1, c1, v0, below, above
    )
    left, right = exchange(low, high, "gy")
    v1, pay, be1, ce1, ge1 = call(
        k_descend1, "descend1",
        [(4, 16, 128), (8, 3, 8, 128)] + [E1] * 3,
        [E1] * 7 + [(2, 16, 128)], 4,
        g1, b1, c1, bc2, below, above, left, right,
    )
    gathered = lax.all_to_all(pay, "gx", 0, 0)
    low, high = call(k_pack_v, "pack_v", [(36, 8, 128)] * 2, [], 4, v0, v1, left, right)
    below, above = exchange(low, high, "gx")
    low, high = call(
        k_pack_y2, "pack_y2", [(30, 8, 128)] * 2, [], 4, v1, below, above, gathered
    )
    left1, right1 = exchange(low, high, "gy")
    v2, own3, *s2 = call(
        k_descend2, "descend2", [E2, (6, 8, 128)] + [E2] * 6, [E2, (384, 128)], 4,
        gathered, left1, right1,
    )
    r0, r1 = swap_chips(own3, "gy", 0), swap_chips(own3, "gy", 1)
    p0, ce0, ge0, wx0, wy0, wz0, wl0, rd0, p1, *w1 = call(
        k_prepare, "prepare", [E0] * 8 + [E1] * 6, [E0, E0, E1], 8,
        *blocks0, be1, ce1, ge1, v0, v1, left, right, below, above, left1, right1,
    )
    pressure, residual = call(
        k_ascend, "ascend", [B0] * 2,
        [(18, 8, 128), (128, 128), E2, E1, E1, E0, E0, (6, 32, 128), (8, 2, 40, 128),
         B0, B0, pltpu.SemaphoreType.DMA((3,))],
        8, own3, r0, r1, v2, *s2,
        p0, ce0, ge0, wx0, wy0, wz0, wl0, rd0, p1, ce1, ge1, *w1, to_hbm=True,
    )
    return pressure, residual


def solution(mesh):
    spec = P("gx", "gy", None)
    return jax.shard_map(
        per_device,
        mesh=mesh,
        in_specs=(spec, spec, spec),
        out_specs=(spec, spec),
        check_vma=False,
    )
```

```python
import jax
import jax.numpy as jnp
from jax import lax
from jax.experimental import pallas as pl
from jax.experimental.pallas import tpu as pltpu
from jax.sharding import PartitionSpec as P

F32 = jnp.float32
BF16 = jnp.bfloat16
OMEGA = 0.8
SHIFT = 0.001
ROBIN = 2.0
INVERSE_SOLID = 1.0 / 3.0
INVERSE_DENSE = 0.125
MIB = 1 << 20


def shift(block, axis, step):
    count = lax.axis_size(axis)
    return lax.ppermute(block, axis, [(i, (i + step) % count) for i in range(count)])


def exchange(low, high, axis):
    return shift(high, axis, 1), shift(low, axis, -1)


def swap_chips(block, axis, parity):
    count = lax.axis_size(axis)
    pairs = [(i, i + 2) for i in range(count - 2) if (i // 2) % 2 == parity]
    if parity == 1:
        pairs = [(0, 1)] + pairs + [(count - 2, count - 1)]
    return lax.ppermute(block, axis, pairs + [(b, a) for a, b in pairs])


def iota(shape, dim):
    return lax.broadcasted_iota(jnp.int32, shape, dim)


def pick(a, w):
    count = a.shape[0]
    a1 = a.astype(BF16)
    rest = a - a1.astype(F32)
    a2 = rest.astype(BF16)
    a3 = (rest - a2.astype(F32)).astype(BF16)
    out = jnp.dot(
        jnp.concatenate([a1, a2, a3], axis=0), w.astype(BF16), preferred_element_type=F32
    )
    return out[:count] + out[count : 2 * count] + out[2 * count :]


def inverse_density(material):
    return jnp.where(
        material == 0, F32(1.0), jnp.where(material == 1, F32(INVERSE_SOLID), F32(INVERSE_DENSE))
    )


def reaction_of(flags):
    return F32(SHIFT) + F32(ROBIN) * flags.astype(F32)


def harmonic(a, b):
    return (2.0 * a * b) * (1.0 / jnp.maximum(a + b, F32(1e-30)))


def step_of(d):
    return jnp.where(d > 0, F32(OMEGA) / jnp.where(d > 0, d, F32(1.0)), F32(0.0))


def fold_level0(tmp):
    parts = []
    for h in range(2):
        parts.append(
            jnp.concatenate(
                [
                    tmp[x, h, pl.ds(0, 24, stride=2), :] + tmp[x, h, pl.ds(1, 24, stride=2), :]
                    for x in range(4)
                ],
                axis=0,
            )
        )
    w = jnp.where(iota((256, 128), 0) // 2 == iota((256, 128), 1), F32(0.125), F32(0.0))
    return pick(jnp.concatenate(parts, axis=1), w).reshape(4, 24, 128)


def fold_level1(tmp):
    parts = [
        tmp[x, pl.ds(0, 8, stride=2), :] + tmp[x, pl.ds(1, 8, stride=2), :] for x in range(2)
    ]
    row = iota((256, 128), 0)
    lane = iota((256, 128), 1)
    hit = ((row % 128) // 2 == lane % 64) & (row // 128 == lane // 64)
    return pick(jnp.concatenate(parts, axis=1), jnp.where(hit, F32(0.125), F32(0.0)))


def fold_level2(tiles):
    count = tiles.shape[0] // 64
    hit = (iota((128, 128), 0) % 64) // 2 == iota((128, 128), 1) % 32
    t = pick(tiles, jnp.where(hit, F32(0.125), F32(0.0))).reshape(count, 8, 8, 128)
    keep = iota(t.shape, 2) // 2 == iota(t.shape, 3) // 32
    t = jnp.sum(jnp.where(keep, t, F32(0.0)), axis=2)
    return [t[k] for k in range(count)]


def next_y(v):
    return pltpu.roll(v, v.shape[0] - 1, 0)


def last_y(v):
    return pltpu.roll(v, 1, 0)


def next_z(v):
    return pltpu.roll(v, v.shape[1] - 1, 1)


def last_z(v):
    return pltpu.roll(v, 1, 1)


def weights(b, s, v, scaling, low, high, unroll):
    wx, wy, wz, wl, rd, c, g = s
    scale = F32(scaling)
    prev = scale * harmonic(b[low - 1], b[low])
    wx[low - 1] = prev
    shape = prev.shape
    inside = iota(shape, 1) < shape[1] - 1

    def body(x, prev):
        here = b[x]
        cur = scale * harmonic(here, b[x + 1])
        wx[x] = cur
        fy = scale * harmonic(here, next_y(here))
        wy[x] = fy
        fz = jnp.where(inside, scale * harmonic(here, next_z(here)), F32(0.0))
        wz[x] = fz
        fl = last_z(fz)
        wl[x] = fl
        r = step_of((prev + cur) + (fy + last_y(fy)) + (fz + fl) + c[x])
        rd[x] = r
        v[x] = r * g[x]
        return cur

    lax.fori_loop(low, high, body, prev, unroll=unroll)


def row_residual(v, s, x, prev):
    wx, wy, wz, wl, rd, c, g = s
    here = v[x]
    cur = wx[x] * (here - v[x + 1])
    fy = wy[x] * (here - next_y(here))
    fz = wz[x] * (here - next_z(here)) + wl[x] * (here - last_z(here))
    flux = (cur - prev) + (fy - last_y(fy)) + fz
    return here, g[x] - (flux + c[x] * here), cur


def sweep(src, dst, s, low, high, unroll):
    rd = s[4]

    def body(x, prev):
        here, res, cur = row_residual(src, s, x, prev)
        dst[x] = here + rd[x] * res
        return cur

    first = s[0][low - 1] * (src[low - 1] - src[low])
    lax.fori_loop(low, high, body, first, unroll=unroll)


def residual_rows(v, s, low, high):
    prev = s[0][low - 1] * (v[low - 1] - v[low])
    for x in range(low, high):
        here, res, prev = row_residual(v, s, x, prev)
        yield x, here, res


def place(axis):
    return lax.axis_index(axis)


def gate(inside, value):
    return jnp.where(inside, value, F32(0.0))


STRIPS = 54


def k_load0(m, f, g, left, right, b0, c0, g0, mv, fv, sems):
    copies = [
        pltpu.make_async_copy(m, mv, sems.at[0]),
        pltpu.make_async_copy(f, fv, sems.at[1]),
        pltpu.make_async_copy(g, g0, sems.at[2]),
    ]
    for copy in copies:
        copy.start()

    def strips(a, own):
        for x in range(8):
            for out, at, ninth, tenth, inside in (
                (left, 0, 8, 9, place("gy") > 0),
                (right, 24, 23, 22, place("gy") < lax.axis_size("gy") - 1),
            ):
                near = own[x, at : at + 8, :]
                far = own[x, ninth : ninth + 1, :]
                if a == 0:
                    near, far = gate(inside, near), gate(inside, far)
                if a == 1:
                    far = far + harmonic(b0[x, ninth : ninth + 1, :], b0[x, tenth : tenth + 1, :])
                for h in range(2):
                    cut = slice(128 * h, 128 * h + 128)
                    out[16 * a + 2 * x + h] = near[:, cut]
                    out[48 + 2 * a + h, x : x + 1, :] = far[:, cut]

    copies[0].wait()
    for x in range(8):
        b0[x] = inverse_density(mv[x])
    strips(0, b0)
    copies[1].wait()
    for x in range(8):
        c0[x] = reaction_of(fv[x])
    strips(1, c0)
    copies[2].wait()
    strips(2, g0)


def k_edge0(b0, c0, g0, low, high):
    for k in range(3):
        low[k] = gate(place("gx") > 0, b0[k])
        high[k] = gate(place("gx") < lax.axis_size("gx") - 1, b0[5 + k])
        low[3 + k] = c0[k] + harmonic(b0[2], b0[3]) if k == 2 else c0[k]
        high[3 + k] = c0[5 + k] + harmonic(b0[5], b0[4]) if k == 0 else c0[5 + k]
        low[6 + k] = g0[k]
        high[6 + k] = g0[5 + k]


def split_pair(tmp, k, value):
    for h in range(2):
        tmp[k, h] = value[:, 128 * h : 128 * h + 128]


def k_coefs(b0, c0, left, right, b1, c1, bc2, tmp0, tmp1):
    for k, (src, out) in enumerate(((b0, b1), (c0, c1))):
        for x in range(4):
            pair = src[2 * x] + src[2 * x + 1]
            for h in range(2):
                t = 16 * k + 4 * x + h
                tmp0[x, h, 0:8, :] = left[t] + left[t + 2]
                tmp0[x, h, 8:40, :] = pair[:, 128 * h : 128 * h + 128]
                tmp0[x, h, 40:48, :] = right[t] + right[t + 2]
        t = fold_level0(tmp0)
        for x in range(4):
            out[x] = t[x]
        for x in range(2):
            tmp1[x] = (t[2 * x] + t[2 * x + 1])[4:20, :]
        bc2[k] = fold_level1(tmp1)


CORNERS = 37


def k_corner0(left, right, low, high):
    for out, first, edge, third, fourth, inside in (
        (low, 0, 0, 2, 3, place("gx") > 0),
        (high, 5, 7, 5, 4, place("gx") < lax.axis_size("gx") - 1),
    ):
        out[36] = jnp.zeros((8, 128), F32)
        for side, strips in enumerate((left, right)):
            for h in range(2):
                for k in range(3):
                    x = first + k
                    at = 18 * side + 2 * k + h
                    out[at] = gate(inside, strips[2 * x + h])
                    c = strips[16 + 2 * x + h]
                    if x == third:
                        c = c + harmonic(strips[2 * x + h], strips[2 * fourth + h])
                    out[at + 6] = c
                    out[at + 12] = strips[32 + 2 * x + h]
                at = 2 * side + h
                out[36, at : at + 1, :] = gate(inside, strips[48 + h, edge : edge + 1, :])


def blocks0(b0, c0, g0, below, above, left, right, under, over):
    for a, own in enumerate((b0, c0, g0)):
        for x in range(-3, 11):
            if 0 <= x < 8:
                tiles = [[s[16 * a + 2 * x + h] for h in range(2)] for s in (left, right)]
                ninth = [[s[48 + 2 * a + h, x : x + 1, :] for h in range(2)] for s in (left, right)]
                yield a, x, own[x], tiles, ninth
            else:
                k = x + 3 if x < 0 else x - 8
                main, far = (below, under) if x < 0 else (above, over)
                tiles = [[far[18 * side + 6 * a + 2 * k + h] for h in range(2)] for side in range(2)]
                ninth = None
                if a == 0 and x in (-1, 8):
                    ninth = [
                        [far[36, 2 * side + h : 2 * side + h + 1, :] for h in range(2)]
                        for side in range(2)
                    ]
                yield a, x, main[3 * a + k], tiles, ninth


def assemble_deep(args, exts):
    zero = jnp.zeros((4, 256), F32)
    for a, x, own, tiles, ninth in blocks0(*args):
        ext = exts[a]
        r = 4 + x
        ext[r, 0:4, :] = zero
        ext[r, 12:44, :] = own
        ext[r, 52:56, :] = zero
        for h in range(2):
            cut = pl.ds(128 * h, 128)
            ext[r, 4:12, cut] = tiles[0][h]
            ext[r, 44:52, cut] = tiles[1][h]
            if ninth is not None:
                ext[r, 3:4, cut] = ninth[0][h]
                ext[r, 52:53, cut] = ninth[1][h]
    for x in (0, 15):
        exts[0][x] = jnp.zeros(exts[0].shape[1:], F32)


def assemble0(args, exts):
    for a, x, own, tiles, _ in blocks0(*args):
        ext = exts[a]
        r = 4 + x
        ext[r, 4:36, :] = own
        for h in range(2):
            cut = pl.ds(128 * h, 128)
            ext[r, 0:4, cut] = tiles[0][h][4:8, :]
            ext[r, 36:40, cut] = tiles[1][h][0:4, :]
    for x in (0, 15):
        exts[0][x] = jnp.zeros(exts[0].shape[1:], F32)


def k_descend0(
    b0, c0, g0, below, above, left, right, under, over, b1, c1,
    v0, g1, low, high,
    be, ce, ge, wx, wy, wz, wl, rd, va, vb, tmp,
):
    assemble_deep((b0, c0, g0, below, above, left, right, under, over), (be, ce, ge))
    s = (wx, wy, wz, wl, rd, ce, ge)
    weights(be, s, va, 1.0, 1, 15, 7)
    sweep(va, vb, s, 2, 14, 6)
    sweep(vb, va, s, 3, 13, 5)
    for x in range(8):
        v0[x] = va[4 + x, 8:48, :]
    kept = None
    for x, here, res in residual_rows(va, s, 4, 12):
        if x % 2 == 0:
            kept = res
        else:
            split_pair(tmp, (x - 4) // 2, (kept + res)[4:52, :])
    t = fold_level0(tmp)
    for x in range(4):
        g1[x] = t[x]
        low[x] = gate(place("gx") > 0, b1[x])
        high[x] = gate(place("gx") < lax.axis_size("gx") - 1, b1[x])
    for k in range(3):
        low[4 + k] = c1[k]
        high[4 + k] = c1[1 + k]
        low[7 + k] = t[k]
        high[7 + k] = t[1 + k]


def k_descend1(
    g1, b1, c1, bc2, below, above,
    v1, pay, be, ce, ge,
    wx, wy, wz, wl, rd, va, vb, tmp,
):
    zeros = jnp.zeros((4, 128), F32)
    for ext, own, base, reach in ((be, b1, 0, 4), (ce, c1, 4, 3), (ge, g1, 7, 3)):
        for x in range(-reach, 4 + reach):
            if x < 0:
                val = below[base + x + reach]
            elif x < 4:
                val = own[x]
            else:
                val = above[base + x - 4]
            ext[4 + x, 0:4, :] = zeros
            ext[4 + x, 4:28, :] = val
            ext[4 + x, 28:32, :] = zeros

    s = (wx, wy, wz, wl, rd, ce, ge)
    weights(be, s, va, 0.25, 1, 11, 10)
    sweep(va, vb, s, 2, 10, 8)
    sweep(vb, va, s, 3, 9, 6)
    for x in range(4):
        v1[x] = va[4 + x, 8:24, :]
    kept = None
    for x, here, res in residual_rows(va, s, 4, 8):
        if x % 2 == 0:
            kept = res[8:24, :]
        else:
            tmp[(x - 4) // 2] = kept + res[8:24, :]
    g2 = fold_level1(tmp)
    for k in range(8):
        pay[k, 0] = g2
        pay[k, 1] = bc2[0]
        pay[k, 2] = bc2[1]


def k_pack_v(v0, v1, low, high):
    for out, first in ((low, 0), (high, 5)):
        for k in range(3):
            for q in range(5):
                for h in range(2):
                    out[10 * k + 2 * q + h] = v0[
                        first + k, 8 * q : 8 * q + 8, 128 * h : 128 * h + 128
                    ]
        for k in range(4):
            for q in range(2):
                out[30 + 2 * k + q] = v1[k, 8 * q : 8 * q + 8, :]


def k_pack_y2(v1, below, above, gathered, low, high):
    for out, q, inside in (
        (low, 0, place("gy") > 0), (high, 1, place("gy") < lax.axis_size("gy") - 1)
    ):
        for k in range(3):
            for i in range(8):
                val = gathered[i, k]
                out[8 * k + i] = gate(inside, val) if k == 1 else val
        cut = pl.ds(4 * q, 4)
        for t, x in enumerate(range(-4, 8)):
            if x < 0:
                val = below[30 + 2 * (x + 4) + q, cut, :]
            elif x < 4:
                val = v1[x, pl.ds(12 * q, 4), :]
            else:
                val = above[30 + 2 * (x - 4) + q, cut, :]
            half = 4 * (t % 2)
            out[24 + t // 2, half : half + 4, :] = val


def upper(shape):
    return iota(shape, len(shape) - 1) >= 64


def pair_next(v):
    mask = upper(v[0].shape)
    out = []
    for i in range(8):
        after = v[i + 1] if i < 7 else jnp.zeros_like(v[0])
        out.append(pltpu.roll(jnp.where(mask, v[i], after), 64, 1))
    return out


def pair_last(f):
    mask = upper(f[0].shape)
    out = []
    for i in range(8):
        before = f[i - 1] if i > 0 else jnp.zeros_like(f[0])
        out.append(pltpu.roll(jnp.where(mask, before, f[i]), 64, 1))
    return out


def weights2(b, c, scaling):
    scale = F32(scaling)
    inside = iota(b[0].shape, 1) % 64 < 63
    wx = [scale * harmonic(p, q) for p, q in zip(b, pair_next(b))]
    wy = [scale * harmonic(p, next_y(p)) for p in b]
    wz = [jnp.where(inside, scale * harmonic(p, next_z(p)), F32(0.0)) for p in b]
    back = pair_last(wx)
    rd = []
    for i in range(8):
        d = (wx[i] + back[i]) + (wy[i] + last_y(wy[i])) + (wz[i] + last_z(wz[i])) + c[i]
        rd.append(step_of(d))
    return wx, wy, wz, rd


def residual2(v, g, c, wx, wy, wz):
    fx = [w * (p - q) for w, p, q in zip(wx, v, pair_next(v))]
    back = pair_last(fx)
    out = []
    for i in range(8):
        fy = wy[i] * (v[i] - next_y(v[i]))
        fz = wz[i] * (v[i] - next_z(v[i]))
        flux = (fx[i] - back[i]) + (fy - last_y(fy)) + (fz - last_z(fz))
        out.append(g[i] - (flux + c[i] * v[i]))
    return out


def k_descend2(gathered, left, right, v2, pay, wx2, wy2, wz2, rd2, ce2, ge2, be2, tmp):
    for k, ext in enumerate((ge2, be2, ce2)):
        for i in range(8):
            ext[i, 0:8, :] = left[8 * k + i]
            ext[i, 8:16, :] = gathered[i, k]
            ext[i, 16:24, :] = right[8 * k + i]
    b = [be2[i] for i in range(8)]
    c = [ce2[i] for i in range(8)]
    g = [ge2[i] for i in range(8)]
    wx, wy, wz, rd = weights2(b, c, 0.0625)
    for i in range(8):
        wx2[i] = wx[i]
        wy2[i] = wy[i]
        wz2[i] = wz[i]
        rd2[i] = rd[i]
    v = [p * q for p, q in zip(rd, g)]
    for _ in range(2):
        r = residual2(v, g, c, wx, wy, wz)
        v = [p + q * s for p, q, s in zip(v, rd, r)]
    r = residual2(v, g, c, wx, wy, wz)
    for i in range(8):
        v2[i] = v[i]
    for k, src in enumerate((r, b, c)):
        for t in range(2):
            for i in range(8):
                at = 64 * (2 * k + t) + 8 * i
                tmp[at : at + 8, :] = src[i][4 + 8 * t : 12 + 8 * t, :]
    for t, tile in enumerate(fold_level2(tmp[...])):
        pay[t] = tile


TILES = 6


def block_next(v):
    head = iota(v[0].shape, 1) < 32
    out = []
    for t in range(TILES):
        after = v[t + 1] if t < TILES - 1 else jnp.zeros_like(v[0])
        out.append(pltpu.roll(jnp.where(head, after, v[t]), 96, 1))
    return out


def block_last(f):
    tail = iota(f[0].shape, 1) >= 96
    out = []
    for t in range(TILES):
        before = f[t - 1] if t > 0 else jnp.zeros_like(f[0])
        out.append(pltpu.roll(jnp.where(tail, before, f[t]), 32, 1))
    return out


def solve3(g, b, c):
    scale = F32(0.015625)
    shape = g[0].shape
    inside_x = iota(shape, 0) < 7
    inside_z = iota(shape, 1) % 32 < 31
    zero = F32(0.0)
    wx = [jnp.where(inside_x, scale * harmonic(p, next_y(p)), zero) for p in b]
    wy = [scale * harmonic(p, q) for p, q in zip(b, block_next(b))]
    wz = [jnp.where(inside_z, scale * harmonic(p, next_z(p)), zero) for p in b]
    xl = [last_y(p) for p in wx]
    yl = block_last(wy)
    zl = [last_z(p) for p in wz]
    rd = []
    for t in range(TILES):
        d = (wx[t] + xl[t]) + (wy[t] + yl[t]) + (wz[t] + zl[t]) + c[t]
        rd.append(step_of(d))
    e = [p * q for p, q in zip(rd, g)]
    for _ in range(7):
        up = block_next(e)
        down = block_last(e)
        new = []
        for t in range(TILES):
            h = e[t]
            flux = wx[t] * (h - next_y(h)) + xl[t] * (h - last_y(h))
            flux = flux + (wy[t] * (h - up[t]) + yl[t] * (h - down[t]))
            flux = flux + (wz[t] * (h - next_z(h)) + zl[t] * (h - last_z(h)))
            new.append(h + rd[t] * (g[t] - (flux + c[t] * h)))
        e = new
    return e


def k_prepare(
    b0, c0, g0, below0, above0, left0, right0, under0, over0, be1, ce1, ge1,
    v0, v1, below, above, left1, right1,
    p0, ce, ge, wx, wy, wz, wl, rd, p1, wx1, wy1, wz1, wl1, rd1,
    be, va, va1,
):
    assemble0((b0, c0, g0, below0, above0, left0, right0, under0, over0), (be, ce, ge))
    weights(be, (wx, wy, wz, wl, rd, ce, ge), va, 1.0, 2, 14, 6)
    weights(be1, (wx1, wy1, wz1, wl1, rd1, ce1, ge1), va1, 0.25, 1, 11, 10)
    zero = jnp.zeros((8, 128), F32)
    for t, x in enumerate(range(-4, 8)):
        p1[t, 0:8, :] = zero
        p1[t, 24:32, :] = zero
        if 0 <= x < 4:
            p1[t, 8:24, :] = v1[x]
        else:
            src, k = (below, x + 4) if x < 0 else (above, x - 4)
            for q in range(2):
                p1[t, 8 + 8 * q : 16 + 8 * q, :] = src[30 + 2 * k + q]
        half = 4 * (t % 2)
        p1[t, 4:8, :] = left1[24 + t // 2, half : half + 4, :]
        p1[t, 24:28, :] = right1[24 + t // 2, half : half + 4, :]
    for x in range(-3, 11):
        if 0 <= x < 8:
            p0[4 + x] = v0[x]
        else:
            src, k = (below, x + 3) if x < 0 else (above, x - 8)
            for q in range(5):
                for h in range(2):
                    p0[4 + x, 8 * q : 8 * q + 8, 128 * h : 128 * h + 128] = (
                        src[10 * k + 2 * q + h]
                    )


def k_ascend(
    own3, r0, r1, v2, wx2, wy2, wz2, rd2, ce2, ge2,
    p0, ce0, ge0, wx0, wy0, wz0, wl0, rd0,
    p1, ce1, ge1, wx1, wy1, wz1, wl1, rd1,
    pressure, residual,
    all3, m2, p2, p1a, p1b, p0a, p0b, f1, f0, own, res0, sems,
):
    ix = place("gx")
    iy = place("gy")
    count = lax.axis_size("gy")
    even_chip = lax.rem(iy // 2, 2) == 0
    zero = F32(0.0)

    for k in range(3):
        first = [jnp.where(even_chip, r1[2 * k + t], r0[2 * k + t]) for t in range(2)]
        last = [jnp.where(even_chip, r0[2 * k + t], r1[2 * k + t]) for t in range(2)]
        at = TILES * k
        all3[at] = gate(iy >= 2, first[0])
        all3[at + 1] = jnp.where(iy >= 2, first[1], gate(iy == 1, first[0]))
        all3[at + 2] = own3[2 * k]
        all3[at + 3] = own3[2 * k + 1]
        all3[at + 4] = jnp.where(iy < count - 2, last[0], gate(iy == count - 2, last[1]))
        all3[at + 5] = gate(iy < count - 2, last[1])
    e = solve3(*[[all3[TILES * k + t] for t in range(TILES)] for k in range(3)])

    group = iota((8, 128), 1) // 32 == iota((8, 128), 0) // 2
    for t in range(2):
        for i in range(8):
            row = jnp.broadcast_to(e[2 + t][i : i + 1, :], (8, 128))
            m2[16 * i + 8 * t : 16 * i + 8 * t + 8, :] = jnp.where(group, row, zero)
    spread = jnp.where(
        iota((128, 128), 0) % 32 == (iota((128, 128), 1) % 64) // 2, F32(1.0), zero
    )
    fine = pick(m2[...], spread)
    for i in range(8):
        p2[i] = v2[i]
        p2[i, 4:20, :] += fine[16 * i : 16 * i + 16, :]
    v = [p2[i] for i in range(8)]
    g = [ge2[i] for i in range(8)]
    c = [ce2[i] for i in range(8)]
    wx = [wx2[i] for i in range(8)]
    wy = [wy2[i] for i in range(8)]
    wz = [wz2[i] for i in range(8)]
    for _ in range(2):
        r = residual2(v, g, c, wx, wy, wz)
        v = [v[i] + rd2[i] * r[i] for i in range(8)]
    for i in range(8):
        p2[i] = v[i]

    parts = []
    for q in range(3):
        at = ix + (q - 1)
        inside = jnp.logical_and(at >= 0, at < lax.axis_size("gx"))
        parts.append(jnp.where(inside, p2[jnp.clip(at, 0, 7), 4:20, :], zero))
    row = iota((128, 256), 0)
    lane = iota((128, 256), 1)
    hit = (row % 64 == (lane % 128) // 2) & (row // 64 == lane // 128)
    fine = pick(jnp.concatenate(parts, axis=0), jnp.where(hit, F32(1.0), zero))
    for q in range(3):
        for h in range(2):
            part = fine[16 * q : 16 * q + 16, 128 * h : 128 * h + 128]
            f1[2 * q + h, pl.ds(0, 16, stride=2), :] = part
            f1[2 * q + h, pl.ds(1, 16, stride=2), :] = part
    for x in range(12):
        p1a[x] = p1[x] + f1[x // 2]
    s1 = (wx1, wy1, wz1, wl1, rd1, ce1, ge1)
    sweep(p1a, p1b, s1, 1, 11, 10)
    sweep(p1b, p1a, s1, 2, 10, 8)

    wide = jnp.where(iota((128, 256), 0) == iota((128, 256), 1) // 2, F32(1.0), zero)
    fine = pick(jnp.concatenate([p1a[2 + x, 6:26, :] for x in range(8)], axis=0), wide)
    for x in range(8):
        for h in range(2):
            part = fine[20 * x : 20 * x + 20, 128 * h : 128 * h + 128]
            f0[x, h, pl.ds(0, 20, stride=2), :] = part
            f0[x, h, pl.ds(1, 20, stride=2), :] = part
    for x in range(1, 15):
        for h in range(2):
            cut = pl.ds(128 * h, 128)
            p0a[x, :, cut] = p0[x, :, cut] + f0[x // 2, h]
    s0 = (wx0, wy0, wz0, wl0, rd0, ce0, ge0)
    sweep(p0a, p0b, s0, 2, 14, 6)
    sweep(p0b, p0a, s0, 3, 13, 5)
    for x in range(8):
        own[x] = p0a[4 + x, 4:36, :]
    copies = [pltpu.make_async_copy(own, pressure, sems.at[0])]
    copies[0].start()
    for x, here, res in residual_rows(p0a, s0, 4, 12):
        res0[x - 4] = res[4:36, :]
        if x % 4 == 3:
            cut = pl.ds(x - 7, 4)
            copies.append(pltpu.make_async_copy(res0.at[cut], residual.at[cut], sems.at[x // 4]))
            copies[-1].start()
    for copy in copies:
        copy.wait()


def call(kernel, name, outs, scratch, limit, *args, anywhere=(), to_hbm=False):
    vmem = pl.BlockSpec(memory_space=pltpu.VMEM)
    hbm = pl.BlockSpec(memory_space=pltpu.HBM)
    specs = [vmem for _ in args]
    for k in anywhere:
        specs[k] = hbm
    return pl.pallas_call(
        kernel,
        name=name,
        out_shape=[jax.ShapeDtypeStruct(s, F32) for s in outs],
        in_specs=specs,
        out_specs=[hbm if to_hbm else vmem for _ in outs],
        scratch_shapes=[pltpu.VMEM(s, F32) if isinstance(s, tuple) else s for s in scratch],
        compiler_params=pltpu.CompilerParams(vmem_limit_bytes=limit * MIB),
    )(*args)


B0 = (8, 32, 256)
E0 = (16, 40, 256)
E1 = (12, 32, 128)
E2 = (8, 24, 128)


def per_device(source, material, flags):
    source, material, flags = (
        pltpu.with_memory_space_constraint(a, pltpu.HBM) for a in (source, material, flags)
    )
    left, right, b0, c0, g0 = call(
        k_load0, "load0", [(STRIPS, 8, 128)] * 2 + [B0] * 3,
        [pltpu.VMEM(B0, jnp.int32), pltpu.VMEM(B0, jnp.int32), pltpu.SemaphoreType.DMA((3,))],
        4, material, flags, source, anywhere=(0, 1, 2),
    )
    left0, right0 = exchange(left, right, "gy")
    low, high = call(k_edge0, "edge0", [(9, 32, 256)] * 2, [], 4, b0, c0, g0)
    below0, above0 = exchange(low, high, "gx")
    low, high = call(k_corner0, "corner0", [(CORNERS, 8, 128)] * 2, [], 4, left0, right0)
    under0, over0 = exchange(low, high, "gx")
    b1, c1, bc2 = call(
        k_coefs, "coefs", [(4, 24, 128), (4, 24, 128), (2, 8, 128)],
        [(4, 2, 48, 128), (2, 16, 128)], 4, b0, c0, left0, right0,
    )
    own0 = (b0, c0, g0, below0, above0, left0, right0, under0, over0)
    v0, g1, low, high = call(
        k_descend0, "descend0",
        [(8, 40, 256), (4, 24, 128), (10, 24, 128), (10, 24, 128)],
        [(16, 56, 256)] * 10 + [(4, 2, 48, 128)], 16, *own0, b1, c1,
    )
    below, above = exchange(low, high, "gx")
    v1, pay, be1, ce1, ge1 = call(
        k_descend1, "descend1",
        [(4, 16, 128), (8, 3, 8, 128)] + [E1] * 3,
        [E1] * 7 + [(2, 16, 128)], 4,
        g1, b1, c1, bc2, below, above,
    )
    gathered = lax.all_to_all(pay, "gx", 0, 0)
    low, high = call(k_pack_v, "pack_v", [(38, 8, 128)] * 2, [], 4, v0, v1)
    below, above = exchange(low, high, "gx")
    low, high = call(
        k_pack_y2, "pack_y2", [(30, 8, 128)] * 2, [], 4, v1, below, above, gathered
    )
    left1, right1 = exchange(low, high, "gy")
    v2, own3, *s2 = call(
        k_descend2, "descend2", [E2, (6, 8, 128)] + [E2] * 6, [E2, (384, 128)], 4,
        gathered, left1, right1,
    )
    r0, r1 = swap_chips(own3, "gy", 0), swap_chips(own3, "gy", 1)
    p0, ce0, ge0, wx0, wy0, wz0, wl0, rd0, p1, *w1 = call(
        k_prepare, "prepare", [E0] * 8 + [E1] * 6, [E0, E0, E1], 8,
        *own0, be1, ce1, ge1, v0, v1, below, above, left1, right1,
    )
    pressure, residual = call(
        k_ascend, "ascend", [B0] * 2,
        [(18, 8, 128), (128, 128), E2, E1, E1, E0, E0, (6, 32, 128), (8, 2, 40, 128),
         B0, B0, pltpu.SemaphoreType.DMA((3,))],
        8, own3, r0, r1, v2, *s2,
        p0, ce0, ge0, wx0, wy0, wz0, wl0, rd0, p1, ce1, ge1, *w1, to_hbm=True,
    )
    return pressure, residual


def solution(mesh):
    spec = P("gx", "gy", None)
    return jax.shard_map(
        per_device,
        mesh=mesh,
        in_specs=(spec, spec, spec),
        out_specs=(spec, spec),
        check_vma=False,
    )
```

```python
import jax
import jax.numpy as jnp
from jax import lax
from jax.experimental import pallas as pl
from jax.experimental.pallas import tpu as pltpu
from jax.sharding import PartitionSpec as P

F32 = jnp.float32
BF16 = jnp.bfloat16
OMEGA = 0.8
SHIFT = 0.001
ROBIN = 2.0
INVERSE_SOLID = 1.0 / 3.0
INVERSE_DENSE = 0.125
MIB = 1 << 20


def shift(block, axis, step):
    count = lax.axis_size(axis)
    return lax.ppermute(block, axis, [(i, (i + step) % count) for i in range(count)])


def exchange(low, high, axis):
    return shift(high, axis, 1), shift(low, axis, -1)


def swap_chips(block, axis, parity):
    count = lax.axis_size(axis)
    pairs = [(i, i + 2) for i in range(count - 2) if (i // 2) % 2 == parity]
    if parity == 1:
        pairs = [(0, 1)] + pairs + [(count - 2, count - 1)]
    return lax.ppermute(block, axis, pairs + [(b, a) for a, b in pairs])


def iota(shape, dim):
    return lax.broadcasted_iota(jnp.int32, shape, dim)


def pick(a, w):
    count = a.shape[0]
    a1 = a.astype(BF16).astype(F32)
    a2 = (a - a1).astype(BF16).astype(F32)
    parts = [a1, a2, (a - a1) - a2]
    if 3 * count % 16:
        parts.append(jnp.zeros((16 - 3 * count % 16, a.shape[1]), F32))
    stacked = jnp.concatenate(parts, axis=0).astype(BF16)
    out = jnp.dot(stacked, w.astype(BF16), preferred_element_type=F32)
    return out[:count] + out[count : 2 * count] + out[2 * count : 3 * count]


def inverse_density(material):
    return jnp.where(
        material == 0, F32(1.0), jnp.where(material == 1, F32(INVERSE_SOLID), F32(INVERSE_DENSE))
    )


def reaction_of(flags):
    return F32(SHIFT) + F32(ROBIN) * flags.astype(F32)


def harmonic(a, b):
    return (2.0 * a * b) * (1.0 / jnp.maximum(a + b, F32(1e-30)))


def step_of(d):
    return jnp.where(d > 0, F32(OMEGA) / jnp.where(d > 0, d, F32(1.0)), F32(0.0))


def fold_level0(tmp):
    parts = []
    for h in range(2):
        parts.append(
            jnp.concatenate(
                [
                    tmp[x, h, pl.ds(0, 24, stride=2), :] + tmp[x, h, pl.ds(1, 24, stride=2), :]
                    for x in range(4)
                ],
                axis=0,
            )
        )
    w = jnp.where(iota((256, 128), 0) // 2 == iota((256, 128), 1), F32(0.125), F32(0.0))
    return pick(jnp.concatenate(parts, axis=1), w).reshape(4, 24, 128)


def fold_level1(tmp):
    parts = [
        tmp[x, pl.ds(0, 8, stride=2), :] + tmp[x, pl.ds(1, 8, stride=2), :] for x in range(2)
    ]
    row = iota((256, 128), 0)
    lane = iota((256, 128), 1)
    hit = ((row % 128) // 2 == lane % 64) & (row // 128 == lane // 64)
    return pick(jnp.concatenate(parts, axis=1), jnp.where(hit, F32(0.125), F32(0.0)))


def fold_level2(tiles):
    count = tiles.shape[0] // 64
    hit = (iota((128, 128), 0) % 64) // 2 == iota((128, 128), 1) % 32
    t = pick(tiles, jnp.where(hit, F32(0.125), F32(0.0))).reshape(count, 8, 8, 128)
    keep = iota(t.shape, 2) // 2 == iota(t.shape, 3) // 32
    t = jnp.sum(jnp.where(keep, t, F32(0.0)), axis=2)
    return [t[k] for k in range(count)]


def next_y(v):
    return pltpu.roll(v, v.shape[0] - 1, 0)


def last_y(v):
    return pltpu.roll(v, 1, 0)


def next_z(v):
    return pltpu.roll(v, v.shape[1] - 1, 1)


def last_z(v):
    return pltpu.roll(v, 1, 1)


def weights(b, s, v, scaling, low, high, unroll):
    wx, wy, wz, wl, rd, c, g = s
    scale = F32(scaling)
    prev = scale * harmonic(b[low - 1], b[low])
    wx[low - 1] = prev
    shape = prev.shape
    inside = iota(shape, 1) < shape[1] - 1

    def body(x, prev):
        here = b[x]
        cur = scale * harmonic(here, b[x + 1])
        wx[x] = cur
        fy = scale * harmonic(here, next_y(here))
        wy[x] = fy
        fz = jnp.where(inside, scale * harmonic(here, next_z(here)), F32(0.0))
        wz[x] = fz
        fl = last_z(fz)
        wl[x] = fl
        r = step_of((prev + cur) + (fy + last_y(fy)) + (fz + fl) + c[x])
        rd[x] = r
        v[x] = r * g[x]
        return cur

    lax.fori_loop(low, high, body, prev, unroll=unroll)


def row_residual(v, s, x, prev):
    wx, wy, wz, wl, rd, c, g = s
    here = v[x]
    cur = wx[x] * (here - v[x + 1])
    fy = wy[x] * (here - next_y(here))
    fz = wz[x] * (here - next_z(here)) + wl[x] * (here - last_z(here))
    flux = (cur - prev) + (fy - last_y(fy)) + fz
    return here, g[x] - (flux + c[x] * here), cur


def sweep(src, dst, s, low, high, unroll):
    rd = s[4]

    def body(x, prev):
        here, res, cur = row_residual(src, s, x, prev)
        dst[x] = here + rd[x] * res
        return cur

    first = s[0][low - 1] * (src[low - 1] - src[low])
    lax.fori_loop(low, high, body, first, unroll=unroll)


def residual_rows(v, s, low, high):
    prev = s[0][low - 1] * (v[low - 1] - v[low])
    for x in range(low, high):
        here, res, prev = row_residual(v, s, x, prev)
        yield x, here, res


def place(axis):
    return lax.axis_index(axis)


def gate(inside, value):
    return jnp.where(inside, value, F32(0.0))


STRIPS = 54


def k_load0(m, f, g, left, right, b0, c0, g0, mv, fv, sems):
    copies = [
        pltpu.make_async_copy(m, mv, sems.at[0]),
        pltpu.make_async_copy(f, fv, sems.at[1]),
        pltpu.make_async_copy(g, g0, sems.at[2]),
    ]
    for copy in copies:
        copy.start()

    def strips(a, own):
        for x in range(8):
            for out, at, ninth, tenth, inside in (
                (left, 0, 8, 9, place("gy") > 0),
                (right, 24, 23, 22, place("gy") < lax.axis_size("gy") - 1),
            ):
                near = own[x, at : at + 8, :]
                far = own[x, ninth : ninth + 1, :]
                if a == 0:
                    near, far = gate(inside, near), gate(inside, far)
                if a == 1:
                    far = far + harmonic(b0[x, ninth : ninth + 1, :], b0[x, tenth : tenth + 1, :])
                for h in range(2):
                    cut = slice(128 * h, 128 * h + 128)
                    out[16 * a + 2 * x + h] = near[:, cut]
                    out[48 + 2 * a + h, x : x + 1, :] = far[:, cut]

    copies[0].wait()
    for x in range(8):
        b0[x] = inverse_density(mv[x])
    strips(0, b0)
    copies[1].wait()
    for x in range(8):
        c0[x] = reaction_of(fv[x])
    strips(1, c0)
    copies[2].wait()
    strips(2, g0)


def k_edge0(b0, c0, g0, low, high):
    for k in range(3):
        low[k] = gate(place("gx") > 0, b0[k])
        high[k] = gate(place("gx") < lax.axis_size("gx") - 1, b0[5 + k])
        low[3 + k] = c0[k] + harmonic(b0[2], b0[3]) if k == 2 else c0[k]
        high[3 + k] = c0[5 + k] + harmonic(b0[5], b0[4]) if k == 0 else c0[5 + k]
        low[6 + k] = g0[k]
        high[6 + k] = g0[5 + k]


def split_pair(tmp, k, value):
    for h in range(2):
        tmp[k, h] = value[:, 128 * h : 128 * h + 128]


def k_coefs(b0, c0, left, right, b1, c1, bc2, tmp0, tmp1):
    for k, (src, out) in enumerate(((b0, b1), (c0, c1))):
        for x in range(4):
            pair = src[2 * x] + src[2 * x + 1]
            for h in range(2):
                t = 16 * k + 4 * x + h
                tmp0[x, h, 0:8, :] = left[t] + left[t + 2]
                tmp0[x, h, 8:40, :] = pair[:, 128 * h : 128 * h + 128]
                tmp0[x, h, 40:48, :] = right[t] + right[t + 2]
        t = fold_level0(tmp0)
        for x in range(4):
            out[x] = t[x]
        for x in range(2):
            tmp1[x] = (t[2 * x] + t[2 * x + 1])[4:20, :]
        bc2[k] = fold_level1(tmp1)


CORNERS = 37


def k_corner0(left, right, low, high):
    for out, first, edge, third, fourth, inside in (
        (low, 0, 0, 2, 3, place("gx") > 0),
        (high, 5, 7, 5, 4, place("gx") < lax.axis_size("gx") - 1),
    ):
        out[36] = jnp.zeros((8, 128), F32)
        for side, strips in enumerate((left, right)):
            for h in range(2):
                for k in range(3):
                    x = first + k
                    at = 18 * side + 2 * k + h
                    out[at] = gate(inside, strips[2 * x + h])
                    c = strips[16 + 2 * x + h]
                    if x == third:
                        c = c + harmonic(strips[2 * x + h], strips[2 * fourth + h])
                    out[at + 6] = c
                    out[at + 12] = strips[32 + 2 * x + h]
                at = 2 * side + h
                out[36, at : at + 1, :] = gate(inside, strips[48 + h, edge : edge + 1, :])


def blocks0(b0, c0, g0, below, above, left, right, under, over):
    for a, own in enumerate((b0, c0, g0)):
        for x in range(-3, 11):
            if 0 <= x < 8:
                tiles = [[s[16 * a + 2 * x + h] for h in range(2)] for s in (left, right)]
                ninth = [[s[48 + 2 * a + h, x : x + 1, :] for h in range(2)] for s in (left, right)]
                yield a, x, own[x], tiles, ninth
            else:
                k = x + 3 if x < 0 else x - 8
                main, far = (below, under) if x < 0 else (above, over)
                tiles = [[far[18 * side + 6 * a + 2 * k + h] for h in range(2)] for side in range(2)]
                ninth = None
                if a == 0 and x in (-1, 8):
                    ninth = [
                        [far[36, 2 * side + h : 2 * side + h + 1, :] for h in range(2)]
                        for side in range(2)
                    ]
                yield a, x, main[3 * a + k], tiles, ninth


def assemble_deep(args, exts):
    zero = jnp.zeros((4, 256), F32)
    for a, x, own, tiles, ninth in blocks0(*args):
        ext = exts[a]
        r = 4 + x
        ext[r, 0:4, :] = zero
        ext[r, 12:44, :] = own
        ext[r, 52:56, :] = zero
        for h in range(2):
            cut = pl.ds(128 * h, 128)
            ext[r, 4:12, cut] = tiles[0][h]
            ext[r, 44:52, cut] = tiles[1][h]
            if ninth is not None:
                ext[r, 3:4, cut] = ninth[0][h]
                ext[r, 52:53, cut] = ninth[1][h]
    for x in (0, 15):
        exts[0][x] = jnp.zeros(exts[0].shape[1:], F32)


def assemble0(args, exts):
    for a, x, own, tiles, _ in blocks0(*args):
        ext = exts[a]
        r = 4 + x
        ext[r, 4:36, :] = own
        for h in range(2):
            cut = pl.ds(128 * h, 128)
            ext[r, 0:4, cut] = tiles[0][h][4:8, :]
            ext[r, 36:40, cut] = tiles[1][h][0:4, :]
    for x in (0, 15):
        exts[0][x] = jnp.zeros(exts[0].shape[1:], F32)


def k_descend0(
    b0, c0, g0, below, above, left, right, under, over, b1, c1,
    v0, g1, low, high,
    be, ce, ge, wx, wy, wz, wl, rd, va, vb, tmp,
):
    assemble_deep((b0, c0, g0, below, above, left, right, under, over), (be, ce, ge))
    s = (wx, wy, wz, wl, rd, ce, ge)
    weights(be, s, va, 1.0, 1, 15, 7)
    sweep(va, vb, s, 2, 14, 12)
    sweep(vb, va, s, 3, 13, 10)
    for x in range(8):
        v0[x] = va[4 + x, 8:48, :]
    kept = None
    for x, here, res in residual_rows(va, s, 4, 12):
        if x % 2 == 0:
            kept = res
        else:
            split_pair(tmp, (x - 4) // 2, (kept + res)[4:52, :])
    t = fold_level0(tmp)
    for x in range(4):
        g1[x] = t[x]
        low[x] = gate(place("gx") > 0, b1[x])
        high[x] = gate(place("gx") < lax.axis_size("gx") - 1, b1[x])
    for k in range(3):
        low[4 + k] = c1[k]
        high[4 + k] = c1[1 + k]
        low[7 + k] = t[k]
        high[7 + k] = t[1 + k]


def k_descend1(
    g1, b1, c1, bc2, below, above,
    v1, pay, be, ce, ge,
    wx, wy, wz, wl, rd, va, vb, tmp,
):
    zeros = jnp.zeros((4, 128), F32)
    for ext, own, base, reach in ((be, b1, 0, 4), (ce, c1, 4, 3), (ge, g1, 7, 3)):
        for x in range(-reach, 4 + reach):
            if x < 0:
                val = below[base + x + reach]
            elif x < 4:
                val = own[x]
            else:
                val = above[base + x - 4]
            ext[4 + x, 0:4, :] = zeros
            ext[4 + x, 4:28, :] = val
            ext[4 + x, 28:32, :] = zeros

    s = (wx, wy, wz, wl, rd, ce, ge)
    weights(be, s, va, 0.25, 1, 11, 10)
    sweep(va, vb, s, 2, 10, 8)
    sweep(vb, va, s, 3, 9, 6)
    for x in range(4):
        v1[x] = va[4 + x, 8:24, :]
    kept = None
    for x, here, res in residual_rows(va, s, 4, 8):
        if x % 2 == 0:
            kept = res[8:24, :]
        else:
            tmp[(x - 4) // 2] = kept + res[8:24, :]
    g2 = fold_level1(tmp)
    for k in range(8):
        pay[k, 0] = g2
        pay[k, 1] = bc2[0]
        pay[k, 2] = bc2[1]


def k_pack_v(v0, v1, low, high):
    for out, first in ((low, 0), (high, 5)):
        for k in range(3):
            for q in range(5):
                for h in range(2):
                    out[10 * k + 2 * q + h] = v0[
                        first + k, 8 * q : 8 * q + 8, 128 * h : 128 * h + 128
                    ]
        for k in range(4):
            for q in range(2):
                out[30 + 2 * k + q] = v1[k, 8 * q : 8 * q + 8, :]


def k_pack_y2(v1, below, above, gathered, low, high):
    for out, q, inside in (
        (low, 0, place("gy") > 0), (high, 1, place("gy") < lax.axis_size("gy") - 1)
    ):
        for k in range(3):
            for i in range(8):
                val = gathered[i, k]
                out[8 * k + i] = gate(inside, val) if k == 1 else val
        cut = pl.ds(4 * q, 4)
        for t, x in enumerate(range(-4, 8)):
            if x < 0:
                val = below[30 + 2 * (x + 4) + q, cut, :]
            elif x < 4:
                val = v1[x, pl.ds(12 * q, 4), :]
            else:
                val = above[30 + 2 * (x - 4) + q, cut, :]
            half = 4 * (t % 2)
            out[24 + t // 2, half : half + 4, :] = val


def upper(shape):
    return iota(shape, len(shape) - 1) >= 64


def pair_next(v):
    mask = upper(v[0].shape)
    out = []
    for i in range(8):
        after = v[i + 1] if i < 7 else jnp.zeros_like(v[0])
        out.append(pltpu.roll(jnp.where(mask, v[i], after), 64, 1))
    return out


def pair_last(f):
    mask = upper(f[0].shape)
    out = []
    for i in range(8):
        before = f[i - 1] if i > 0 else jnp.zeros_like(f[0])
        out.append(pltpu.roll(jnp.where(mask, before, f[i]), 64, 1))
    return out


def weights2(b, c, scaling):
    scale = F32(scaling)
    inside = iota(b[0].shape, 1) % 64 < 63
    wx = [scale * harmonic(p, q) for p, q in zip(b, pair_next(b))]
    wy = [scale * harmonic(p, next_y(p)) for p in b]
    wz = [jnp.where(inside, scale * harmonic(p, next_z(p)), F32(0.0)) for p in b]
    back = pair_last(wx)
    rd = []
    for i in range(8):
        d = (wx[i] + back[i]) + (wy[i] + last_y(wy[i])) + (wz[i] + last_z(wz[i])) + c[i]
        rd.append(step_of(d))
    return wx, wy, wz, rd


def residual2(v, g, c, wx, wy, wz):
    fx = [w * (p - q) for w, p, q in zip(wx, v, pair_next(v))]
    back = pair_last(fx)
    out = []
    for i in range(8):
        fy = wy[i] * (v[i] - next_y(v[i]))
        fz = wz[i] * (v[i] - next_z(v[i]))
        flux = (fx[i] - back[i]) + (fy - last_y(fy)) + (fz - last_z(fz))
        out.append(g[i] - (flux + c[i] * v[i]))
    return out


def k_descend2(gathered, left, right, v2, pay, wx2, wy2, wz2, rd2, ce2, ge2, be2, tmp):
    for k, ext in enumerate((ge2, be2, ce2)):
        for i in range(8):
            ext[i, 0:8, :] = left[8 * k + i]
            ext[i, 8:16, :] = gathered[i, k]
            ext[i, 16:24, :] = right[8 * k + i]
    b = [be2[i] for i in range(8)]
    c = [ce2[i] for i in range(8)]
    g = [ge2[i] for i in range(8)]
    wx, wy, wz, rd = weights2(b, c, 0.0625)
    for i in range(8):
        wx2[i] = wx[i]
        wy2[i] = wy[i]
        wz2[i] = wz[i]
        rd2[i] = rd[i]
    v = [p * q for p, q in zip(rd, g)]
    for _ in range(2):
        r = residual2(v, g, c, wx, wy, wz)
        v = [p + q * s for p, q, s in zip(v, rd, r)]
    r = residual2(v, g, c, wx, wy, wz)
    for i in range(8):
        v2[i] = v[i]
    for k, src in enumerate((r, b, c)):
        for t in range(2):
            for i in range(8):
                at = 64 * (2 * k + t) + 8 * i
                tmp[at : at + 8, :] = src[i][4 + 8 * t : 12 + 8 * t, :]
    for t, tile in enumerate(fold_level2(tmp[...])):
        pay[t] = tile


TILES = 6


def block_next(v):
    head = iota(v[0].shape, 1) < 32
    out = []
    for t in range(TILES):
        after = v[t + 1] if t < TILES - 1 else jnp.zeros_like(v[0])
        out.append(pltpu.roll(jnp.where(head, after, v[t]), 96, 1))
    return out


def block_last(f):
    tail = iota(f[0].shape, 1) >= 96
    out = []
    for t in range(TILES):
        before = f[t - 1] if t > 0 else jnp.zeros_like(f[0])
        out.append(pltpu.roll(jnp.where(tail, before, f[t]), 32, 1))
    return out


def solve3(g, b, c):
    scale = F32(0.015625)
    shape = g[0].shape
    inside_x = iota(shape, 0) < 7
    inside_z = iota(shape, 1) % 32 < 31
    zero = F32(0.0)
    wx = [jnp.where(inside_x, scale * harmonic(p, next_y(p)), zero) for p in b]
    wy = [scale * harmonic(p, q) for p, q in zip(b, block_next(b))]
    wz = [jnp.where(inside_z, scale * harmonic(p, next_z(p)), zero) for p in b]
    xl = [last_y(p) for p in wx]
    yl = block_last(wy)
    zl = [last_z(p) for p in wz]
    rd = []
    for t in range(TILES):
        d = (wx[t] + xl[t]) + (wy[t] + yl[t]) + (wz[t] + zl[t]) + c[t]
        rd.append(step_of(d))
    e = [p * q for p, q in zip(rd, g)]
    for _ in range(7):
        up = block_next(e)
        down = block_last(e)
        new = []
        for t in range(TILES):
            h = e[t]
            flux = wx[t] * (h - next_y(h)) + xl[t] * (h - last_y(h))
            flux = flux + (wy[t] * (h - up[t]) + yl[t] * (h - down[t]))
            flux = flux + (wz[t] * (h - next_z(h)) + zl[t] * (h - last_z(h)))
            new.append(h + rd[t] * (g[t] - (flux + c[t] * h)))
        e = new
    return e


def k_prepare(
    b0, c0, g0, below0, above0, left0, right0, under0, over0, be1, ce1, ge1,
    v0, v1, below, above, left1, right1,
    p0, ce, ge, wx, wy, wz, wl, rd, p1, wx1, wy1, wz1, wl1, rd1,
    be, va, va1,
):
    assemble0((b0, c0, g0, below0, above0, left0, right0, under0, over0), (be, ce, ge))
    weights(be, (wx, wy, wz, wl, rd, ce, ge), va, 1.0, 2, 14, 6)
    weights(be1, (wx1, wy1, wz1, wl1, rd1, ce1, ge1), va1, 0.25, 1, 11, 10)
    zero = jnp.zeros((8, 128), F32)
    for t, x in enumerate(range(-4, 8)):
        p1[t, 0:8, :] = zero
        p1[t, 24:32, :] = zero
        if 0 <= x < 4:
            p1[t, 8:24, :] = v1[x]
        else:
            src, k = (below, x + 4) if x < 0 else (above, x - 4)
            for q in range(2):
                p1[t, 8 + 8 * q : 16 + 8 * q, :] = src[30 + 2 * k + q]
        half = 4 * (t % 2)
        p1[t, 4:8, :] = left1[24 + t // 2, half : half + 4, :]
        p1[t, 24:28, :] = right1[24 + t // 2, half : half + 4, :]
    for x in range(-3, 11):
        if 0 <= x < 8:
            p0[4 + x] = v0[x]
        else:
            src, k = (below, x + 3) if x < 0 else (above, x - 8)
            for q in range(5):
                for h in range(2):
                    p0[4 + x, 8 * q : 8 * q + 8, 128 * h : 128 * h + 128] = (
                        src[10 * k + 2 * q + h]
                    )


def k_ascend(
    own3, r0, r1, v2, wx2, wy2, wz2, rd2, ce2, ge2,
    p0, ce0, ge0, wx0, wy0, wz0, wl0, rd0,
    p1, ce1, ge1, wx1, wy1, wz1, wl1, rd1,
    pressure, residual,
    all3, m2, p2, p1a, p1b, p0a, p0b, f1, f0, own, res0, sems,
):
    ix = place("gx")
    iy = place("gy")
    count = lax.axis_size("gy")
    even_chip = lax.rem(iy // 2, 2) == 0
    zero = F32(0.0)

    for k in range(3):
        first = [jnp.where(even_chip, r1[2 * k + t], r0[2 * k + t]) for t in range(2)]
        last = [jnp.where(even_chip, r0[2 * k + t], r1[2 * k + t]) for t in range(2)]
        at = TILES * k
        all3[at] = gate(iy >= 2, first[0])
        all3[at + 1] = jnp.where(iy >= 2, first[1], gate(iy == 1, first[0]))
        all3[at + 2] = own3[2 * k]
        all3[at + 3] = own3[2 * k + 1]
        all3[at + 4] = jnp.where(iy < count - 2, last[0], gate(iy == count - 2, last[1]))
        all3[at + 5] = gate(iy < count - 2, last[1])
    e = solve3(*[[all3[TILES * k + t] for t in range(TILES)] for k in range(3)])

    group = iota((8, 128), 1) // 32 == iota((8, 128), 0) // 2
    for t in range(2):
        for i in range(8):
            row = jnp.broadcast_to(e[2 + t][i : i + 1, :], (8, 128))
            m2[16 * i + 8 * t : 16 * i + 8 * t + 8, :] = jnp.where(group, row, zero)
    spread = jnp.where(
        iota((128, 128), 0) % 32 == (iota((128, 128), 1) % 64) // 2, F32(1.0), zero
    )
    fine = pick(m2[...], spread)
    for i in range(8):
        p2[i] = v2[i]
        p2[i, 4:20, :] += fine[16 * i : 16 * i + 16, :]
    v = [p2[i] for i in range(8)]
    g = [ge2[i] for i in range(8)]
    c = [ce2[i] for i in range(8)]
    wx = [wx2[i] for i in range(8)]
    wy = [wy2[i] for i in range(8)]
    wz = [wz2[i] for i in range(8)]
    for _ in range(2):
        r = residual2(v, g, c, wx, wy, wz)
        v = [v[i] + rd2[i] * r[i] for i in range(8)]
    for i in range(8):
        p2[i] = v[i]

    parts = []
    for q in range(3):
        at = ix + (q - 1)
        inside = jnp.logical_and(at >= 0, at < lax.axis_size("gx"))
        parts.append(jnp.where(inside, p2[jnp.clip(at, 0, 7), 4:20, :], zero))
    row = iota((128, 256), 0)
    lane = iota((128, 256), 1)
    hit = (row % 64 == (lane % 128) // 2) & (row // 64 == lane // 128)
    fine = pick(jnp.concatenate(parts, axis=0), jnp.where(hit, F32(1.0), zero))
    for q in range(3):
        for h in range(2):
            part = fine[16 * q : 16 * q + 16, 128 * h : 128 * h + 128]
            f1[2 * q + h, pl.ds(0, 16, stride=2), :] = part
            f1[2 * q + h, pl.ds(1, 16, stride=2), :] = part
    for x in range(12):
        p1a[x] = p1[x] + f1[x // 2]
    s1 = (wx1, wy1, wz1, wl1, rd1, ce1, ge1)
    sweep(p1a, p1b, s1, 1, 11, 10)
    sweep(p1b, p1a, s1, 2, 10, 8)

    wide = jnp.where(iota((128, 256), 0) == iota((128, 256), 1) // 2, F32(1.0), zero)
    fine = pick(jnp.concatenate([p1a[2 + x, 6:26, :] for x in range(8)], axis=0), wide)
    for x in range(8):
        for h in range(2):
            part = fine[20 * x : 20 * x + 20, 128 * h : 128 * h + 128]
            f0[x, h, pl.ds(0, 20, stride=2), :] = part
            f0[x, h, pl.ds(1, 20, stride=2), :] = part
    for x in range(1, 15):
        for h in range(2):
            cut = pl.ds(128 * h, 128)
            p0a[x, :, cut] = p0[x, :, cut] + f0[x // 2, h]
    s0 = (wx0, wy0, wz0, wl0, rd0, ce0, ge0)
    sweep(p0a, p0b, s0, 2, 14, 12)
    sweep(p0b, p0a, s0, 3, 13, 10)
    for x in range(8):
        own[x] = p0a[4 + x, 4:36, :]
    copies = [pltpu.make_async_copy(own, pressure, sems.at[0])]
    copies[0].start()
    for x, here, res in residual_rows(p0a, s0, 4, 12):
        res0[x - 4] = res[4:36, :]
        if x % 4 == 3:
            cut = pl.ds(x - 7, 4)
            copies.append(pltpu.make_async_copy(res0.at[cut], residual.at[cut], sems.at[x // 4]))
            copies[-1].start()
    for copy in copies:
        copy.wait()


def call(kernel, name, outs, scratch, limit, *args, anywhere=(), to_hbm=False):
    vmem = pl.BlockSpec(memory_space=pltpu.VMEM)
    hbm = pl.BlockSpec(memory_space=pltpu.HBM)
    specs = [vmem for _ in args]
    for k in anywhere:
        specs[k] = hbm
    return pl.pallas_call(
        kernel,
        name=name,
        out_shape=[jax.ShapeDtypeStruct(s, F32) for s in outs],
        in_specs=specs,
        out_specs=[hbm if to_hbm else vmem for _ in outs],
        scratch_shapes=[pltpu.VMEM(s, F32) if isinstance(s, tuple) else s for s in scratch],
        compiler_params=pltpu.CompilerParams(vmem_limit_bytes=limit * MIB),
    )(*args)


B0 = (8, 32, 256)
E0 = (16, 40, 256)
E1 = (12, 32, 128)
E2 = (8, 24, 128)


def per_device(source, material, flags):
    source, material, flags = (
        pltpu.with_memory_space_constraint(a, pltpu.HBM) for a in (source, material, flags)
    )
    left, right, b0, c0, g0 = call(
        k_load0, "load0", [(STRIPS, 8, 128)] * 2 + [B0] * 3,
        [pltpu.VMEM(B0, jnp.int32), pltpu.VMEM(B0, jnp.int32), pltpu.SemaphoreType.DMA((3,))],
        4, material, flags, source, anywhere=(0, 1, 2),
    )
    left0, right0 = exchange(left, right, "gy")
    low, high = call(k_edge0, "edge0", [(9, 32, 256)] * 2, [], 4, b0, c0, g0)
    below0, above0 = exchange(low, high, "gx")
    low, high = call(k_corner0, "corner0", [(CORNERS, 8, 128)] * 2, [], 4, left0, right0)
    under0, over0 = exchange(low, high, "gx")
    b1, c1, bc2 = call(
        k_coefs, "coefs", [(4, 24, 128), (4, 24, 128), (2, 8, 128)],
        [(4, 2, 48, 128), (2, 16, 128)], 4, b0, c0, left0, right0,
    )
    own0 = (b0, c0, g0, below0, above0, left0, right0, under0, over0)
    v0, g1, low, high = call(
        k_descend0, "descend0",
        [(8, 40, 256), (4, 24, 128), (10, 24, 128), (10, 24, 128)],
        [(16, 56, 256)] * 10 + [(4, 2, 48, 128)], 16, *own0, b1, c1,
    )
    below, above = exchange(low, high, "gx")
    v1, pay, be1, ce1, ge1 = call(
        k_descend1, "descend1",
        [(4, 16, 128), (8, 3, 8, 128)] + [E1] * 3,
        [E1] * 7 + [(2, 16, 128)], 4,
        g1, b1, c1, bc2, below, above,
    )
    gathered = lax.all_to_all(pay, "gx", 0, 0)
    low, high = call(k_pack_v, "pack_v", [(38, 8, 128)] * 2, [], 4, v0, v1)
    below, above = exchange(low, high, "gx")
    low, high = call(
        k_pack_y2, "pack_y2", [(30, 8, 128)] * 2, [], 4, v1, below, above, gathered
    )
    left1, right1 = exchange(low, high, "gy")
    v2, own3, *s2 = call(
        k_descend2, "descend2", [E2, (6, 8, 128)] + [E2] * 6, [E2, (384, 128)], 4,
        gathered, left1, right1,
    )
    r0, r1 = swap_chips(own3, "gy", 0), swap_chips(own3, "gy", 1)
    p0, ce0, ge0, wx0, wy0, wz0, wl0, rd0, p1, *w1 = call(
        k_prepare, "prepare", [E0] * 8 + [E1] * 6, [E0, E0, E1], 8,
        *own0, be1, ce1, ge1, v0, v1, below, above, left1, right1,
    )
    pressure, residual = call(
        k_ascend, "ascend", [B0] * 2,
        [(18, 8, 128), (128, 128), E2, E1, E1, E0, E0, (6, 32, 128), (8, 2, 40, 128),
         B0, B0, pltpu.SemaphoreType.DMA((3,))],
        8, own3, r0, r1, v2, *s2,
        p0, ce0, ge0, wx0, wy0, wz0, wl0, rd0, p1, ce1, ge1, *w1, to_hbm=True,
    )
    return pressure, residual


def solution(mesh):
    spec = P("gx", "gy", None)
    return jax.shard_map(
        per_device,
        mesh=mesh,
        in_specs=(spec, spec, spec),
        out_specs=(spec, spec),
        check_vma=False,
    )
```

```python
import jax
import jax.numpy as jnp
from jax import lax
from jax.experimental import pallas as pl
from jax.experimental.pallas import tpu as pltpu
from jax.sharding import PartitionSpec as P

F32 = jnp.float32
BF16 = jnp.bfloat16
OMEGA = 0.8
SHIFT = 0.001
ROBIN = 2.0
INVERSE_SOLID = 1.0 / 3.0
INVERSE_DENSE = 0.125
MIB = 1 << 20


def shift(block, axis, step):
    count = lax.axis_size(axis)
    return lax.ppermute(block, axis, [(i, (i + step) % count) for i in range(count)])


def exchange(low, high, axis):
    return shift(high, axis, 1), shift(low, axis, -1)


def swap_chips(block, axis, parity):
    count = lax.axis_size(axis)
    pairs = [(i, i + 2) for i in range(count - 2) if (i // 2) % 2 == parity]
    if parity == 1:
        pairs = [(0, 1)] + pairs + [(count - 2, count - 1)]
    return lax.ppermute(block, axis, pairs + [(b, a) for a, b in pairs])


def iota(shape, dim):
    return lax.broadcasted_iota(jnp.int32, shape, dim)


def pick(a, w):
    count = a.shape[0]
    a1 = a.astype(BF16).astype(F32)
    a2 = (a - a1).astype(BF16).astype(F32)
    parts = [a1, a2, (a - a1) - a2]
    if 3 * count % 16:
        parts.append(jnp.zeros((16 - 3 * count % 16, a.shape[1]), F32))
    stacked = jnp.concatenate(parts, axis=0).astype(BF16)
    out = jnp.dot(stacked, w.astype(BF16), preferred_element_type=F32)
    return out[:count] + out[count : 2 * count] + out[2 * count : 3 * count]


def inverse_density(material):
    return jnp.where(
        material == 0, F32(1.0), jnp.where(material == 1, F32(INVERSE_SOLID), F32(INVERSE_DENSE))
    )


def reaction_of(flags):
    return F32(SHIFT) + F32(ROBIN) * flags.astype(F32)


def harmonic(a, b):
    return (2.0 * a * b) * (1.0 / jnp.maximum(a + b, F32(1e-30)))


def step_of(d):
    return jnp.where(d > 0, F32(OMEGA) / jnp.where(d > 0, d, F32(1.0)), F32(0.0))


def fold_level0(tmp):
    parts = []
    for h in range(2):
        parts.append(
            jnp.concatenate(
                [
                    tmp[x, h, pl.ds(0, 24, stride=2), :] + tmp[x, h, pl.ds(1, 24, stride=2), :]
                    for x in range(4)
                ],
                axis=0,
            )
        )
    w = jnp.where(iota((256, 128), 0) // 2 == iota((256, 128), 1), F32(0.125), F32(0.0))
    return pick(jnp.concatenate(parts, axis=1), w).reshape(4, 24, 128)


def fold_level1(tmp):
    parts = [
        tmp[x, pl.ds(0, 8, stride=2), :] + tmp[x, pl.ds(1, 8, stride=2), :] for x in range(2)
    ]
    row = iota((256, 128), 0)
    lane = iota((256, 128), 1)
    hit = ((row % 128) // 2 == lane % 64) & (row // 128 == lane // 64)
    return pick(jnp.concatenate(parts, axis=1), jnp.where(hit, F32(0.125), F32(0.0)))


def fold_level2(tiles):
    count = tiles.shape[0] // 64
    hit = (iota((128, 128), 0) % 64) // 2 == iota((128, 128), 1) % 32
    t = pick(tiles, jnp.where(hit, F32(0.125), F32(0.0))).reshape(count, 8, 8, 128)
    keep = iota(t.shape, 2) // 2 == iota(t.shape, 3) // 32
    t = jnp.sum(jnp.where(keep, t, F32(0.0)), axis=2)
    return [t[k] for k in range(count)]


def next_y(v):
    return pltpu.roll(v, v.shape[0] - 1, 0)


def last_y(v):
    return pltpu.roll(v, 1, 0)


def next_z(v):
    return pltpu.roll(v, v.shape[1] - 1, 1)


def last_z(v):
    return pltpu.roll(v, 1, 1)


def weights(b, s, v, scaling, low, high, unroll):
    wx, wy, wz, wl, rd, c, g = s
    scale = F32(scaling)
    prev = scale * harmonic(b[low - 1], b[low])
    wx[low - 1] = prev
    shape = prev.shape
    inside = iota(shape, 1) < shape[1] - 1

    def body(x, prev):
        here = b[x]
        cur = scale * harmonic(here, b[x + 1])
        wx[x] = cur
        fy = scale * harmonic(here, next_y(here))
        wy[x] = fy
        fz = jnp.where(inside, scale * harmonic(here, next_z(here)), F32(0.0))
        wz[x] = fz
        fl = last_z(fz)
        wl[x] = fl
        r = step_of((prev + cur) + (fy + last_y(fy)) + (fz + fl) + c[x])
        rd[x] = r
        v[x] = r * g[x]
        return cur

    lax.fori_loop(low, high, body, prev, unroll=unroll)


def row_residual(v, s, x, prev):
    wx, wy, wz, wl, rd, c, g = s
    here = v[x]
    cur = wx[x] * (here - v[x + 1])
    fy = wy[x] * (here - next_y(here))
    fz = wz[x] * (here - next_z(here)) + wl[x] * (here - last_z(here))
    flux = (cur - prev) + (fy - last_y(fy)) + fz
    return here, g[x] - (flux + c[x] * here), cur


def sweep(src, dst, s, low, high, unroll):
    rd = s[4]

    def body(x, prev):
        here, res, cur = row_residual(src, s, x, prev)
        dst[x] = here + rd[x] * res
        return cur

    first = s[0][low - 1] * (src[low - 1] - src[low])
    lax.fori_loop(low, high, body, first, unroll=unroll)


def residual_rows(v, s, low, high):
    prev = s[0][low - 1] * (v[low - 1] - v[low])
    for x in range(low, high):
        here, res, prev = row_residual(v, s, x, prev)
        yield x, here, res


def place(axis):
    return lax.axis_index(axis)


def gate(inside, value):
    return jnp.where(inside, value, F32(0.0))


STRIPS = 54


def k_load0(m, f, g, left, right, b0, c0, g0, mv, fv, sems):
    copies = [
        pltpu.make_async_copy(m, mv, sems.at[0]),
        pltpu.make_async_copy(f, fv, sems.at[1]),
        pltpu.make_async_copy(g, g0, sems.at[2]),
    ]
    for copy in copies:
        copy.start()

    def strips(a, own):
        for x in range(8):
            for out, at, ninth, tenth, inside in (
                (left, 0, 8, 9, place("gy") > 0),
                (right, 24, 23, 22, place("gy") < lax.axis_size("gy") - 1),
            ):
                near = own[x, at : at + 8, :]
                far = own[x, ninth : ninth + 1, :]
                if a == 0:
                    near, far = gate(inside, near), gate(inside, far)
                if a == 1:
                    far = far + harmonic(b0[x, ninth : ninth + 1, :], b0[x, tenth : tenth + 1, :])
                for h in range(2):
                    cut = slice(128 * h, 128 * h + 128)
                    out[16 * a + 2 * x + h] = near[:, cut]
                    out[48 + 2 * a + h, x : x + 1, :] = far[:, cut]

    copies[0].wait()
    for x in range(8):
        b0[x] = inverse_density(mv[x])
    strips(0, b0)
    copies[1].wait()
    for x in range(8):
        c0[x] = reaction_of(fv[x])
    strips(1, c0)
    copies[2].wait()
    strips(2, g0)


def k_edge0(b0, c0, g0, low, high):
    for k in range(3):
        low[k] = gate(place("gx") > 0, b0[k])
        high[k] = gate(place("gx") < lax.axis_size("gx") - 1, b0[5 + k])
        low[3 + k] = c0[k] + harmonic(b0[2], b0[3]) if k == 2 else c0[k]
        high[3 + k] = c0[5 + k] + harmonic(b0[5], b0[4]) if k == 0 else c0[5 + k]
        low[6 + k] = g0[k]
        high[6 + k] = g0[5 + k]


def split_pair(tmp, k, value):
    for h in range(2):
        tmp[k, h] = value[:, 128 * h : 128 * h + 128]


def k_coefs(b0, c0, left, right, b1, c1, bc2, tmp0, tmp1):
    for k, (src, out) in enumerate(((b0, b1), (c0, c1))):
        for x in range(4):
            pair = src[2 * x] + src[2 * x + 1]
            for h in range(2):
                t = 16 * k + 4 * x + h
                tmp0[x, h, 0:8, :] = left[t] + left[t + 2]
                tmp0[x, h, 8:40, :] = pair[:, 128 * h : 128 * h + 128]
                tmp0[x, h, 40:48, :] = right[t] + right[t + 2]
        t = fold_level0(tmp0)
        for x in range(4):
            out[x] = t[x]
        for x in range(2):
            tmp1[x] = (t[2 * x] + t[2 * x + 1])[4:20, :]
        bc2[k] = fold_level1(tmp1)


CORNERS = 37


def k_corner0(left, right, low, high):
    for out, first, edge, third, fourth, inside in (
        (low, 0, 0, 2, 3, place("gx") > 0),
        (high, 5, 7, 5, 4, place("gx") < lax.axis_size("gx") - 1),
    ):
        out[36] = jnp.zeros((8, 128), F32)
        for side, strips in enumerate((left, right)):
            for h in range(2):
                for k in range(3):
                    x = first + k
                    at = 18 * side + 2 * k + h
                    out[at] = gate(inside, strips[2 * x + h])
                    c = strips[16 + 2 * x + h]
                    if x == third:
                        c = c + harmonic(strips[2 * x + h], strips[2 * fourth + h])
                    out[at + 6] = c
                    out[at + 12] = strips[32 + 2 * x + h]
                at = 2 * side + h
                out[36, at : at + 1, :] = gate(inside, strips[48 + h, edge : edge + 1, :])


def blocks0(b0, c0, g0, below, above, left, right, under, over):
    for a, own in enumerate((b0, c0, g0)):
        for x in range(-3, 11):
            if 0 <= x < 8:
                tiles = [[s[16 * a + 2 * x + h] for h in range(2)] for s in (left, right)]
                ninth = [[s[48 + 2 * a + h, x : x + 1, :] for h in range(2)] for s in (left, right)]
                yield a, x, own[x], tiles, ninth
            else:
                k = x + 3 if x < 0 else x - 8
                main, far = (below, under) if x < 0 else (above, over)
                tiles = [[far[18 * side + 6 * a + 2 * k + h] for h in range(2)] for side in range(2)]
                ninth = None
                if a == 0 and x in (-1, 8):
                    ninth = [
                        [far[36, 2 * side + h : 2 * side + h + 1, :] for h in range(2)]
                        for side in range(2)
                    ]
                yield a, x, main[3 * a + k], tiles, ninth


def assemble_deep(args, exts):
    zero = jnp.zeros((4, 256), F32)
    for a, x, own, tiles, ninth in blocks0(*args):
        ext = exts[a]
        r = 4 + x
        ext[r, 0:4, :] = zero
        ext[r, 12:44, :] = own
        ext[r, 52:56, :] = zero
        for h in range(2):
            cut = pl.ds(128 * h, 128)
            ext[r, 4:12, cut] = tiles[0][h]
            ext[r, 44:52, cut] = tiles[1][h]
            if ninth is not None:
                ext[r, 3:4, cut] = ninth[0][h]
                ext[r, 52:53, cut] = ninth[1][h]
    for x in (0, 15):
        exts[0][x] = jnp.zeros(exts[0].shape[1:], F32)


def assemble0(args, exts):
    for a, x, own, tiles, _ in blocks0(*args):
        ext = exts[a]
        r = 4 + x
        ext[r, 4:36, :] = own
        for h in range(2):
            cut = pl.ds(128 * h, 128)
            ext[r, 0:4, cut] = tiles[0][h][4:8, :]
            ext[r, 36:40, cut] = tiles[1][h][0:4, :]
    for x in (0, 15):
        exts[0][x] = jnp.zeros(exts[0].shape[1:], F32)


def k_descend0(
    b0, c0, g0, below, above, left, right, under, over, b1, c1,
    v0, g1, low, high,
    be, ce, ge, wx, wy, wz, wl, rd, va, vb, tmp,
):
    assemble_deep((b0, c0, g0, below, above, left, right, under, over), (be, ce, ge))
    s = (wx, wy, wz, wl, rd, ce, ge)
    weights(be, s, va, 1.0, 1, 15, 7)
    sweep(va, vb, s, 2, 14, 12)
    sweep(vb, va, s, 3, 13, 10)
    for x in range(8):
        v0[x] = va[4 + x, 8:48, :]
    kept = None
    for x, here, res in residual_rows(va, s, 4, 12):
        if x % 2 == 0:
            kept = res
        else:
            split_pair(tmp, (x - 4) // 2, (kept + res)[4:52, :])
    t = fold_level0(tmp)
    for x in range(4):
        g1[x] = t[x]
        low[x] = gate(place("gx") > 0, b1[x])
        high[x] = gate(place("gx") < lax.axis_size("gx") - 1, b1[x])
    for k in range(3):
        low[4 + k] = c1[k]
        high[4 + k] = c1[1 + k]
        low[7 + k] = t[k]
        high[7 + k] = t[1 + k]


def k_descend1(
    g1, b1, c1, bc2, below, above,
    v1, pay, be, ce, ge,
    wx, wy, wz, wl, rd, va, vb, tmp,
):
    zeros = jnp.zeros((4, 128), F32)
    for ext, own, base, reach in ((be, b1, 0, 4), (ce, c1, 4, 3), (ge, g1, 7, 3)):
        for x in range(-reach, 4 + reach):
            if x < 0:
                val = below[base + x + reach]
            elif x < 4:
                val = own[x]
            else:
                val = above[base + x - 4]
            ext[4 + x, 0:4, :] = zeros
            ext[4 + x, 4:28, :] = val
            ext[4 + x, 28:32, :] = zeros

    s = (wx, wy, wz, wl, rd, ce, ge)
    weights(be, s, va, 0.25, 1, 11, 10)
    sweep(va, vb, s, 2, 10, 8)
    sweep(vb, va, s, 3, 9, 6)
    for x in range(4):
        v1[x] = va[4 + x, 8:24, :]
    kept = None
    for x, here, res in residual_rows(va, s, 4, 8):
        if x % 2 == 0:
            kept = res[8:24, :]
        else:
            tmp[(x - 4) // 2] = kept + res[8:24, :]
    g2 = fold_level1(tmp)
    for k in range(8):
        pay[k, 0] = g2
        pay[k, 1] = bc2[0]
        pay[k, 2] = bc2[1]


def k_pack_v(v0, v1, low, high):
    for out, first, edge, second in ((low, 0, 0, 1), (high, 5, 7, 6)):
        for k in range(3):
            for q in range(4):
                for h in range(2):
                    out[8 * k + 2 * q + h] = v0[
                        first + k, 4 + 8 * q : 12 + 8 * q, 128 * h : 128 * h + 128
                    ]
        out[25] = jnp.zeros((8, 128), F32)
        for h in range(2):
            cut = slice(128 * h, 128 * h + 128)
            for side, at in ((0, 2), (1, 36)):
                t = 4 * side + 2 * h
                out[24, t : t + 2, :] = v0[edge, at : at + 2, cut]
                near = 3 if side == 0 else 36
                t = 2 * side + h
                out[25, t : t + 1, :] = v0[second, near : near + 1, cut]
        for k in range(4):
            for q in range(2):
                out[26 + 2 * k + q] = v1[k, 8 * q : 8 * q + 8, :]


def k_pack_y2(v1, below, above, gathered, low, high):
    for out, q, inside in (
        (low, 0, place("gy") > 0), (high, 1, place("gy") < lax.axis_size("gy") - 1)
    ):
        for k in range(3):
            for i in range(8):
                val = gathered[i, k]
                out[8 * k + i] = gate(inside, val) if k == 1 else val
        cut = pl.ds(4 * q, 4)
        for t, x in enumerate(range(-4, 8)):
            if x < 0:
                val = below[26 + 2 * (x + 4) + q, cut, :]
            elif x < 4:
                val = v1[x, pl.ds(12 * q, 4), :]
            else:
                val = above[26 + 2 * (x - 4) + q, cut, :]
            half = 4 * (t % 2)
            out[24 + t // 2, half : half + 4, :] = val


def upper(shape):
    return iota(shape, len(shape) - 1) >= 64


def pair_next(v):
    mask = upper(v[0].shape)
    out = []
    for i in range(8):
        after = v[i + 1] if i < 7 else jnp.zeros_like(v[0])
        out.append(pltpu.roll(jnp.where(mask, v[i], after), 64, 1))
    return out


def pair_last(f):
    mask = upper(f[0].shape)
    out = []
    for i in range(8):
        before = f[i - 1] if i > 0 else jnp.zeros_like(f[0])
        out.append(pltpu.roll(jnp.where(mask, before, f[i]), 64, 1))
    return out


def weights2(b, c, scaling):
    scale = F32(scaling)
    inside = iota(b[0].shape, 1) % 64 < 63
    wx = [scale * harmonic(p, q) for p, q in zip(b, pair_next(b))]
    wy = [scale * harmonic(p, next_y(p)) for p in b]
    wz = [jnp.where(inside, scale * harmonic(p, next_z(p)), F32(0.0)) for p in b]
    back = pair_last(wx)
    rd = []
    for i in range(8):
        d = (wx[i] + back[i]) + (wy[i] + last_y(wy[i])) + (wz[i] + last_z(wz[i])) + c[i]
        rd.append(step_of(d))
    return wx, wy, wz, rd


def residual2(v, g, c, wx, wy, wz):
    fx = [w * (p - q) for w, p, q in zip(wx, v, pair_next(v))]
    back = pair_last(fx)
    out = []
    for i in range(8):
        fy = wy[i] * (v[i] - next_y(v[i]))
        fz = wz[i] * (v[i] - next_z(v[i]))
        flux = (fx[i] - back[i]) + (fy - last_y(fy)) + (fz - last_z(fz))
        out.append(g[i] - (flux + c[i] * v[i]))
    return out


def k_descend2(gathered, left, right, v2, pay, wx2, wy2, wz2, rd2, ce2, ge2, be2, tmp):
    for k, ext in enumerate((ge2, be2, ce2)):
        for i in range(8):
            ext[i, 0:8, :] = left[8 * k + i]
            ext[i, 8:16, :] = gathered[i, k]
            ext[i, 16:24, :] = right[8 * k + i]
    b = [be2[i] for i in range(8)]
    c = [ce2[i] for i in range(8)]
    g = [ge2[i] for i in range(8)]
    wx, wy, wz, rd = weights2(b, c, 0.0625)
    for i in range(8):
        wx2[i] = wx[i]
        wy2[i] = wy[i]
        wz2[i] = wz[i]
        rd2[i] = rd[i]
    v = [p * q for p, q in zip(rd, g)]
    for _ in range(2):
        r = residual2(v, g, c, wx, wy, wz)
        v = [p + q * s for p, q, s in zip(v, rd, r)]
    r = residual2(v, g, c, wx, wy, wz)
    for i in range(8):
        v2[i] = v[i]
    for k, src in enumerate((r, b, c)):
        for t in range(2):
            for i in range(8):
                at = 64 * (2 * k + t) + 8 * i
                tmp[at : at + 8, :] = src[i][4 + 8 * t : 12 + 8 * t, :]
    for t, tile in enumerate(fold_level2(tmp[...])):
        pay[t] = tile


TILES = 6


def block_next(v):
    head = iota(v[0].shape, 1) < 32
    out = []
    for t in range(TILES):
        after = v[t + 1] if t < TILES - 1 else jnp.zeros_like(v[0])
        out.append(pltpu.roll(jnp.where(head, after, v[t]), 96, 1))
    return out


def block_last(f):
    tail = iota(f[0].shape, 1) >= 96
    out = []
    for t in range(TILES):
        before = f[t - 1] if t > 0 else jnp.zeros_like(f[0])
        out.append(pltpu.roll(jnp.where(tail, before, f[t]), 32, 1))
    return out


def solve3(g, b, c):
    scale = F32(0.015625)
    shape = g[0].shape
    inside_x = iota(shape, 0) < 7
    inside_z = iota(shape, 1) % 32 < 31
    zero = F32(0.0)
    wx = [jnp.where(inside_x, scale * harmonic(p, next_y(p)), zero) for p in b]
    wy = [scale * harmonic(p, q) for p, q in zip(b, block_next(b))]
    wz = [jnp.where(inside_z, scale * harmonic(p, next_z(p)), zero) for p in b]
    xl = [last_y(p) for p in wx]
    yl = block_last(wy)
    zl = [last_z(p) for p in wz]
    keep, add, sides = [], [], []
    for t in range(TILES):
        faces = (wx[t], xl[t], wy[t], yl[t], wz[t], zl[t])
        d = (wx[t] + xl[t]) + (wy[t] + yl[t]) + (wz[t] + zl[t]) + c[t]
        rd = step_of(d)
        keep.append(1.0 - rd * d)
        add.append(rd * g[t])
        sides.append([rd * w for w in faces])
    e = add
    for first in (0, 0, 1, 1, 1, 1, 2):
        up = block_next(e)
        down = block_last(e)
        new = list(e)
        for t in range(first, TILES - first):
            h = e[t]
            w = sides[t]
            x = w[0] * next_y(h) + w[1] * last_y(h)
            y = w[2] * up[t] + w[3] * down[t]
            z = w[4] * next_z(h) + w[5] * last_z(h)
            new[t] = (add[t] + keep[t] * h) + (x + y) + z
        e = new
    return e


def k_prepare(
    b0, c0, g0, below0, above0, left0, right0, under0, over0, be1, ce1, ge1,
    v0, v1, below, above, left1, right1,
    p0, ce, ge, wx, wy, wz, wl, rd, p1, wx1, wy1, wz1, wl1, rd1,
    be, va, va1,
):
    assemble0((b0, c0, g0, below0, above0, left0, right0, under0, over0), (be, ce, ge))
    weights(be, (wx, wy, wz, wl, rd, ce, ge), va, 1.0, 2, 14, 6)
    weights(be1, (wx1, wy1, wz1, wl1, rd1, ce1, ge1), va1, 0.25, 1, 11, 10)
    zero = jnp.zeros((8, 128), F32)
    for t, x in enumerate(range(-4, 8)):
        p1[t, 0:8, :] = zero
        p1[t, 24:32, :] = zero
        if 0 <= x < 4:
            p1[t, 8:24, :] = v1[x]
        else:
            src, k = (below, x + 4) if x < 0 else (above, x - 4)
            for q in range(2):
                p1[t, 8 + 8 * q : 16 + 8 * q, :] = src[26 + 2 * k + q]
        half = 4 * (t % 2)
        p1[t, 4:8, :] = left1[24 + t // 2, half : half + 4, :]
        p1[t, 24:28, :] = right1[24 + t // 2, half : half + 4, :]
    for x in range(-3, 11):
        if 0 <= x < 8:
            p0[4 + x] = v0[x]
        else:
            src, k = (below, x + 3) if x < 0 else (above, x - 8)
            p0[4 + x, 0:4, :] = jnp.zeros((4, 256), F32)
            p0[4 + x, 36:40, :] = jnp.zeros((4, 256), F32)
            for h in range(2):
                cut = slice(128 * h, 128 * h + 128)
                for q in range(4):
                    p0[4 + x, 4 + 8 * q : 12 + 8 * q, cut] = src[8 * k + 2 * q + h]
                if x in (-1, 8):
                    p0[4 + x, 2:4, cut] = src[24, 2 * h : 2 * h + 2, :]
                    p0[4 + x, 36:38, cut] = src[24, 4 + 2 * h : 6 + 2 * h, :]
                if x in (-2, 9):
                    p0[4 + x, 3:4, cut] = src[25, h : h + 1, :]
                    p0[4 + x, 36:37, cut] = src[25, 2 + h : 3 + h, :]


def k_ascend(
    own3, r0, r1, v2, wx2, wy2, wz2, rd2, ce2, ge2,
    p0, ce0, ge0, wx0, wy0, wz0, wl0, rd0,
    p1, ce1, ge1, wx1, wy1, wz1, wl1, rd1,
    pressure, residual,
    all3, m2, p2, p1a, p1b, p0a, p0b, f1, f0, own, res0, sems,
):
    ix = place("gx")
    iy = place("gy")
    count = lax.axis_size("gy")
    even_chip = lax.rem(iy // 2, 2) == 0
    zero = F32(0.0)

    for k in range(3):
        first = [jnp.where(even_chip, r1[2 * k + t], r0[2 * k + t]) for t in range(2)]
        last = [jnp.where(even_chip, r0[2 * k + t], r1[2 * k + t]) for t in range(2)]
        at = TILES * k
        all3[at] = gate(iy >= 2, first[0])
        all3[at + 1] = jnp.where(iy >= 2, first[1], gate(iy == 1, first[0]))
        all3[at + 2] = own3[2 * k]
        all3[at + 3] = own3[2 * k + 1]
        all3[at + 4] = jnp.where(iy < count - 2, last[0], gate(iy == count - 2, last[1]))
        all3[at + 5] = gate(iy < count - 2, last[1])
    e = solve3(*[[all3[TILES * k + t] for t in range(TILES)] for k in range(3)])

    group = iota((8, 128), 1) // 32 == iota((8, 128), 0) // 2
    for t in range(2):
        for i in range(8):
            row = jnp.broadcast_to(e[2 + t][i : i + 1, :], (8, 128))
            m2[16 * i + 8 * t : 16 * i + 8 * t + 8, :] = jnp.where(group, row, zero)
    spread = jnp.where(
        iota((128, 128), 0) % 32 == (iota((128, 128), 1) % 64) // 2, F32(1.0), zero
    )
    fine = pick(m2[...], spread)
    for i in range(8):
        p2[i] = v2[i]
        p2[i, 4:20, :] += fine[16 * i : 16 * i + 16, :]
    v = [p2[i] for i in range(8)]
    g = [ge2[i] for i in range(8)]
    c = [ce2[i] for i in range(8)]
    wx = [wx2[i] for i in range(8)]
    wy = [wy2[i] for i in range(8)]
    wz = [wz2[i] for i in range(8)]
    for _ in range(2):
        r = residual2(v, g, c, wx, wy, wz)
        v = [v[i] + rd2[i] * r[i] for i in range(8)]
    for i in range(8):
        p2[i] = v[i]

    parts = []
    for q in range(3):
        at = ix + (q - 1)
        inside = jnp.logical_and(at >= 0, at < lax.axis_size("gx"))
        parts.append(jnp.where(inside, p2[jnp.clip(at, 0, 7), 4:20, :], zero))
    row = iota((128, 256), 0)
    lane = iota((128, 256), 1)
    hit = (row % 64 == (lane % 128) // 2) & (row // 64 == lane // 128)
    fine = pick(jnp.concatenate(parts, axis=0), jnp.where(hit, F32(1.0), zero))
    for q in range(3):
        for h in range(2):
            part = fine[16 * q : 16 * q + 16, 128 * h : 128 * h + 128]
            f1[2 * q + h, pl.ds(0, 16, stride=2), :] = part
            f1[2 * q + h, pl.ds(1, 16, stride=2), :] = part
    for x in range(12):
        p1a[x] = p1[x] + f1[x // 2]
    s1 = (wx1, wy1, wz1, wl1, rd1, ce1, ge1)
    sweep(p1a, p1b, s1, 1, 11, 10)
    sweep(p1b, p1a, s1, 2, 10, 8)

    wide = jnp.where(iota((128, 256), 0) == iota((128, 256), 1) // 2, F32(1.0), zero)
    fine = pick(jnp.concatenate([p1a[2 + x, 6:26, :] for x in range(8)], axis=0), wide)
    for x in range(8):
        for h in range(2):
            part = fine[20 * x : 20 * x + 20, 128 * h : 128 * h + 128]
            f0[x, h, pl.ds(0, 20, stride=2), :] = part
            f0[x, h, pl.ds(1, 20, stride=2), :] = part
    for x in range(1, 15):
        for h in range(2):
            cut = pl.ds(128 * h, 128)
            p0a[x, :, cut] = p0[x, :, cut] + f0[x // 2, h]
    s0 = (wx0, wy0, wz0, wl0, rd0, ce0, ge0)
    sweep(p0a, p0b, s0, 2, 14, 12)
    sweep(p0b, p0a, s0, 3, 13, 10)
    for x in range(8):
        own[x] = p0a[4 + x, 4:36, :]
    copies = [pltpu.make_async_copy(own, pressure, sems.at[0])]
    copies[0].start()
    for x, here, res in residual_rows(p0a, s0, 4, 12):
        res0[x - 4] = res[4:36, :]
        if x % 4 == 3:
            cut = pl.ds(x - 7, 4)
            copies.append(pltpu.make_async_copy(res0.at[cut], residual.at[cut], sems.at[x // 4]))
            copies[-1].start()
    for copy in copies:
        copy.wait()


def call(kernel, name, outs, scratch, limit, *args, anywhere=(), to_hbm=False):
    vmem = pl.BlockSpec(memory_space=pltpu.VMEM)
    hbm = pl.BlockSpec(memory_space=pltpu.HBM)
    specs = [vmem for _ in args]
    for k in anywhere:
        specs[k] = hbm
    return pl.pallas_call(
        kernel,
        name=name,
        out_shape=[jax.ShapeDtypeStruct(s, F32) for s in outs],
        in_specs=specs,
        out_specs=[hbm if to_hbm else vmem for _ in outs],
        scratch_shapes=[pltpu.VMEM(s, F32) if isinstance(s, tuple) else s for s in scratch],
        compiler_params=pltpu.CompilerParams(vmem_limit_bytes=limit * MIB),
    )(*args)


B0 = (8, 32, 256)
E0 = (16, 40, 256)
E1 = (12, 32, 128)
E2 = (8, 24, 128)


def per_device(source, material, flags):
    source, material, flags = (
        pltpu.with_memory_space_constraint(a, pltpu.HBM) for a in (source, material, flags)
    )
    left, right, b0, c0, g0 = call(
        k_load0, "load0", [(STRIPS, 8, 128)] * 2 + [B0] * 3,
        [pltpu.VMEM(B0, jnp.int32), pltpu.VMEM(B0, jnp.int32), pltpu.SemaphoreType.DMA((3,))],
        4, material, flags, source, anywhere=(0, 1, 2),
    )
    left0, right0 = exchange(left, right, "gy")
    low, high = call(k_edge0, "edge0", [(9, 32, 256)] * 2, [], 4, b0, c0, g0)
    below0, above0 = exchange(low, high, "gx")
    low, high = call(k_corner0, "corner0", [(CORNERS, 8, 128)] * 2, [], 4, left0, right0)
    under0, over0 = exchange(low, high, "gx")
    b1, c1, bc2 = call(
        k_coefs, "coefs", [(4, 24, 128), (4, 24, 128), (2, 8, 128)],
        [(4, 2, 48, 128), (2, 16, 128)], 4, b0, c0, left0, right0,
    )
    own0 = (b0, c0, g0, below0, above0, left0, right0, under0, over0)
    v0, g1, low, high = call(
        k_descend0, "descend0",
        [(8, 40, 256), (4, 24, 128), (10, 24, 128), (10, 24, 128)],
        [(16, 56, 256)] * 10 + [(4, 2, 48, 128)], 16, *own0, b1, c1,
    )
    below, above = exchange(low, high, "gx")
    v1, pay, be1, ce1, ge1 = call(
        k_descend1, "descend1",
        [(4, 16, 128), (8, 3, 8, 128)] + [E1] * 3,
        [E1] * 7 + [(2, 16, 128)], 4,
        g1, b1, c1, bc2, below, above,
    )
    gathered = lax.all_to_all(pay, "gx", 0, 0)
    low, high = call(k_pack_v, "pack_v", [(34, 8, 128)] * 2, [], 4, v0, v1)
    below, above = exchange(low, high, "gx")
    low, high = call(
        k_pack_y2, "pack_y2", [(30, 8, 128)] * 2, [], 4, v1, below, above, gathered
    )
    left1, right1 = exchange(low, high, "gy")
    v2, own3, *s2 = call(
        k_descend2, "descend2", [E2, (6, 8, 128)] + [E2] * 6, [E2, (384, 128)], 4,
        gathered, left1, right1,
    )
    r0, r1 = swap_chips(own3, "gy", 0), swap_chips(own3, "gy", 1)
    p0, ce0, ge0, wx0, wy0, wz0, wl0, rd0, p1, *w1 = call(
        k_prepare, "prepare", [E0] * 8 + [E1] * 6, [E0, E0, E1], 8,
        *own0, be1, ce1, ge1, v0, v1, below, above, left1, right1,
    )
    pressure, residual = call(
        k_ascend, "ascend", [B0] * 2,
        [(18, 8, 128), (128, 128), E2, E1, E1, E0, E0, (6, 32, 128), (8, 2, 40, 128),
         B0, B0, pltpu.SemaphoreType.DMA((3,))],
        8, own3, r0, r1, v2, *s2,
        p0, ce0, ge0, wx0, wy0, wz0, wl0, rd0, p1, ce1, ge1, *w1, to_hbm=True,
    )
    return pressure, residual


def solution(mesh):
    spec = P("gx", "gy", None)
    return jax.shard_map(
        per_device,
        mesh=mesh,
        in_specs=(spec, spec, spec),
        out_specs=(spec, spec),
        check_vma=False,
    )
```

```python
import jax
import jax.numpy as jnp
from jax import lax
from jax.experimental import pallas as pl
from jax.experimental.pallas import tpu as pltpu
from jax.sharding import PartitionSpec as P

F32 = jnp.float32
BF16 = jnp.bfloat16
OMEGA = 0.8
SHIFT = 0.001
ROBIN = 2.0
INVERSE_SOLID = 1.0 / 3.0
INVERSE_DENSE = 0.125
MIB = 1 << 20


def shift(block, axis, step):
    count = lax.axis_size(axis)
    return lax.ppermute(block, axis, [(i, (i + step) % count) for i in range(count)])


def exchange(low, high, axis):
    return shift(high, axis, 1), shift(low, axis, -1)


def swap_chips(block, axis, parity):
    count = lax.axis_size(axis)
    pairs = [(i, i + 2) for i in range(count - 2) if (i // 2) % 2 == parity]
    if parity == 1:
        pairs = [(0, 1)] + pairs + [(count - 2, count - 1)]
    return lax.ppermute(block, axis, pairs + [(b, a) for a, b in pairs])


def iota(shape, dim):
    return lax.broadcasted_iota(jnp.int32, shape, dim)


def pick(a, w):
    count = a.shape[0]
    a1 = a.astype(BF16).astype(F32)
    a2 = (a - a1).astype(BF16).astype(F32)
    parts = [a1, a2, (a - a1) - a2]
    if 3 * count % 16:
        parts.append(jnp.zeros((16 - 3 * count % 16, a.shape[1]), F32))
    stacked = jnp.concatenate(parts, axis=0).astype(BF16)
    out = jnp.dot(stacked, w.astype(BF16), preferred_element_type=F32)
    return out[:count] + out[count : 2 * count] + out[2 * count : 3 * count]


def inverse_density(material):
    return jnp.where(
        material == 0, F32(1.0), jnp.where(material == 1, F32(INVERSE_SOLID), F32(INVERSE_DENSE))
    )


def reaction_of(flags):
    return F32(SHIFT) + F32(ROBIN) * flags.astype(F32)


def harmonic(a, b):
    return (2.0 * a * b) * (1.0 / jnp.maximum(a + b, F32(1e-30)))


def step_of(d):
    return jnp.where(d > 0, F32(OMEGA) / jnp.where(d > 0, d, F32(1.0)), F32(0.0))


def fold_level0(tmp):
    parts = []
    for h in range(2):
        parts.append(
            jnp.concatenate(
                [
                    tmp[x, h, pl.ds(0, 24, stride=2), :] + tmp[x, h, pl.ds(1, 24, stride=2), :]
                    for x in range(4)
                ],
                axis=0,
            )
        )
    w = jnp.where(iota((256, 128), 0) // 2 == iota((256, 128), 1), F32(0.125), F32(0.0))
    return pick(jnp.concatenate(parts, axis=1), w).reshape(4, 24, 128)


def fold_level1(tmp):
    parts = [
        tmp[x, pl.ds(0, 8, stride=2), :] + tmp[x, pl.ds(1, 8, stride=2), :] for x in range(2)
    ]
    row = iota((256, 128), 0)
    lane = iota((256, 128), 1)
    hit = ((row % 128) // 2 == lane % 64) & (row // 128 == lane // 64)
    return pick(jnp.concatenate(parts, axis=1), jnp.where(hit, F32(0.125), F32(0.0)))


def fold_level2(tiles):
    count = tiles.shape[0] // 64
    hit = (iota((128, 128), 0) % 64) // 2 == iota((128, 128), 1) % 32
    t = pick(tiles, jnp.where(hit, F32(0.125), F32(0.0))).reshape(count, 8, 8, 128)
    keep = iota(t.shape, 2) // 2 == iota(t.shape, 3) // 32
    t = jnp.sum(jnp.where(keep, t, F32(0.0)), axis=2)
    return [t[k] for k in range(count)]


def next_y(v):
    return pltpu.roll(v, v.shape[0] - 1, 0)


def last_y(v):
    return pltpu.roll(v, 1, 0)


def next_z(v):
    return pltpu.roll(v, v.shape[1] - 1, 1)


def last_z(v):
    return pltpu.roll(v, 1, 1)


def weights(b, s, v, scaling, low, high, unroll):
    wx, wy, wz, wl, rd, c, g = s
    scale = F32(scaling)
    prev = scale * harmonic(b[low - 1], b[low])
    wx[low - 1] = prev
    shape = prev.shape
    inside = iota(shape, 1) < shape[1] - 1

    def body(x, prev):
        here = b[x]
        cur = scale * harmonic(here, b[x + 1])
        wx[x] = cur
        fy = scale * harmonic(here, next_y(here))
        wy[x] = fy
        fz = jnp.where(inside, scale * harmonic(here, next_z(here)), F32(0.0))
        wz[x] = fz
        fl = last_z(fz)
        wl[x] = fl
        r = step_of((prev + cur) + (fy + last_y(fy)) + (fz + fl) + c[x])
        rd[x] = r
        v[x] = r * g[x]
        return cur

    lax.fori_loop(low, high, body, prev, unroll=unroll)


def row_residual(v, s, x, prev):
    wx, wy, wz, wl, rd, c, g = s
    here = v[x]
    cur = wx[x] * (here - v[x + 1])
    fy = wy[x] * (here - next_y(here))
    fz = wz[x] * (here - next_z(here)) + wl[x] * (here - last_z(here))
    flux = (cur - prev) + (fy - last_y(fy)) + fz
    return here, g[x] - (flux + c[x] * here), cur


def sweep(src, dst, s, low, high, unroll):
    rd = s[4]

    def body(x, prev):
        here, res, cur = row_residual(src, s, x, prev)
        dst[x] = here + rd[x] * res
        return cur

    first = s[0][low - 1] * (src[low - 1] - src[low])
    lax.fori_loop(low, high, body, first, unroll=unroll)


def residual_rows(v, s, low, high):
    prev = s[0][low - 1] * (v[low - 1] - v[low])
    for x in range(low, high):
        here, res, prev = row_residual(v, s, x, prev)
        yield x, here, res


def place(axis):
    return lax.axis_index(axis)


def gate(inside, value):
    return jnp.where(inside, value, F32(0.0))


STRIPS = 54


def k_load0(m, f, g, left, right, b0, c0, g0, mv, fv, sems):
    copies = [
        pltpu.make_async_copy(m, mv, sems.at[0]),
        pltpu.make_async_copy(f, fv, sems.at[1]),
        pltpu.make_async_copy(g, g0, sems.at[2]),
    ]
    for copy in copies:
        copy.start()

    def strips(a, own):
        for x in range(8):
            for out, at, ninth, tenth, inside in (
                (left, 0, 8, 9, place("gy") > 0),
                (right, 24, 23, 22, place("gy") < lax.axis_size("gy") - 1),
            ):
                near = own[x, at : at + 8, :]
                far = own[x, ninth : ninth + 1, :]
                if a == 0:
                    near, far = gate(inside, near), gate(inside, far)
                if a == 1:
                    far = far + harmonic(b0[x, ninth : ninth + 1, :], b0[x, tenth : tenth + 1, :])
                for h in range(2):
                    cut = slice(128 * h, 128 * h + 128)
                    out[16 * a + 2 * x + h] = near[:, cut]
                    out[48 + 2 * a + h, x : x + 1, :] = far[:, cut]

    copies[0].wait()
    for x in range(8):
        b0[x] = inverse_density(mv[x])
    strips(0, b0)
    copies[1].wait()
    for x in range(8):
        c0[x] = reaction_of(fv[x])
    strips(1, c0)
    copies[2].wait()
    strips(2, g0)


def k_edge0(b0, c0, g0, low, high):
    for k in range(3):
        low[k] = gate(place("gx") > 0, b0[k])
        high[k] = gate(place("gx") < lax.axis_size("gx") - 1, b0[5 + k])
        low[3 + k] = c0[k] + harmonic(b0[2], b0[3]) if k == 2 else c0[k]
        high[3 + k] = c0[5 + k] + harmonic(b0[5], b0[4]) if k == 0 else c0[5 + k]
        low[6 + k] = g0[k]
        high[6 + k] = g0[5 + k]


def split_pair(tmp, k, value):
    for h in range(2):
        tmp[k, h] = value[:, 128 * h : 128 * h + 128]


def k_coefs(b0, c0, left, right, b1, c1, bc2, tmp0, tmp1):
    for k, (src, out) in enumerate(((b0, b1), (c0, c1))):
        for x in range(4):
            pair = src[2 * x] + src[2 * x + 1]
            for h in range(2):
                t = 16 * k + 4 * x + h
                tmp0[x, h, 0:8, :] = left[t] + left[t + 2]
                tmp0[x, h, 8:40, :] = pair[:, 128 * h : 128 * h + 128]
                tmp0[x, h, 40:48, :] = right[t] + right[t + 2]
        t = fold_level0(tmp0)
        for x in range(4):
            out[x] = t[x]
        for x in range(2):
            tmp1[x] = (t[2 * x] + t[2 * x + 1])[4:20, :]
        bc2[k] = fold_level1(tmp1)


CORNERS = 37


def k_corner0(left, right, low, high):
    for out, first, edge, third, fourth, inside in (
        (low, 0, 0, 2, 3, place("gx") > 0),
        (high, 5, 7, 5, 4, place("gx") < lax.axis_size("gx") - 1),
    ):
        out[36] = jnp.zeros((8, 128), F32)
        for side, strips in enumerate((left, right)):
            for h in range(2):
                for k in range(3):
                    x = first + k
                    at = 18 * side + 2 * k + h
                    out[at] = gate(inside, strips[2 * x + h])
                    c = strips[16 + 2 * x + h]
                    if x == third:
                        c = c + harmonic(strips[2 * x + h], strips[2 * fourth + h])
                    out[at + 6] = c
                    out[at + 12] = strips[32 + 2 * x + h]
                at = 2 * side + h
                out[36, at : at + 1, :] = gate(inside, strips[48 + h, edge : edge + 1, :])


def blocks0(b0, c0, g0, below, above, left, right, under, over):
    for a, own in enumerate((b0, c0, g0)):
        for x in range(-3, 11):
            if 0 <= x < 8:
                tiles = [[s[16 * a + 2 * x + h] for h in range(2)] for s in (left, right)]
                ninth = [[s[48 + 2 * a + h, x : x + 1, :] for h in range(2)] for s in (left, right)]
                yield a, x, own[x], tiles, ninth
            else:
                k = x + 3 if x < 0 else x - 8
                main, far = (below, under) if x < 0 else (above, over)
                tiles = [[far[18 * side + 6 * a + 2 * k + h] for h in range(2)] for side in range(2)]
                ninth = None
                if a == 0 and x in (-1, 8):
                    ninth = [
                        [far[36, 2 * side + h : 2 * side + h + 1, :] for h in range(2)]
                        for side in range(2)
                    ]
                yield a, x, main[3 * a + k], tiles, ninth


def assemble_deep(args, exts):
    zero = jnp.zeros((4, 256), F32)
    for a, x, own, tiles, ninth in blocks0(*args):
        ext = exts[a]
        r = 4 + x
        ext[r, 0:4, :] = zero
        ext[r, 12:44, :] = own
        ext[r, 52:56, :] = zero
        for h in range(2):
            cut = pl.ds(128 * h, 128)
            ext[r, 4:12, cut] = tiles[0][h]
            ext[r, 44:52, cut] = tiles[1][h]
            if ninth is not None:
                ext[r, 3:4, cut] = ninth[0][h]
                ext[r, 52:53, cut] = ninth[1][h]
    for x in (0, 15):
        exts[0][x] = jnp.zeros(exts[0].shape[1:], F32)


def assemble0(args, exts):
    for a, x, own, tiles, _ in blocks0(*args):
        ext = exts[a]
        r = 4 + x
        ext[r, 4:36, :] = own
        for h in range(2):
            cut = pl.ds(128 * h, 128)
            ext[r, 0:4, cut] = tiles[0][h][4:8, :]
            ext[r, 36:40, cut] = tiles[1][h][0:4, :]
    for x in (0, 15):
        exts[0][x] = jnp.zeros(exts[0].shape[1:], F32)


def k_descend0(
    b0, c0, g0, below, above, left, right, under, over, b1, c1,
    v0, g1, low, high,
    be, ce, ge, wx, wy, wz, wl, rd, va, vb, tmp,
):
    assemble_deep((b0, c0, g0, below, above, left, right, under, over), (be, ce, ge))
    s = (wx, wy, wz, wl, rd, ce, ge)
    weights(be, s, va, 1.0, 1, 15, 7)
    sweep(va, vb, s, 2, 14, 12)
    sweep(vb, va, s, 3, 13, 10)
    for x in range(8):
        v0[x] = va[4 + x, 8:48, :]
    kept = None
    for x, here, res in residual_rows(va, s, 4, 12):
        if x % 2 == 0:
            kept = res
        else:
            split_pair(tmp, (x - 4) // 2, (kept + res)[4:52, :])
    t = fold_level0(tmp)
    for x in range(4):
        g1[x] = t[x]
        low[x] = gate(place("gx") > 0, b1[x])
        high[x] = gate(place("gx") < lax.axis_size("gx") - 1, b1[x])
    for k in range(3):
        low[4 + k] = c1[k]
        high[4 + k] = c1[1 + k]
        low[7 + k] = t[k]
        high[7 + k] = t[1 + k]


def k_descend1(
    g1, b1, c1, bc2, below, above,
    v1, pay, be, ce, ge,
    wx, wy, wz, wl, rd, va, vb, tmp,
):
    zeros = jnp.zeros((4, 128), F32)
    for ext, own, base, reach in ((be, b1, 0, 4), (ce, c1, 4, 3), (ge, g1, 7, 3)):
        for x in range(-reach, 4 + reach):
            if x < 0:
                val = below[base + x + reach]
            elif x < 4:
                val = own[x]
            else:
                val = above[base + x - 4]
            ext[4 + x, 0:4, :] = zeros
            ext[4 + x, 4:28, :] = val
            ext[4 + x, 28:32, :] = zeros

    s = (wx, wy, wz, wl, rd, ce, ge)
    weights(be, s, va, 0.25, 1, 11, 10)
    sweep(va, vb, s, 2, 10, 8)
    sweep(vb, va, s, 3, 9, 6)
    for x in range(4):
        v1[x] = va[4 + x, 8:24, :]
    kept = None
    for x, here, res in residual_rows(va, s, 4, 8):
        if x % 2 == 0:
            kept = res[8:24, :]
        else:
            tmp[(x - 4) // 2] = kept + res[8:24, :]
    g2 = fold_level1(tmp)
    for k in range(8):
        pay[k, 0] = g2
        pay[k, 1] = bc2[0]
        pay[k, 2] = bc2[1]


def k_pack_v(v0, v1, low, high):
    for out, first in ((low, 0), (high, 5)):
        for k in range(3):
            for q in range(5):
                for h in range(2):
                    out[10 * k + 2 * q + h] = v0[
                        first + k, 8 * q : 8 * q + 8, 128 * h : 128 * h + 128
                    ]
        for k in range(4):
            for q in range(2):
                out[30 + 2 * k + q] = v1[k, 8 * q : 8 * q + 8, :]


def k_pack_y2(v1, below, above, gathered, low, high):
    for out, q, inside in (
        (low, 0, place("gy") > 0), (high, 1, place("gy") < lax.axis_size("gy") - 1)
    ):
        for k in range(3):
            for i in range(8):
                val = gathered[i, k]
                out[8 * k + i] = gate(inside, val) if k == 1 else val
        cut = pl.ds(4 * q, 4)
        for t, x in enumerate(range(-4, 8)):
            if x < 0:
                val = below[30 + 2 * (x + 4) + q, cut, :]
            elif x < 4:
                val = v1[x, pl.ds(12 * q, 4), :]
            else:
                val = above[30 + 2 * (x - 4) + q, cut, :]
            half = 4 * (t % 2)
            out[24 + t // 2, half : half + 4, :] = val


def upper(shape):
    return iota(shape, len(shape) - 1) >= 64


def pair_next(v):
    mask = upper(v[0].shape)
    out = []
    for i in range(8):
        after = v[i + 1] if i < 7 else jnp.zeros_like(v[0])
        out.append(pltpu.roll(jnp.where(mask, v[i], after), 64, 1))
    return out


def pair_last(f):
    mask = upper(f[0].shape)
    out = []
    for i in range(8):
        before = f[i - 1] if i > 0 else jnp.zeros_like(f[0])
        out.append(pltpu.roll(jnp.where(mask, before, f[i]), 64, 1))
    return out


def weights2(b, c, scaling):
    scale = F32(scaling)
    inside = iota(b[0].shape, 1) % 64 < 63
    wx = [scale * harmonic(p, q) for p, q in zip(b, pair_next(b))]
    wy = [scale * harmonic(p, next_y(p)) for p in b]
    wz = [jnp.where(inside, scale * harmonic(p, next_z(p)), F32(0.0)) for p in b]
    back = pair_last(wx)
    rd = []
    for i in range(8):
        d = (wx[i] + back[i]) + (wy[i] + last_y(wy[i])) + (wz[i] + last_z(wz[i])) + c[i]
        rd.append(step_of(d))
    return wx, wy, wz, rd


def residual2(v, g, c, wx, wy, wz):
    fx = [w * (p - q) for w, p, q in zip(wx, v, pair_next(v))]
    back = pair_last(fx)
    out = []
    for i in range(8):
        fy = wy[i] * (v[i] - next_y(v[i]))
        fz = wz[i] * (v[i] - next_z(v[i]))
        flux = (fx[i] - back[i]) + (fy - last_y(fy)) + (fz - last_z(fz))
        out.append(g[i] - (flux + c[i] * v[i]))
    return out


def k_descend2(gathered, left, right, v2, pay, wx2, wy2, wz2, rd2, ce2, ge2, be2, tmp):
    for k, ext in enumerate((ge2, be2, ce2)):
        for i in range(8):
            ext[i, 0:8, :] = left[8 * k + i]
            ext[i, 8:16, :] = gathered[i, k]
            ext[i, 16:24, :] = right[8 * k + i]
    b = [be2[i] for i in range(8)]
    c = [ce2[i] for i in range(8)]
    g = [ge2[i] for i in range(8)]
    wx, wy, wz, rd = weights2(b, c, 0.0625)
    for i in range(8):
        wx2[i] = wx[i]
        wy2[i] = wy[i]
        wz2[i] = wz[i]
        rd2[i] = rd[i]
    v = [p * q for p, q in zip(rd, g)]
    for _ in range(2):
        r = residual2(v, g, c, wx, wy, wz)
        v = [p + q * s for p, q, s in zip(v, rd, r)]
    r = residual2(v, g, c, wx, wy, wz)
    for i in range(8):
        v2[i] = v[i]
    for k, src in enumerate((r, b, c)):
        for t in range(2):
            for i in range(8):
                at = 64 * (2 * k + t) + 8 * i
                tmp[at : at + 8, :] = src[i][4 + 8 * t : 12 + 8 * t, :]
    for t, tile in enumerate(fold_level2(tmp[...])):
        pay[t] = tile


TILES = 6


def block_next(v):
    head = iota(v[0].shape, 1) < 32
    out = []
    for t in range(TILES):
        after = v[t + 1] if t < TILES - 1 else jnp.zeros_like(v[0])
        out.append(pltpu.roll(jnp.where(head, after, v[t]), 96, 1))
    return out


def block_last(f):
    tail = iota(f[0].shape, 1) >= 96
    out = []
    for t in range(TILES):
        before = f[t - 1] if t > 0 else jnp.zeros_like(f[0])
        out.append(pltpu.roll(jnp.where(tail, before, f[t]), 32, 1))
    return out


def solve3(g, b, c):
    scale = F32(0.015625)
    shape = g[0].shape
    inside_x = iota(shape, 0) < 7
    inside_z = iota(shape, 1) % 32 < 31
    zero = F32(0.0)
    wx = [jnp.where(inside_x, scale * harmonic(p, next_y(p)), zero) for p in b]
    wy = [scale * harmonic(p, q) for p, q in zip(b, block_next(b))]
    wz = [jnp.where(inside_z, scale * harmonic(p, next_z(p)), zero) for p in b]
    xl = [last_y(p) for p in wx]
    yl = block_last(wy)
    zl = [last_z(p) for p in wz]
    rd = []
    for t in range(TILES):
        d = (wx[t] + xl[t]) + (wy[t] + yl[t]) + (wz[t] + zl[t]) + c[t]
        rd.append(step_of(d))
    e = [p * q for p, q in zip(rd, g)]
    for _ in range(7):
        up = block_next(e)
        down = block_last(e)
        new = []
        for t in range(TILES):
            h = e[t]
            flux = wx[t] * (h - next_y(h)) + xl[t] * (h - last_y(h))
            flux = flux + (wy[t] * (h - up[t]) + yl[t] * (h - down[t]))
            flux = flux + (wz[t] * (h - next_z(h)) + zl[t] * (h - last_z(h)))
            new.append(h + rd[t] * (g[t] - (flux + c[t] * h)))
        e = new
    return e


def k_prepare(
    b0, c0, g0, below0, above0, left0, right0, under0, over0, be1, ce1, ge1,
    v0, v1, below, above, left1, right1,
    p0, ce, ge, wx, wy, wz, wl, rd, p1, wx1, wy1, wz1, wl1, rd1,
    be, va, va1,
):
    assemble0((b0, c0, g0, below0, above0, left0, right0, under0, over0), (be, ce, ge))
    weights(be, (wx, wy, wz, wl, rd, ce, ge), va, 1.0, 2, 14, 6)
    weights(be1, (wx1, wy1, wz1, wl1, rd1, ce1, ge1), va1, 0.25, 1, 11, 10)
    zero = jnp.zeros((8, 128), F32)
    for t, x in enumerate(range(-4, 8)):
        p1[t, 0:8, :] = zero
        p1[t, 24:32, :] = zero
        if 0 <= x < 4:
            p1[t, 8:24, :] = v1[x]
        else:
            src, k = (below, x + 4) if x < 0 else (above, x - 4)
            for q in range(2):
                p1[t, 8 + 8 * q : 16 + 8 * q, :] = src[30 + 2 * k + q]
        half = 4 * (t % 2)
        p1[t, 4:8, :] = left1[24 + t // 2, half : half + 4, :]
        p1[t, 24:28, :] = right1[24 + t // 2, half : half + 4, :]
    for x in range(-3, 11):
        if 0 <= x < 8:
            p0[4 + x] = v0[x]
        else:
            src, k = (below, x + 3) if x < 0 else (above, x - 8)
            for q in range(5):
                for h in range(2):
                    p0[4 + x, 8 * q : 8 * q + 8, 128 * h : 128 * h + 128] = (
                        src[10 * k + 2 * q + h]
                    )


def k_ascend(
    own3, r0, r1, v2, wx2, wy2, wz2, rd2, ce2, ge2,
    p0, ce0, ge0, wx0, wy0, wz0, wl0, rd0,
    p1, ce1, ge1, wx1, wy1, wz1, wl1, rd1,
    pressure, residual,
    all3, m2, p2, p1a, p1b, p0a, p0b, f1, f0, own, res0, sems,
):
    ix = place("gx")
    iy = place("gy")
    count = lax.axis_size("gy")
    even_chip = lax.rem(iy // 2, 2) == 0
    zero = F32(0.0)

    for k in range(3):
        first = [jnp.where(even_chip, r1[2 * k + t], r0[2 * k + t]) for t in range(2)]
        last = [jnp.where(even_chip, r0[2 * k + t], r1[2 * k + t]) for t in range(2)]
        at = TILES * k
        all3[at] = gate(iy >= 2, first[0])
        all3[at + 1] = jnp.where(iy >= 2, first[1], gate(iy == 1, first[0]))
        all3[at + 2] = own3[2 * k]
        all3[at + 3] = own3[2 * k + 1]
        all3[at + 4] = jnp.where(iy < count - 2, last[0], gate(iy == count - 2, last[1]))
        all3[at + 5] = gate(iy < count - 2, last[1])
    e = solve3(*[[all3[TILES * k + t] for t in range(TILES)] for k in range(3)])

    group = iota((8, 128), 1) // 32 == iota((8, 128), 0) // 2
    for t in range(2):
        for i in range(8):
            row = jnp.broadcast_to(e[2 + t][i : i + 1, :], (8, 128))
            m2[16 * i + 8 * t : 16 * i + 8 * t + 8, :] = jnp.where(group, row, zero)
    spread = jnp.where(
        iota((128, 128), 0) % 32 == (iota((128, 128), 1) % 64) // 2, F32(1.0), zero
    )
    fine = pick(m2[...], spread)
    for i in range(8):
        p2[i] = v2[i]
        p2[i, 4:20, :] += fine[16 * i : 16 * i + 16, :]
    v = [p2[i] for i in range(8)]
    g = [ge2[i] for i in range(8)]
    c = [ce2[i] for i in range(8)]
    wx = [wx2[i] for i in range(8)]
    wy = [wy2[i] for i in range(8)]
    wz = [wz2[i] for i in range(8)]
    for _ in range(2):
        r = residual2(v, g, c, wx, wy, wz)
        v = [v[i] + rd2[i] * r[i] for i in range(8)]
    for i in range(8):
        p2[i] = v[i]

    parts = []
    for q in range(3):
        at = ix + (q - 1)
        inside = jnp.logical_and(at >= 0, at < lax.axis_size("gx"))
        parts.append(jnp.where(inside, p2[jnp.clip(at, 0, 7), 4:20, :], zero))
    row = iota((128, 256), 0)
    lane = iota((128, 256), 1)
    hit = (row % 64 == (lane % 128) // 2) & (row // 64 == lane // 128)
    fine = pick(jnp.concatenate(parts, axis=0), jnp.where(hit, F32(1.0), zero))
    for q in range(3):
        for h in range(2):
            part = fine[16 * q : 16 * q + 16, 128 * h : 128 * h + 128]
            f1[2 * q + h, pl.ds(0, 16, stride=2), :] = part
            f1[2 * q + h, pl.ds(1, 16, stride=2), :] = part
    for x in range(12):
        p1a[x] = p1[x] + f1[x // 2]
    s1 = (wx1, wy1, wz1, wl1, rd1, ce1, ge1)
    sweep(p1a, p1b, s1, 1, 11, 10)
    sweep(p1b, p1a, s1, 2, 10, 8)

    wide = jnp.where(iota((128, 256), 0) == iota((128, 256), 1) // 2, F32(1.0), zero)
    fine = pick(jnp.concatenate([p1a[2 + x, 6:26, :] for x in range(8)], axis=0), wide)
    for x in range(8):
        for h in range(2):
            part = fine[20 * x : 20 * x + 20, 128 * h : 128 * h + 128]
            f0[x, h, pl.ds(0, 20, stride=2), :] = part
            f0[x, h, pl.ds(1, 20, stride=2), :] = part
    for x in range(1, 15):
        for h in range(2):
            cut = pl.ds(128 * h, 128)
            p0a[x, :, cut] = p0[x, :, cut] + f0[x // 2, h]
    s0 = (wx0, wy0, wz0, wl0, rd0, ce0, ge0)
    sweep(p0a, p0b, s0, 2, 14, 12)
    sweep(p0b, p0a, s0, 3, 13, 10)
    for x in range(8):
        own[x] = p0a[4 + x, 4:36, :]
    copies = [pltpu.make_async_copy(own, pressure, sems.at[0])]
    copies[0].start()
    for x, here, res in residual_rows(p0a, s0, 4, 12):
        res0[x - 4] = res[4:36, :]
        if x % 4 == 3:
            cut = pl.ds(x - 7, 4)
            copies.append(pltpu.make_async_copy(res0.at[cut], residual.at[cut], sems.at[x // 4]))
            copies[-1].start()
    for copy in copies:
        copy.wait()


def call(kernel, name, outs, scratch, limit, *args, anywhere=(), to_hbm=False):
    vmem = pl.BlockSpec(memory_space=pltpu.VMEM)
    hbm = pl.BlockSpec(memory_space=pltpu.HBM)
    specs = [vmem for _ in args]
    for k in anywhere:
        specs[k] = hbm
    return pl.pallas_call(
        kernel,
        name=name,
        out_shape=[jax.ShapeDtypeStruct(s, F32) for s in outs],
        in_specs=specs,
        out_specs=[hbm if to_hbm else vmem for _ in outs],
        scratch_shapes=[pltpu.VMEM(s, F32) if isinstance(s, tuple) else s for s in scratch],
        compiler_params=pltpu.CompilerParams(vmem_limit_bytes=limit * MIB),
    )(*args)


B0 = (8, 32, 256)
E0 = (16, 40, 256)
E1 = (12, 32, 128)
E2 = (8, 24, 128)


def per_device(source, material, flags):
    source, material, flags = (
        pltpu.with_memory_space_constraint(a, pltpu.HBM) for a in (source, material, flags)
    )
    left, right, b0, c0, g0 = call(
        k_load0, "load0", [(STRIPS, 8, 128)] * 2 + [B0] * 3,
        [pltpu.VMEM(B0, jnp.int32), pltpu.VMEM(B0, jnp.int32), pltpu.SemaphoreType.DMA((3,))],
        4, material, flags, source, anywhere=(0, 1, 2),
    )
    left0, right0 = exchange(left, right, "gy")
    low, high = call(k_edge0, "edge0", [(9, 32, 256)] * 2, [], 4, b0, c0, g0)
    below0, above0 = exchange(low, high, "gx")
    low, high = call(k_corner0, "corner0", [(CORNERS, 8, 128)] * 2, [], 4, left0, right0)
    under0, over0 = exchange(low, high, "gx")
    b1, c1, bc2 = call(
        k_coefs, "coefs", [(4, 24, 128), (4, 24, 128), (2, 8, 128)],
        [(4, 2, 48, 128), (2, 16, 128)], 4, b0, c0, left0, right0,
    )
    own0 = (b0, c0, g0, below0, above0, left0, right0, under0, over0)
    v0, g1, low, high = call(
        k_descend0, "descend0",
        [(8, 40, 256), (4, 24, 128), (10, 24, 128), (10, 24, 128)],
        [(16, 56, 256)] * 10 + [(4, 2, 48, 128)], 16, *own0, b1, c1,
    )
    below, above = exchange(low, high, "gx")
    v1, pay, be1, ce1, ge1 = call(
        k_descend1, "descend1",
        [(4, 16, 128), (8, 3, 8, 128)] + [E1] * 3,
        [E1] * 7 + [(2, 16, 128)], 4,
        g1, b1, c1, bc2, below, above,
    )
    gathered = lax.all_to_all(pay, "gx", 0, 0)
    low, high = call(k_pack_v, "pack_v", [(38, 8, 128)] * 2, [], 4, v0, v1)
    below, above = exchange(low, high, "gx")
    low, high = call(
        k_pack_y2, "pack_y2", [(30, 8, 128)] * 2, [], 4, v1, below, above, gathered
    )
    left1, right1 = exchange(low, high, "gy")
    v2, own3, *s2 = call(
        k_descend2, "descend2", [E2, (6, 8, 128)] + [E2] * 6, [E2, (384, 128)], 4,
        gathered, left1, right1,
    )
    r1 = swap_chips(own3, "gy", 1)
    r0 = swap_chips(own3, "gy", 0)
    p0, ce0, ge0, wx0, wy0, wz0, wl0, rd0, p1, *w1 = call(
        k_prepare, "prepare", [E0] * 8 + [E1] * 6, [E0, E0, E1], 8,
        *own0, be1, ce1, ge1, v0, v1, below, above, left1, right1,
    )
    pressure, residual = call(
        k_ascend, "ascend", [B0] * 2,
        [(18, 8, 128), (128, 128), E2, E1, E1, E0, E0, (6, 32, 128), (8, 2, 40, 128),
         B0, B0, pltpu.SemaphoreType.DMA((3,))],
        8, own3, r0, r1, v2, *s2,
        p0, ce0, ge0, wx0, wy0, wz0, wl0, rd0, p1, ce1, ge1, *w1, to_hbm=True,
    )
    return pressure, residual


def solution(mesh):
    spec = P("gx", "gy", None)
    return jax.shard_map(
        per_device,
        mesh=mesh,
        in_specs=(spec, spec, spec),
        out_specs=(spec, spec),
        check_vma=False,
    )
```
